128 devices in a mesh: ctx: 16 (over x, y), fsdp: 8 (over z, core).
Axes of the slice: x: 4, y: 4, z: 4, core: 2. Of those that a mesh axis runs over, the one named last changes fastest.
Arguments:
- tokens: bfloat16 [8, 2048, 1024], P('fsdp', 'ctx'), may hold values from -6 to 6
- gain_one: bfloat16 [1024], P('fsdp'), may hold values from 0.5 to 1.5
- w_mamba_in: bfloat16 [1024, 3328], P('fsdp'), may hold values from -0.1875 to 0.1875
- conv_weight: bfloat16 [1792, 4], P('fsdp'), may hold values from -4 to 4
- w_mamba_out: bfloat16 [1536, 1024], P('fsdp'), may hold values from -0.15625 to 0.15625
- w_qkv: bfloat16 [1024, 768], P('fsdp'), may hold values from -0.1875 to 0.1875
- w_attn_out: bfloat16 [512, 1024], P('fsdp'), may hold values from -2 to 2
- gain_two: bfloat16 [1024], P('fsdp'), may hold values from 0.5 to 1.5
- w_gate_up: bfloat16 [1024, 4096], P('fsdp'), may hold values from -0.1875 to 0.1875
- w_down: bfloat16 [2048, 1024], P('fsdp'), may hold values from -0.125 to 0.125
- decays: float32 [8, 2048, 24], P('fsdp', 'ctx'), may hold values from 0.4 to 1, as said below
- input_gates: float32 [8, 2048, 24], P('fsdp', 'ctx'), may hold values from 0 to 2.5
- grad_out: bfloat16 [8, 2048, 1024], P('fsdp', 'ctx'), may hold values from -6 to 6
Outputs:
- output: bfloat16 [8, 2048, 1024], P('fsdp', 'ctx')
- grad_tokens: float32 [8, 2048, 1024], P('fsdp', 'ctx')
- grad_gain_one: float32 [1024], P('fsdp')
- grad_w_mamba_in: float32 [1024, 3328], P('fsdp')
- grad_conv_weight: float32 [1792, 4], P('fsdp')
- grad_w_mamba_out: float32 [1536, 1024], P('fsdp')
- grad_w_qkv: float32 [1024, 768], P('fsdp')
- grad_w_attn_out: float32 [512, 1024], P('fsdp')
- grad_gain_two: float32 [1024], P('fsdp')
- grad_w_gate_up: float32 [1024, 4096], P('fsdp')
- grad_w_down: float32 [2048, 1024], P('fsdp')
The draws below stay inside these ranges and needn't reach their ends.
Inputs may be any that keep to these rules, and one draw needn't show every extreme that they name: `decays`: each entry is exp(-r) with r > 0.
All inputs are finite; a program needn't handle non-finite values.
Results may differ from the reference program's by a relative error of at most 0.025.
Values may be sent and summed in bfloat16 or wider, within the bound.
No kernel may reach another device: no remote copies, remote signals or barrier semaphores. Data moves between devices by JAX's collectives and lax.ppermute only.
A program may use at most 128 MiB of HBM per device.

```python
import math
import jax
import jax.numpy as jnp
from jax import lax

D = 1024
QH = 8
KH = 2
HD = 64
MIXER_HEADS = 24
MP = 64
NS = 128
CONV = 4
FF = 2048
TOK_DEV = 128
SSD_BLOCK = 128
SEQUENCE_TOKENS = 2048
SEQUENCES = 8
MI = 1536
XBC = 1792
QKV = 768


def shared_rates(key, slow_heads):
    random_subkeys = jax.random.split(key, 6)
    all_rows = SEQUENCES * SEQUENCE_TOKENS
    order = jax.random.permutation(random_subkeys[0], MIXER_HEADS)
    is_slow = order < slow_heads
    slow_rate = jnp.exp(jax.random.uniform(random_subkeys[1], (MIXER_HEADS,), minval=math.log(0.1), maxval=math.log(0.5))) / SEQUENCE_TOKENS
    fast_rate = jnp.exp(jax.random.uniform(random_subkeys[2], (MIXER_HEADS,), minval=math.log(1.0 / 50.0), maxval=math.log(1.0 / 30.0)))
    baseline_rate = jnp.where(is_slow, slow_rate, fast_rate)
    device_multiplier = jnp.exp(jax.random.uniform(random_subkeys[3], (all_rows // TOK_DEV, MIXER_HEADS), minval=-math.log(2.0), maxval=math.log(2.0)))
    device_multiplier = jnp.repeat(device_multiplier, TOK_DEV, axis=0)
    token_multiplier = jnp.exp(jax.random.uniform(random_subkeys[4], (all_rows, MIXER_HEADS), minval=-math.log(2.0), maxval=math.log(2.0)))
    spike_keys = jax.random.split(random_subkeys[5], 2)
    spike_rows = jax.random.randint(spike_keys[0], (SEQUENCES, 3), 0, SEQUENCE_TOKENS)
    spike_selected = jnp.any(jnp.arange(SEQUENCE_TOKENS)[None, :, None] == spike_rows[:, None, :], axis=2).reshape(all_rows)
    spike_count = jax.random.uniform(spike_keys[1], (all_rows, MIXER_HEADS), minval=0.22, maxval=0.69)
    rates = baseline_rate[None, :] * device_multiplier * token_multiplier + jnp.where(spike_selected[:, None], spike_count, 0.0)
    return rates.reshape(SEQUENCES, SEQUENCE_TOKENS, MIXER_HEADS)


def draw_decays(key, part):
    slow_heads = MIXER_HEADS // 2
    decay_rates = shared_rates(key, slow_heads)
    return jnp.exp(-decay_rates).astype(jnp.float32)


def draw_input_gates(key, part):
    slow_heads = MIXER_HEADS // 2
    decay_rates = shared_rates(key, slow_heads)
    key = jax.random.fold_in(key, 11)
    roughness = jnp.exp(jax.random.uniform(key, (SEQUENCES, SEQUENCE_TOKENS, MIXER_HEADS), minval=-math.log(2.0), maxval=math.log(2.0)))
    return (2.0 * (1.0 - jnp.exp(-decay_rates)) * roughness).astype(jnp.float32)


def block_scale(own_key, shape, shards, smallest, top_value):
    def one(dim, blocks):
        heights = jax.random.uniform(jax.random.fold_in(jax.random.fold_in(own_key, 6), dim), (blocks,), jnp.float32, smallest / len(shards), top_value / len(shards))
        return jnp.repeat(jnp.exp(heights), shape[dim] // blocks).reshape((-1,) + (1,) * (len(shape) - dim - 1))

    loudness = one(*shards[0])
    for cut in shards[1:]:
        loudness = loudness * one(*cut)
    return loudness


def gaussian(key, dims, scale, most, cuts=(), held_as=jnp.bfloat16):
    values = jax.random.normal(key, dims, jnp.float32) * scale
    if len(cuts) > 0:
        values = block_scale(key, dims, cuts, -0.22, 0.18) * values
    return jnp.clip(values, min=-most, max=most).astype(held_as)


def setup_inputs(seed: int = 0) -> dict:
    streams_of = jax.random.split(jax.random.key(seed), 14)
    return {
        "tokens": gaussian(streams_of[0], (SEQUENCES, SEQUENCE_TOKENS, D), 1.0, 6.0, ((0, 8), (1, 16))),
        "gain_one": jnp.clip(1.0 + 0.1 * jax.random.normal(streams_of[1], (D,), jnp.float32), 0.5, 1.5).astype(jnp.bfloat16),
        "w_mamba_in": gaussian(streams_of[2], (D, MI + XBC), D ** -0.5, 0.1875, ((0, 8),)),
        "conv_weight": gaussian(streams_of[3], (XBC, CONV), (CONV // 2) ** -0.5, 4.0, ((0, 8),)),
        "w_mamba_out": gaussian(streams_of[4], (MI, D), MI ** -0.5, 0.15625, ((0, 8),)),
        "w_qkv": gaussian(streams_of[5], (D, QKV), D ** -0.5, 0.1875, ((0, 8),)),
        "w_attn_out": gaussian(streams_of[6], (QH * HD, D), (QH * HD // 64) ** -0.5, 2.0, ((0, 8),)),
        "gain_two": jnp.clip(1.0 + 0.1 * jax.random.normal(streams_of[7], (D,), jnp.float32), 0.5, 1.5).astype(jnp.bfloat16),
        "w_gate_up": gaussian(streams_of[8], (D, 2 * FF), D ** -0.5, 0.1875, ((0, 8),)),
        "w_down": gaussian(streams_of[9], (FF, D), FF ** -0.5, 0.125, ((0, 8),)),
        "decays": draw_decays(jax.random.fold_in(streams_of[13], 71), 0),
        "input_gates": draw_input_gates(jax.random.fold_in(streams_of[13], 71), 0),
        "grad_out": gaussian(streams_of[12], (SEQUENCES, SEQUENCE_TOKENS, D), 1.0, 6.0, ((0, 8), (1, 16))),
    }


epsilon = 1e-05
rope_base = 10000.0
masked_value = -1e+30
highest = lax.Precision.HIGHEST

@jax.custom_vjp
def low(v):
    return lax.optimization_barrier(v.astype(jnp.bfloat16)).astype(jnp.float32)

@jax.custom_vjp
def low_back(v):
    return v

def low_keep(v):
    return (low(v), None)

def low_pass(kept, grad):
    return (grad,)

def back_keep(v):
    return (v, None)

def back_low(kept, grad):
    return (low(grad),)
low.defvjp(low_keep, low_pass)
low_back.defvjp(back_keep, back_low)

def matmul(left, right):
    return jnp.dot(left, right, precision=highest, preferred_element_type=jnp.float32)

def silu(entries):
    return entries * jax.nn.sigmoid(entries)

def rotate(values, positions, direction):
    half_dim = HD // 2
    frequency = jnp.exp(-jnp.log(rope_base) * (2.0 * jnp.arange(half_dim).astype(jnp.float32) / HD))
    angles = positions[:, None] * frequency[None, :]
    cosine = jnp.cos(angles)[:, None, :]
    sine_part = jnp.sin(angles)[:, None, :]
    front_half = values[..., :half_dim]
    back_half = values[..., half_dim:]
    return jnp.concatenate([front_half * cosine - direction * back_half * sine_part, back_half * cosine + direction * front_half * sine_part], axis=-1)

def ssd_step(state_in, pieces):
    inputs_x, input_b, input_c, gate_vals, log_decay = pieces
    cumulative = jnp.cumsum(log_decay, axis=0)
    length = log_decay.shape[0]
    row_ids = lax.broadcasted_iota(jnp.int32, (length, length), 0)
    col_ids = lax.broadcasted_iota(jnp.int32, (length, length), 1)
    causal = (col_ids <= row_ids)[None]
    spread = cumulative.T[:, :, None] - cumulative.T[:, None, :]
    weights = jnp.where(causal, jnp.exp(jnp.where(causal, spread, 0.0)), 0.0)
    products_cb = jnp.dot(input_c, input_b.T, precision=highest, preferred_element_type=jnp.float32)
    mixing = weights * products_cb[None] * gate_vals.T[:, None, :]
    outputs = jnp.einsum('hts,shp->thp', mixing, inputs_x, precision=highest)
    carried = jnp.exp(cumulative)[:, :, None] * jnp.einsum('hpn,tn->thp', state_in, input_c, precision=highest)
    remain = jnp.exp(cumulative[-1][None, :] - cumulative) * gate_vals
    new_state = jnp.exp(cumulative[-1])[:, None, None] * state_in + jnp.einsum('sh,shp,sn->hpn', remain, inputs_x, input_b, precision=highest)
    return (new_state, outputs + carried)

def ssd_run(inputs_x, input_b, input_c, gate_vals, log_decay, state_in):
    row_count = inputs_x.shape[0]
    block_total = row_count // SSD_BLOCK
    pieces = (inputs_x.reshape(block_total, SSD_BLOCK, inputs_x.shape[1], inputs_x.shape[2]), input_b.reshape(block_total, SSD_BLOCK, input_b.shape[1]), input_c.reshape(block_total, SSD_BLOCK, input_c.shape[1]), gate_vals.reshape(block_total, SSD_BLOCK, gate_vals.shape[1]), log_decay.reshape(block_total, SSD_BLOCK, log_decay.shape[1]))
    final_state, outputs = lax.scan(jax.checkpoint(ssd_step), state_in, pieces)
    return (outputs.reshape(inputs_x.shape), final_state)

def attend(queries, start, key_rows, value_rows):
    query_rows = queries.shape[0]
    group_size = QH // KH
    grouped = queries.reshape(query_rows, KH, group_size, HD)
    scores = jnp.einsum('tgrd,kgd->grtk', grouped, key_rows, precision=highest) * HD ** (-0.5)
    scores = low_back(scores)
    query_pos = start + jnp.arange(query_rows)
    key_pos = jnp.arange(key_rows.shape[0])
    allowed = key_pos[None, :] <= query_pos[:, None]
    scores = jnp.where(allowed, scores, masked_value)
    row_max = lax.optimization_barrier(jnp.max(scores, axis=-1, keepdims=True))
    exponent = jnp.exp(scores - row_max)
    weights = exponent / lax.optimization_barrier(jnp.sum(exponent, axis=-1, keepdims=True))
    mixer_output = jnp.einsum('grtk,kgd->tgrd', low(weights), value_rows, precision=highest)
    return low(low_back(mixer_output)).reshape(query_rows, QH * HD)

def reference(tokens, gain_one, w_mamba_in, conv_weight, w_mamba_out, w_qkv, w_attn_out, gain_two, w_gate_up, w_down, decays, input_gates, grad_out):
    inner_width = MIXER_HEADS * MP
    q_width = QH * HD
    kv_width = KH * HD
    log_decay_all = jnp.log(decays.astype(jnp.float32))
    gate_all = input_gates.astype(jnp.float32)
    positions = jnp.arange(SEQUENCE_TOKENS).astype(jnp.float32)
    query_block = min(512, SEQUENCE_TOKENS)
    blocks = SEQUENCE_TOKENS // query_block

    def layer(hidden_all, g_one, w_min, w_conv, w_mout, w_proj, w_aout, g_two, w_gu, w_dn):

        def one_sequence(items):
            hidden_in, log_decay, gate_vals = items
            normed = hidden_in * lax.rsqrt(lax.optimization_barrier(jnp.mean(hidden_in * hidden_in, axis=-1, keepdims=True)) + epsilon)
            shared = low(normed * g_one)
            projected = low_back(matmul(shared, w_min))
            gating = projected[:, :inner_width]
            conv_in = low(projected[:, inner_width:])
            padded = jnp.pad(conv_in, ((CONV - 1, 0), (0, 0)))
            conv_out = jnp.zeros_like(conv_in)
            for tap_index in range(CONV):
                conv_out = conv_out + padded[tap_index:tap_index + SEQUENCE_TOKENS] * w_conv[:, tap_index][None, :]
            conv_out = low_back(conv_out)
            activated = low(silu(conv_out))
            inputs_x = activated[:, :inner_width].reshape(SEQUENCE_TOKENS, MIXER_HEADS, MP)
            input_b = activated[:, inner_width:inner_width + NS]
            input_c = activated[:, inner_width + NS:]
            ssd_out, final_state = ssd_run(inputs_x, input_b, input_c, gate_vals, log_decay, jnp.zeros((MIXER_HEADS, MP, NS), jnp.float32))
            ssd_out = low_back(ssd_out.reshape(SEQUENCE_TOKENS, inner_width))
            mamba_out = low_back(matmul(low(ssd_out * silu(gating)), w_mout))
            projections = low_back(matmul(shared, w_proj))
            queries = low(rotate(projections[:, :q_width].reshape(SEQUENCE_TOKENS, QH, HD), positions, 1.0))
            key_rows = low(rotate(projections[:, q_width:q_width + kv_width].reshape(SEQUENCE_TOKENS, KH, HD), positions, 1.0))
            value_rows = low(projections[:, q_width + kv_width:].reshape(SEQUENCE_TOKENS, KH, HD))
            starts = jnp.arange(blocks) * query_block
            attended = lax.map(jax.checkpoint(lambda block_item: attend(block_item[0], block_item[1], key_rows, value_rows)), (queries.reshape(blocks, query_block, QH, HD), starts))
            attn_out = low_back(matmul(attended.reshape(SEQUENCE_TOKENS, q_width), w_aout))
            residual = hidden_in + attn_out + mamba_out
            normed_two = residual * lax.rsqrt(lax.optimization_barrier(jnp.mean(residual * residual, axis=-1, keepdims=True)) + epsilon)
            second = low(normed_two * g_two)
            gate_up = low_back(matmul(second, w_gu))
            hidden_act = low(silu(gate_up[:, :FF]) * gate_up[:, FF:])
            return residual + low_back(matmul(hidden_act, w_dn))
        return lax.map(one_sequence, (hidden_all, log_decay_all, gate_all))
    primals = (tokens.astype(jnp.float32), gain_one.astype(jnp.float32), w_mamba_in.astype(jnp.float32), conv_weight.astype(jnp.float32), w_mamba_out.astype(jnp.float32), w_qkv.astype(jnp.float32), w_attn_out.astype(jnp.float32), gain_two.astype(jnp.float32), w_gate_up.astype(jnp.float32), w_down.astype(jnp.float32))
    result, pullback = jax.vjp(layer, *primals)
    gradients = pullback(grad_out.astype(jnp.float32))
    return (result.astype(jnp.bfloat16), gradients[0], gradients[1], gradients[2], gradients[3], gradients[4], gradients[5], gradients[6], gradients[7], gradients[8], gradients[9])
```

```python
import functools

import jax
import jax.numpy as jnp
from jax import lax
from jax.experimental import pallas as pl
from jax.experimental.pallas import tpu as pltpu
from jax.sharding import PartitionSpec as P

D = 1024
QH = 8
KH = 2
HD = 64
MIXER_HEADS = 24
MP = 64
NS = 128
CONV = 4
FF = 2048
SSD_BLOCK = 128
KEY_BLOCK = 512
MI = MIXER_HEADS * MP
XBC = MI + 2 * NS
Q_WIDTH = QH * HD
KV_WIDTH = KH * HD
CTX = 16
OWNERS = 8
HALO = 8
STATE_ROWS = MI // CTX

epsilon = 1e-05
rope_base = 10000.0
masked_value = -1e30
highest = lax.Precision.HIGHEST
bf16 = jnp.bfloat16
f32 = jnp.float32


def passed_along(value, axis, steps):
    count = lax.axis_size(axis)
    leading, last = (max(0, -steps), min(count, count - steps))
    return lax.ppermute(value, axis, [(source, source + steps) for source in range(leading, last)])


def swap(value, axis):
    return lax.all_to_all(value, axis, 0, 0, tiled=True)


def silu(entries):
    return entries * jax.nn.sigmoid(entries)


def silu_slope(entries):
    logistic = jax.nn.sigmoid(entries)
    return logistic * (1.0 + entries * (1.0 - logistic))


def rotate(values, positions, direction):
    half_dim = HD // 2
    frequency = jnp.exp(-jnp.log(rope_base) * (2.0 * jnp.arange(half_dim).astype(jnp.float32) / HD))
    angles = positions[:, None] * frequency[None, :]
    cosine = jnp.cos(angles)[:, None, :]
    sine_part = jnp.sin(angles)[:, None, :]
    front_half = values[..., :half_dim]
    back_half = values[..., half_dim:]
    return jnp.concatenate(
        [
            front_half * cosine - direction * back_half * sine_part,
            back_half * cosine + direction * front_half * sine_part,
        ],
        axis=-1,
    )


def ssd_local(inputs_x, input_b, input_c, gate_vals, cumulative):
    length = cumulative.shape[0]
    row_ids = lax.broadcasted_iota(jnp.int32, (length, length), 0)
    col_ids = lax.broadcasted_iota(jnp.int32, (length, length), 1)
    causal = (col_ids <= row_ids)[None]
    spread = cumulative.T[:, :, None] - cumulative.T[:, None, :]
    weights = jnp.where(causal, jnp.exp(jnp.where(causal, spread, 0.0)), 0.0)
    products_cb = jnp.dot(
        input_c.astype(jnp.bfloat16),
        input_b.T.astype(jnp.bfloat16),
        preferred_element_type=jnp.float32,
    )
    mixing = weights * products_cb[None] * gate_vals.T[:, None, :]
    outputs = jnp.einsum("hts,shp->thp", mixing, inputs_x, precision=highest)
    remain = jnp.exp(cumulative[-1][None, :] - cumulative) * gate_vals
    new_state = jnp.einsum("sh,shp,sn->hpn", remain, inputs_x, input_b, precision=highest)
    return (outputs, new_state)


def rms_back(grad_normed, normed, inverse, gain):
    scaled = grad_normed * gain
    return inverse * (scaled - normed * jnp.mean(scaled * normed, axis=-1, keepdims=True))


def block_scores(grouped_q, query_pos, block_idx, key_block):
    scores = jnp.einsum(
        "tgrd,kgd->grtk",
        grouped_q,
        key_block.reshape(KEY_BLOCK, KH, HD),
        preferred_element_type=jnp.float32,
    ) * HD ** (-0.5)
    key_pos = block_idx * KEY_BLOCK + jnp.arange(KEY_BLOCK)
    allowed = key_pos[None, :] <= query_pos[:, None]
    return jnp.where(allowed, scores, masked_value)


def forward_attend(grouped_q, query_pos, key_all, value_all):
    rows = grouped_q.shape[0]
    group_size = QH // KH
    last_row = jnp.max(query_pos)
    block_count = key_all.shape[0] // KEY_BLOCK

    def total_step(block_idx, carried):

        def total_update(state_pair):
            row_max, row_sum = state_pair
            key_block = lax.dynamic_slice_in_dim(key_all, block_idx * KEY_BLOCK, KEY_BLOCK, 0)
            scores = block_scores(grouped_q, query_pos, block_idx, key_block)
            new_max = jnp.maximum(row_max, jnp.max(scores, axis=-1))
            new_sum = row_sum * jnp.exp(row_max - new_max) + jnp.sum(
                jnp.exp(scores - new_max[..., None]), axis=-1
            )
            return (new_max, new_sum)

        return lax.cond(
            block_idx * KEY_BLOCK <= last_row, total_update, lambda unchanged: unchanged, carried
        )

    start_pair = (
        jnp.full((KH, group_size, rows), masked_value, jnp.float32),
        jnp.zeros((KH, group_size, rows), jnp.float32),
    )
    row_max, row_sum = lax.fori_loop(0, block_count, total_step, start_pair)
    log_total = row_max + jnp.log(row_sum)

    def mix_step(block_idx, totals):

        def mix_update(running):
            key_block = lax.dynamic_slice_in_dim(key_all, block_idx * KEY_BLOCK, KEY_BLOCK, 0)
            value_block = lax.dynamic_slice_in_dim(value_all, block_idx * KEY_BLOCK, KEY_BLOCK, 0)
            scores = block_scores(grouped_q, query_pos, block_idx, key_block)
            probabilities = jnp.exp(scores - log_total[..., None]).astype(jnp.bfloat16)
            return running + jnp.einsum(
                "grtk,kgd->tgrd",
                probabilities,
                value_block.reshape(KEY_BLOCK, KH, HD),
                preferred_element_type=jnp.float32,
            )

        return lax.cond(
            block_idx * KEY_BLOCK <= last_row, mix_update, lambda unchanged: unchanged, totals
        )

    mixer_output = lax.fori_loop(
        0, block_count, mix_step, jnp.zeros((rows, KH, group_size, HD), jnp.float32)
    )
    return (log_total, mixer_output)


def backward_attend(
    grouped_q,
    mixer_gradient,
    mixer_output,
    log_total,
    query_pos,
    key_all,
    value_all,
    grad_keys,
    grad_values,
):
    rows = grouped_q.shape[0]
    group_size = QH // KH
    kv_width = KH * HD
    last_row = jnp.max(query_pos)
    block_count = key_all.shape[0] // KEY_BLOCK
    row_difference = jnp.einsum("apoz,apoz->poa", mixer_gradient.astype(jnp.float32), mixer_output)

    def back_step(block_idx, carried):

        def back_update(triple):
            grad_query, keys_sum, values_sum = triple
            start = block_idx * KEY_BLOCK
            key_block = lax.dynamic_slice_in_dim(key_all, start, KEY_BLOCK, 0)
            value_block = lax.dynamic_slice_in_dim(value_all, start, KEY_BLOCK, 0)
            probabilities = jnp.exp(
                block_scores(grouped_q, query_pos, block_idx, key_block) - log_total[..., None]
            )
            rounded = probabilities.astype(jnp.bfloat16)
            grad_probs = jnp.einsum(
                "tgrd,kgd->grtk",
                mixer_gradient,
                value_block.reshape(KEY_BLOCK, KH, HD),
                preferred_element_type=jnp.float32,
            )
            grad_scores = (probabilities * (grad_probs - row_difference[..., None])).astype(
                jnp.bfloat16
            )
            grad_query = grad_query + jnp.einsum(
                "grtk,kgd->tgrd",
                grad_scores,
                key_block.reshape(KEY_BLOCK, KH, HD),
                preferred_element_type=jnp.float32,
            )
            key_part = jnp.einsum(
                "grtk,tgrd->kgd", grad_scores, grouped_q, preferred_element_type=jnp.float32
            ).reshape(KEY_BLOCK, kv_width)
            value_part = jnp.einsum(
                "grtk,tgrd->kgd", rounded, mixer_gradient, preferred_element_type=jnp.float32
            ).reshape(KEY_BLOCK, kv_width)
            keys_sum = lax.dynamic_update_slice_in_dim(
                keys_sum,
                lax.dynamic_slice_in_dim(keys_sum, start, KEY_BLOCK, 0) + key_part,
                start,
                0,
            )
            values_sum = lax.dynamic_update_slice_in_dim(
                values_sum,
                lax.dynamic_slice_in_dim(values_sum, start, KEY_BLOCK, 0) + value_part,
                start,
                0,
            )
            return (grad_query, keys_sum, values_sum)

        return lax.cond(
            block_idx * KEY_BLOCK <= last_row, back_update, lambda unchanged: unchanged, carried
        )

    start_triple = (jnp.zeros((rows, KH, group_size, HD), jnp.float32), grad_keys, grad_values)
    return lax.fori_loop(0, block_count, back_step, start_triple)


def whole(shape):
    return pl.BlockSpec(shape, lambda *_: (0,) * len(shape))


def params():
    return pltpu.CompilerParams(vmem_limit_bytes=48 * 1024 * 1024)


def cross(left, right):
    return lax.dot_general(left, right, (((0,), (0,)), ((), ())), preferred_element_type=f32)


def prefix_kernel(reverse, parts_ref, decay_ref, out_ref):
    running = jnp.zeros(out_ref.shape[1:], f32)
    for at in range(CTX - 1, -1, -1) if reverse else range(CTX):
        out_ref[at] = running.astype(bf16)
        running = decay_ref[at] * running + parts_ref[at].astype(f32)


def prefix(parts, decay_rows, reverse):
    shape = (CTX, STATE_ROWS, NS)
    return pl.pallas_call(
        functools.partial(prefix_kernel, reverse),
        out_shape=jax.ShapeDtypeStruct(shape, bf16),
        compiler_params=params(),
        name="state_prefix",
    )(parts, decay_rows)


def ffn_grads_kernel(hidden_ref, grad_out_ref, second_ref, grad_gu_ref, out_ref):
    rows = hidden_ref.shape[1]
    out_ref[0, :rows] = cross(hidden_ref[...], grad_out_ref[...]).astype(bf16)
    for block in range(4):
        cols = slice(D * block, D * (block + 1))
        part = cross(second_ref[...], grad_gu_ref[:, cols]).astype(bf16)
        out_ref[0, rows + 128 * block : rows + 128 * (block + 1)] = part


def ffn_grads(hidden_act, grad_out, second, grad_gu):
    rows = hidden_act.shape[0]
    return pl.pallas_call(
        ffn_grads_kernel,
        grid=(OWNERS,),
        in_specs=[
            pl.BlockSpec((rows, FF // OWNERS), lambda f: (0, f)),
            whole((rows, D)),
            pl.BlockSpec((rows, D // OWNERS), lambda f: (0, f)),
            whole((rows, 2 * FF)),
        ],
        out_specs=pl.BlockSpec((1, 768, D), lambda f: (f, 0, 0)),
        out_shape=jax.ShapeDtypeStruct((OWNERS, 768, D), bf16),
        compiler_params=params(),
        name="ffn_grads",
    )(hidden_act, grad_out, second, grad_gu)


def mix_grads_kernel(mamba_ref, attended_ref, branch_ref, shared_ref, grad_m_ref, grad_a_ref, out_ref):
    mamba = cross(mamba_ref[...], branch_ref[...]).astype(bf16)
    attended = cross(attended_ref[...], branch_ref[...]).astype(bf16)
    for owner in range(2):
        out_ref[owner, :192] = mamba[192 * owner : 192 * (owner + 1)]
        out_ref[owner, 192:256] = attended[64 * owner : 64 * (owner + 1)]
        held = shared_ref[:, 128 * owner : 128 * (owner + 1)]
        for block in range(3):
            cols = slice(D * block, D * (block + 1))
            part = cross(held, grad_m_ref[:, cols]).astype(bf16)
            out_ref[owner, 256 + 128 * block : 384 + 128 * block] = part
        out_ref[owner, 640:768, :256] = cross(held, grad_m_ref[:, 3072:3328]).astype(bf16)
        out_ref[owner, 640:768, 256:] = cross(held, grad_a_ref[...]).astype(bf16)


def mix_grads(mamba_in, attended, branch_grad, shared, grad_m, grad_a):
    rows = mamba_in.shape[0]
    return pl.pallas_call(
        mix_grads_kernel,
        grid=(OWNERS // 2,),
        in_specs=[
            pl.BlockSpec((rows, 384), lambda f: (0, f)),
            pl.BlockSpec((rows, 128), lambda f: (0, f)),
            whole((rows, D)),
            pl.BlockSpec((rows, 256), lambda f: (0, f)),
            whole((rows, MI + XBC)),
            whole((rows, 768)),
        ],
        out_specs=pl.BlockSpec((2, 768, D), lambda f: (f, 0, 0)),
        out_shape=jax.ShapeDtypeStruct((OWNERS, 768, D), bf16),
        compiler_params=params(),
        name="mix_grads",
    )(mamba_in, attended, branch_grad, shared, grad_m, grad_a)


def ctx_sum(chunks):
    got = swap(chunks, "ctx")
    mine = jnp.sum(got.astype(f32), axis=0).astype(bf16)
    return swap(jnp.broadcast_to(mine[None], chunks.shape), "ctx")


def on_device(
    tokens,
    gain_one,
    w_mamba_in,
    conv_weight,
    w_mamba_out,
    w_qkv,
    w_attn_out,
    gain_two,
    w_gate_up,
    w_down,
    decays,
    input_gates,
    grad_out,
):
    tokens = tokens[0]
    decays = decays[0]
    input_gates = input_gates[0]
    grad_out = grad_out[0]
    tok_rows = tokens.shape[0]
    group_size = QH // KH
    score_scale = HD ** (-0.5)
    ctx_index = lax.axis_index("ctx")
    offset = ctx_index * tok_rows

    first_weights = lax.all_gather(
        jnp.concatenate([w_mamba_in, w_qkv], axis=1), "fsdp", axis=0, tiled=True
    )
    rest = jnp.concatenate(
        [w_mamba_out, w_attn_out, w_down]
        + [w_gate_up[:, D * block : D * (block + 1)] for block in range(4)],
        axis=0,
    )
    rest_weights = lax.all_gather(rest, "fsdp", axis=0, tiled=False)
    small = jnp.concatenate([gain_one, gain_two, conv_weight.T.reshape(-1)])
    small_all = lax.all_gather(small[None], "fsdp", axis=0, tiled=True)
    gain_first = small_all[:, :128].reshape(D).astype(f32)
    gain_second = small_all[:, 128:256].reshape(D).astype(f32)
    conv_taps = small_all[:, 256:].reshape(OWNERS, CONV, XBC // OWNERS).transpose(1, 0, 2)
    conv_taps = conv_taps.reshape(CONV, XBC).astype(f32)

    log_decay = jnp.log(decays)
    cumulative = jnp.cumsum(log_decay, axis=0)
    whole_decay = jnp.exp(cumulative[-1])
    reach_decay = jnp.exp(cumulative)
    decays_all = lax.all_gather(whole_decay[None], "ctx", axis=0, tiled=True)
    decay_rows = lax.dynamic_slice_in_dim(
        jnp.repeat(decays_all, MP, axis=1), ctx_index * STATE_ROWS, STATE_ROWS, 1
    )[:, :, None]

    halo = passed_along(tokens[tok_rows - HALO :], "ctx", 1)
    hidden_ext = jnp.concatenate([halo, tokens], axis=0).astype(f32)
    inverse_ext = lax.rsqrt(jnp.mean(hidden_ext * hidden_ext, axis=-1, keepdims=True) + epsilon)
    normed_ext = hidden_ext * inverse_ext
    shared_ext = (normed_ext * gain_first).astype(bf16)
    hidden_in, inverse_one = hidden_ext[HALO:], inverse_ext[HALO:]
    normed, shared = normed_ext[HALO:], shared_ext[HALO:]

    projected = jnp.dot(shared_ext, first_weights, preferred_element_type=f32)
    gating = projected[HALO:, :MI]
    padded = projected[HALO - (CONV - 1) :, MI : MI + XBC].astype(bf16)
    projections = projected[HALO:, MI + XBC :]

    conv_out = jnp.zeros((tok_rows, XBC), f32)
    for tap_index in range(CONV):
        conv_out = conv_out + padded[tap_index : tap_index + tok_rows].astype(f32) * conv_taps[tap_index][None, :]
    activated = silu(conv_out).astype(bf16).astype(f32)
    inputs_x = activated[:, :MI].reshape(tok_rows, MIXER_HEADS, MP)
    input_b = activated[:, MI : MI + NS]
    input_c = activated[:, MI + NS :]

    def local_states(part_x, part_b, part_c):
        return ssd_local(part_x, part_b, part_c, input_gates, cumulative)

    (local_out, local_end), pull_states = jax.vjp(local_states, inputs_x, input_b, input_c)

    positions = (offset + jnp.arange(tok_rows)).astype(f32)
    queries = rotate(projections[:, :Q_WIDTH].reshape(tok_rows, QH, HD), positions, 1.0).astype(bf16)
    key_local = rotate(
        projections[:, Q_WIDTH : Q_WIDTH + KV_WIDTH].reshape(tok_rows, KH, HD), positions, 1.0
    )
    key_local = key_local.astype(bf16).reshape(tok_rows, KV_WIDTH)
    value_local = projections[:, Q_WIDTH + KV_WIDTH :].astype(bf16)

    key_value = jnp.concatenate([key_local, value_local], axis=0)
    sent = jnp.concatenate(
        [
            local_end.astype(bf16).reshape(CTX, STATE_ROWS, NS),
            jnp.broadcast_to(key_value[None], (CTX, 2 * tok_rows, KV_WIDTH)),
        ],
        axis=1,
    )
    got = swap(sent, "ctx")
    starts = swap(prefix(got[:, :STATE_ROWS], decay_rows, False), "ctx")
    start_state = starts.reshape(MIXER_HEADS, MP, NS).astype(f32)
    key_all = got[:, STATE_ROWS : STATE_ROWS + tok_rows].reshape(CTX * tok_rows, KV_WIDTH)
    value_all = got[:, STATE_ROWS + tok_rows :].reshape(CTX * tok_rows, KV_WIDTH)

    ssd_out = local_out + reach_decay[:, :, None] * jnp.einsum(
        "hpn,tn->thp", start_state, input_c, precision=highest
    )
    ssd_flat = ssd_out.reshape(tok_rows, MI)
    gate_act = silu(gating)
    mamba_in = (ssd_flat * gate_act).astype(bf16)

    grouped = queries.reshape(tok_rows, KH, group_size, HD)
    query_pos = offset + jnp.arange(tok_rows)
    log_total, mixer_output = forward_attend(grouped, query_pos, key_all, value_all)
    attended = mixer_output.reshape(tok_rows, Q_WIDTH).astype(bf16)

    w_mout = rest_weights[:, :192].reshape(MI, D)
    w_aout = rest_weights[:, 192:256].reshape(Q_WIDTH, D)
    w_dn = rest_weights[:, 256:512].reshape(FF, D)
    w_gu = [
        rest_weights[:, 512 + 128 * block : 640 + 128 * block].reshape(D, D) for block in range(4)
    ]
    mamba_out = jnp.dot(mamba_in, w_mout, preferred_element_type=f32)
    attn_out = jnp.dot(attended, w_aout, preferred_element_type=f32)
    residual = hidden_in + attn_out + mamba_out
    inverse_two = lax.rsqrt(jnp.mean(residual * residual, axis=-1, keepdims=True) + epsilon)
    normed_two = residual * inverse_two
    second = (normed_two * gain_second).astype(bf16)
    gate_up = [jnp.dot(second, block, preferred_element_type=f32) for block in w_gu]
    gate_part = jnp.concatenate(gate_up[:2], axis=1)
    up_part = jnp.concatenate(gate_up[2:], axis=1)
    hidden_act = (silu(gate_part) * up_part).astype(bf16)
    result = residual + jnp.dot(hidden_act, w_dn, preferred_element_type=f32)
    output = result.astype(bf16)

    grad_hidden = jnp.einsum("td,fd->tf", grad_out, w_dn, preferred_element_type=f32)
    grad_gu = jnp.concatenate(
        [grad_hidden * up_part * silu_slope(gate_part), grad_hidden * silu(gate_part)], axis=1
    ).astype(bf16)
    first_share = lax.psum_scatter(
        ffn_grads(hidden_act, grad_out, second, grad_gu), "fsdp", scatter_dimension=0, tiled=True
    )[0]
    grad_second = sum(
        jnp.einsum(
            "tf,df->td",
            grad_gu[:, D * block : D * (block + 1)],
            w_gu[block],
            preferred_element_type=f32,
        )
        for block in range(4)
    )
    grad_g_two = jnp.sum(grad_second * normed_two, axis=0)
    grad_residual = grad_out.astype(f32) + rms_back(
        grad_second, normed_two, inverse_two, gain_second
    )
    branch_grad = grad_residual.astype(bf16)
    grad_attended = jnp.einsum("td,qd->tq", branch_grad, w_aout, preferred_element_type=f32)
    grad_mixed = grad_attended.astype(bf16).reshape(tok_rows, KH, group_size, HD)
    grad_mamba_in = jnp.einsum("td,id->ti", branch_grad, w_mout, preferred_element_type=f32)
    grad_ssd = lax.optimization_barrier((grad_mamba_in * gate_act).astype(bf16)).astype(f32)
    grad_ssd = grad_ssd.reshape(tok_rows, MIXER_HEADS, MP)
    grad_gating = grad_mamba_in * ssd_flat * silu_slope(gating)
    direct = jnp.einsum("th,thp,tn->hpn", reach_decay, grad_ssd, input_c, precision=highest)

    empty_grads = jnp.zeros((key_all.shape[0], KV_WIDTH), f32)
    grad_query, grad_keys, grad_values = backward_attend(
        grouped,
        grad_mixed,
        mixer_output,
        log_total,
        query_pos,
        key_all,
        value_all,
        empty_grads,
        empty_grads,
    )
    grad_query = grad_query.reshape(tok_rows, Q_WIDTH)
    sent_back = jnp.concatenate(
        [
            direct.astype(bf16).reshape(CTX, STATE_ROWS, NS),
            grad_keys.astype(bf16).reshape(CTX, tok_rows, KV_WIDTH),
            grad_values.astype(bf16).reshape(CTX, tok_rows, KV_WIDTH),
        ],
        axis=1,
    )
    got_back = swap(sent_back, "ctx")
    ends = swap(prefix(got_back[:, :STATE_ROWS], decay_rows, True), "ctx")
    carried_back = ends.reshape(MIXER_HEADS, MP, NS).astype(f32)
    shares = jnp.sum(got_back[:, STATE_ROWS:].astype(f32), axis=0)
    key_share, value_share = shares[:tok_rows], shares[tok_rows:]

    grad_x_ssd, grad_b, grad_c = pull_states((grad_ssd, carried_back))
    grad_c = grad_c + jnp.einsum(
        "th,thp,hpn->tn", reach_decay, grad_ssd, start_state, precision=highest
    )
    grad_act = jnp.concatenate([grad_x_ssd.reshape(tok_rows, MI), grad_b, grad_c], axis=1)
    grad_conv_out = (grad_act * silu_slope(conv_out)).astype(bf16)
    ahead_rows = passed_along(grad_conv_out[: CONV - 1], "ctx", -1)
    extended = jnp.concatenate([grad_conv_out, ahead_rows], axis=0)
    grad_conv_in = jnp.zeros((tok_rows, XBC), f32)
    grad_tap_list = []
    for tap_index in range(CONV):
        lead = CONV - 1 - tap_index
        grad_conv_in = grad_conv_in + extended[lead : lead + tok_rows].astype(f32) * conv_taps[tap_index][None, :]
        grad_tap_list.append(
            jnp.sum(
                grad_conv_out.astype(f32) * padded[tap_index : tap_index + tok_rows].astype(f32),
                axis=0,
            )
        )
    grad_conv = jnp.stack(grad_tap_list, axis=0)
    grad_proj_m = jnp.concatenate([grad_gating, grad_conv_in], axis=1).astype(bf16)

    grad_q_pre = rotate(grad_query.reshape(tok_rows, QH, HD) * score_scale, positions, -1.0)
    grad_k_pre = rotate((key_share * score_scale).reshape(tok_rows, KH, HD), positions, -1.0)
    grad_proj_a = jnp.concatenate(
        [
            grad_q_pre.reshape(tok_rows, Q_WIDTH),
            grad_k_pre.reshape(tok_rows, KV_WIDTH),
            value_share,
        ],
        axis=1,
    ).astype(bf16)
    second_share = lax.psum_scatter(
        mix_grads(mamba_in, attended, branch_grad, shared, grad_proj_m, grad_proj_a),
        "fsdp",
        scatter_dimension=0,
        tiled=True,
    )[0]
    grad_proj = jnp.concatenate([grad_proj_m, grad_proj_a], axis=1)
    grad_shared = jnp.einsum("tc,dc->td", grad_proj, first_weights, preferred_element_type=f32)
    grad_g_one = jnp.sum(grad_shared * normed, axis=0)
    grad_tokens = grad_residual + rms_back(grad_shared, normed, inverse_one, gain_first)

    conv_owned = grad_conv.reshape(CONV, OWNERS, XBC // OWNERS).transpose(1, 0, 2)
    small_grads = jnp.concatenate(
        [
            grad_g_one.reshape(OWNERS, 128),
            conv_owned.reshape(OWNERS, 896),
            grad_g_two.reshape(OWNERS, 128),
            jnp.zeros((OWNERS, 896), f32),
        ],
        axis=1,
    ).astype(bf16).reshape(OWNERS, 2, D)
    small_got = jnp.sum(swap(small_grads, "fsdp").astype(f32), axis=0).astype(bf16)
    small_rows = jnp.concatenate([small_got, jnp.zeros((14, D), bf16)], axis=0)

    first_sum = ctx_sum(first_share.reshape(CTX, 48, D)).reshape(768, D).astype(f32)
    second_chunks = jnp.concatenate(
        [second_share.reshape(CTX, 48, D), small_rows.reshape(CTX, 1, D)], axis=1
    )
    second_sum = ctx_sum(second_chunks).astype(f32)
    small_sum = second_sum[:2, 48]
    second_sum = second_sum[:, :48].reshape(768, D)

    def widened(blocks):
        return blocks.reshape(4, 128, D).transpose(1, 0, 2).reshape(128, 4 * D)

    in_grads = widened(second_sum[256:])
    return (
        output[None],
        grad_tokens[None],
        small_sum[0, :128],
        in_grads[:, : MI + XBC],
        small_sum[0, 128:].reshape(CONV, XBC // OWNERS).T,
        second_sum[:192],
        in_grads[:, MI + XBC :],
        second_sum[192:256],
        small_sum[1, :128],
        widened(first_sum[256:]),
        first_sum[:256],
    )


def solution(mesh):
    in_specs = (
        P("fsdp", "ctx", None),
        P("fsdp"),
        P("fsdp", None),
        P("fsdp", None),
        P("fsdp", None),
        P("fsdp", None),
        P("fsdp", None),
        P("fsdp"),
        P("fsdp", None),
        P("fsdp", None),
        P("fsdp", "ctx", None),
        P("fsdp", "ctx", None),
        P("fsdp", "ctx", None),
    )
    out_specs = (
        P("fsdp", "ctx", None),
        P("fsdp", "ctx", None),
        P("fsdp"),
        P("fsdp", None),
        P("fsdp", None),
        P("fsdp", None),
        P("fsdp", None),
        P("fsdp", None),
        P("fsdp"),
        P("fsdp", None),
        P("fsdp", None),
    )
    return jax.shard_map(
        on_device, mesh=mesh, in_specs=in_specs, out_specs=out_specs, check_vma=False
    )
```

```python
import functools

import jax
import jax.numpy as jnp
from jax import lax
from jax.experimental import pallas as pl
from jax.experimental.pallas import tpu as pltpu
from jax.sharding import PartitionSpec as P

D = 1024
QH = 8
KH = 2
HD = 64
MIXER_HEADS = 24
MP = 64
NS = 128
CONV = 4
FF = 2048
MI = MIXER_HEADS * MP
XBC = MI + 2 * NS
Q_WIDTH = QH * HD
KV_WIDTH = KH * HD
QKV = Q_WIDTH + 2 * KV_WIDTH
CTX = 16
OWNERS = 8
ROWS = 128
KEYS = CTX * ROWS
HALO = 16
PAIRS = MIXER_HEADS // 2
STATE_ROWS = MI // CTX
SENT_ROWS = STATE_ROWS + 2 * ROWS

epsilon = 1e-05
rope_base = 10000.0
masked_value = -1e30
score_scale = HD ** (-0.5)
bf16 = jnp.bfloat16
f32 = jnp.float32


def passed_along(value, axis, steps):
    count = lax.axis_size(axis)
    leading, last = (max(0, -steps), min(count, count - steps))
    return lax.ppermute(value, axis, [(source, source + steps) for source in range(leading, last)])


def swap(value, axis):
    return lax.all_to_all(value, axis, 0, 0, tiled=True)


def rms_back(grad_normed, normed, inverse, gain):
    scaled = grad_normed * gain
    return inverse * (scaled - normed * jnp.mean(scaled * normed, axis=-1, keepdims=True))


def params():
    return pltpu.CompilerParams(vmem_limit_bytes=60 * 1024 * 1024)


def whole(shape):
    return pl.BlockSpec(shape, lambda *_: (0,) * len(shape))


def struct(shape, dtype):
    return jax.ShapeDtypeStruct(shape, dtype)


def dot(left, right):
    return jnp.dot(left, right, preferred_element_type=f32)


def dot_last(left, right):
    return lax.dot_general(left, right, (((1,), (1,)), ((), ())), preferred_element_type=f32)


def dot_first(left, right):
    return lax.dot_general(left, right, (((0,), (0,)), ((), ())), preferred_element_type=f32)


def lanes(rows=ROWS):
    return lax.broadcasted_iota(jnp.int32, (rows, 128), 1)


def by_head(first, second):
    return jnp.where(lanes() < MP, first, second)


def turned(values):
    ahead = pltpu.roll(values, 96, 1)
    behind = pltpu.roll(values, 32, 1)
    return jnp.where(lax.rem(lanes(), HD) < HD // 2, -ahead, behind)


def half_filled(pair, head):
    group = head // (QH // KH)
    placed = pair if head % 2 == group else pltpu.roll(pair, 64, 1)
    return jnp.where(lanes() // HD == group, placed, 0.0).astype(bf16)


def state_pieces(block, store):
    for piece in range(4):
        row = ROWS * block[0] + 32 * piece
        store(row // STATE_ROWS, row % STATE_ROWS, block[1][32 * piece : 32 * (piece + 1)])


def enter_kernel(
    proj_ref,
    taps_ref,
    cum_ref,
    cum_t_ref,
    gate_ref,
    gate_t_ref,
    cos_ref,
    sin_ref,
    conv_in_ref,
    conv_out_ref,
    act_ref,
    local_ref,
    query_ref,
    sent_ref,
    ext_ref,
):
    for at in range(0, XBC, 256):
        cols = slice(at, at + 256)
        low = proj_ref[:, MI + at : MI + at + 256].astype(bf16)
        conv_in_ref[:, cols] = low
        ext_ref[...] = low.astype(f32)
        conv = jnp.zeros((ROWS, 256), f32)
        for tap in range(CONV):
            start = HALO - (CONV - 1) + tap
            conv = conv + ext_ref[start : start + ROWS, :] * taps_ref[tap : tap + 1, cols]
        conv_out_ref[:, cols] = conv
        act_ref[:, cols] = (conv * jax.nn.sigmoid(conv)).astype(bf16)

    cos, sin = cos_ref[...], sin_ref[...]
    for part in range(QKV // 128):
        at = MI + XBC + 128 * part
        values = proj_ref[HALO:, at : at + 128]
        if part < 5:
            values = values * cos + turned(values) * sin
        if part < 4:
            for head in (2 * part, 2 * part + 1):
                query_ref[head * ROWS : (head + 1) * ROWS] = half_filled(values, head)
        else:
            begin = STATE_ROWS + ROWS * (part - 4)
            low = values.astype(bf16)
            for to in range(CTX):
                sent_ref[to, begin : begin + ROWS] = low

    inputs_b = act_ref[:, MI : MI + NS]
    inputs_c = act_ref[:, MI + NS :]
    products = dot_last(inputs_c, inputs_b)
    row_ids = lax.broadcasted_iota(jnp.int32, (ROWS, ROWS), 0)
    causal = lanes() <= row_ids
    cum = cum_ref[...]
    remain_all = jnp.exp(cum[ROWS - 1 : ROWS] - cum) * gate_ref[...]

    def store(to, row, value):
        sent_ref[to, row : row + 32] = value

    for pair in range(PAIRS):
        cols = slice(128 * pair, 128 * (pair + 1))
        inputs_x = act_ref[:, cols]
        outs = []
        for head in (2 * pair, 2 * pair + 1):
            spread = cum[:, head : head + 1] - cum_t_ref[head : head + 1, :]
            weights = jnp.exp(jnp.where(causal, spread, masked_value))
            mixing = weights * products * gate_t_ref[head : head + 1, :]
            outs.append(dot(mixing.astype(bf16), inputs_x))
        local_ref[:, cols] = by_head(*outs)
        remain = by_head(*(remain_all[:, head : head + 1] for head in (2 * pair, 2 * pair + 1)))
        state = dot_first((inputs_x.astype(f32) * remain).astype(bf16), inputs_b).astype(bf16)
        state_pieces((pair, state), store)


def enter(projected, taps, cum, gates, cos, sin):
    return pl.pallas_call(
        enter_kernel,
        out_shape=(
            struct((ROWS + HALO, XBC), bf16),
            struct((ROWS, XBC), f32),
            struct((ROWS, XBC), bf16),
            struct((ROWS, MI), f32),
            struct((QH * ROWS, 128), bf16),
            struct((CTX, SENT_ROWS, NS), bf16),
        ),
        scratch_shapes=[pltpu.VMEM((ROWS + HALO, 256), f32)],
        compiler_params=params(),
        name="enter",
    )(projected, taps, cum, cum.T, gates, gates.T, cos, sin)


def prefix_kernel(reverse, parts_ref, decay_ref, out_ref):
    running = jnp.zeros(out_ref.shape[1:], f32)
    for at in range(CTX - 1, -1, -1) if reverse else range(CTX):
        out_ref[at] = running.astype(bf16)
        running = decay_ref[at] * running + parts_ref[at].astype(f32)


def prefix(got, decay_rows, reverse):
    return pl.pallas_call(
        functools.partial(prefix_kernel, reverse),
        grid=(1,),
        in_specs=[whole((CTX, STATE_ROWS, NS)), whole((CTX, STATE_ROWS, 1))],
        out_specs=whole((CTX, STATE_ROWS, NS)),
        out_shape=struct((CTX, STATE_ROWS, NS), bf16),
        compiler_params=params(),
        name="state_prefix",
    )(got, decay_rows)


def key_mask(first_row):
    keys = lax.broadcasted_iota(jnp.int32, (KEYS, 4 * ROWS), 0)
    queries = lax.rem(lax.broadcasted_iota(jnp.int32, (KEYS, 4 * ROWS), 1), ROWS)
    return keys <= queries + first_row


def attend_kernel(first_row_ref, query_ref, got_ref, attended_ref, total_ref):
    keys = got_ref[:, STATE_ROWS : STATE_ROWS + ROWS].reshape(KEYS, 128)
    values = got_ref[:, STATE_ROWS + ROWS :].reshape(KEYS, 128)
    allowed = key_mask(first_row_ref[0])
    for group in range(KH):
        queries = query_ref[512 * group : 512 * (group + 1)]
        scores = dot_last(keys, queries) * score_scale
        scores = jnp.where(allowed, scores, masked_value)
        top = jnp.max(scores, axis=0, keepdims=True)
        exponent = jnp.exp(scores - top)
        total = jnp.sum(exponent, axis=0, keepdims=True)
        probs = (exponent * (1.0 / total)).astype(bf16)
        total_ref[group] = jnp.broadcast_to(top + jnp.log(total), (8, 512))
        mixed = dot_first(values, probs)[64 * group : 64 * (group + 1)]
        for part in range(2):
            both = [mixed[:, 128 * (2 * part + k) : 128 * (2 * part + k + 1)] for k in range(2)]
            at = 256 * group + 128 * part
            attended_ref[:, at : at + 128] = jnp.concatenate(both, axis=0).T.astype(bf16)


def attend(first_row, queries, got):
    return pl.pallas_call(
        attend_kernel,
        in_specs=[
            pl.BlockSpec(memory_space=pltpu.SMEM),
            pl.BlockSpec(memory_space=pltpu.VMEM),
            pl.BlockSpec(memory_space=pltpu.VMEM),
        ],
        out_shape=(struct((ROWS, Q_WIDTH), bf16), struct((KH, 8, 512), f32)),
        compiler_params=params(),
        name="attend",
    )(first_row, queries, got)


def leave_kernel(local_ref, starts_ref, act_ref, cum_ref, gating_ref, ssd_ref, mamba_ref):
    inputs_c = act_ref[...]
    reach = jnp.exp(cum_ref[...])
    starts = starts_ref[...].reshape(MI, NS)
    for pair in range(PAIRS):
        cols = slice(128 * pair, 128 * (pair + 1))
        scale = by_head(*(reach[:, head : head + 1] for head in (2 * pair, 2 * pair + 1)))
        out = local_ref[:, cols] + scale * dot_last(inputs_c, starts[cols])
        ssd_ref[:, cols] = out
        gating = gating_ref[HALO:, cols]
        mamba_ref[:, cols] = (out * (gating * jax.nn.sigmoid(gating))).astype(bf16)


def leave(local_out, starts, activated, cum, projected):
    return pl.pallas_call(
        leave_kernel,
        grid=(1,),
        in_specs=[
            whole((ROWS, MI)),
            whole((CTX, STATE_ROWS, NS)),
            pl.BlockSpec((ROWS, NS), lambda i: (0, (MI + NS) // NS)),
            whole((ROWS, MIXER_HEADS)),
            whole((ROWS + HALO, MI)),
        ],
        out_specs=(whole((ROWS, MI)), whole((ROWS, MI))),
        out_shape=(struct((ROWS, MI), f32), struct((ROWS, MI), bf16)),
        compiler_params=params(),
        name="leave",
    )(local_out, starts, activated, cum, projected)


def middle_kernel(
    mamba_ref,
    attended_ref,
    tokens_ref,
    grad_out_ref,
    gain_ref,
    ssd_ref,
    gating_ref,
    rest_ref,
    down_hbm_ref,
    output_ref,
    grad_residual_ref,
    branch_ref,
    grad_gain_ref,
    grad_attended_ref,
    grad_ssd_ref,
    grad_gating_ref,
    early_ref,
    mout_ref,
    aout_ref,
    left_ref,
    right_ref,
    gu_ref,
    own_gu_ref,
    own_down_ref,
    own_mout_ref,
    own_aout_ref,
    sems,
    own_sems,
):
    def fetch(begin, rows, target, sem):
        copy = pltpu.make_async_copy(rest_ref.at[:, pl.ds(begin, rows)], target, sems.at[sem])
        copy.start()
        return copy

    get_mout = fetch(0, 192, mout_ref, 0)
    get_aout = fetch(192, 64, aout_ref, 1)
    get_gu = {}
    for order, block in enumerate((0, 2)):
        get_gu[block] = fetch(384 + 128 * block, 128, gu_ref.at[block], 2 + order)
    get_down = []
    for owner in range(OWNERS):
        source = down_hbm_ref.at[:, pl.ds(16 * owner, 16)]
        get_down.append(pltpu.make_async_copy(source, left_ref.at[owner], sems.at[8 + owner]))
    for side in range(2):
        source = rest_ref.at[:, pl.ds(256, 128), pl.ds(512 * side, 512)]
        target = right_ref.at[:, pl.ds(128 * side, 128)]
        get_down.append(pltpu.make_async_copy(source, target, sems.at[6 + side]))
    for copy in get_down:
        copy.start()
    for order, block in enumerate((1, 3)):
        get_gu[block] = fetch(384 + 128 * block, 128, gu_ref.at[block], 4 + order)

    get_mout.wait()
    mamba_out = dot(mamba_ref[...], mout_ref[...].reshape(MI, D))
    get_aout.wait()
    attn_out = dot(attended_ref[...], aout_ref[...].reshape(Q_WIDTH, D))
    residual = tokens_ref[...].astype(f32) + attn_out + mamba_out
    inverse = lax.rsqrt(jnp.mean(residual * residual, axis=-1, keepdims=True) + epsilon)
    normed = residual * inverse
    gain = gain_ref[...]
    second = (normed * gain).astype(bf16)
    second_turned = second.T
    sending = []

    def send(source, target, sem):
        copy = pltpu.make_async_copy(source, target, own_sems.at[sem])
        copy.start()
        sending.append(copy)

    grad_out = grad_out_ref[...]
    result = jnp.zeros((ROWS, D), f32)
    grad_second = jnp.zeros((ROWS, D), f32)
    for half in range(2):
        get_gu[half].wait()
        get_gu[2 + half].wait()
        w_gate = gu_ref[half].reshape(D, D)
        w_up = gu_ref[2 + half].reshape(D, D)
        gate = dot(second, w_gate)
        up = dot(second, w_up)
        logistic = jax.nn.sigmoid(gate)
        active = gate * logistic
        hidden = (active * up).astype(bf16)
        if half == 0:
            for copy in get_down:
                copy.wait()
        w_left = left_ref[4 * half : 4 * (half + 1)].reshape(D, 512)
        w_right = right_ref[4 * half : 4 * (half + 1)].reshape(D, 512)
        result = result + jnp.concatenate([dot(hidden, w_left), dot(hidden, w_right)], axis=1)
        grad_hidden = dot_last(grad_out[:, :512], w_left) + dot_last(grad_out[:, 512:], w_right)
        slope = logistic * (1.0 + gate * (1.0 - logistic))
        grad_gate = (grad_hidden * up * slope).astype(bf16)
        grad_up = (grad_hidden * active).astype(bf16)
        grad_second = grad_second + dot_last(grad_gate, w_gate) + dot_last(grad_up, w_up)
        while sending:
            sending.pop().wait()
        for side, grads in enumerate((grad_gate, grad_up)):
            own_gu_ref[side] = dot(second_turned, grads).astype(bf16).reshape(OWNERS, 128, D)
            begin = 512 + 128 * (half + 2 * side)
            send(own_gu_ref.at[side], early_ref.at[:, pl.ds(begin, 128)], side)
        own_down_ref[...] = dot_first(hidden, grad_out).astype(bf16).reshape(4, 256, D)
        send(own_down_ref, early_ref.at[pl.ds(4 * half, 4), pl.ds(256, 256)], 2)
    output_ref[...] = (residual + result).astype(bf16)
    grad_gain_ref[...] = jnp.broadcast_to(
        jnp.sum(grad_second * normed, axis=0, keepdims=True), (8, D)
    )
    grad_residual = grad_out.astype(f32) + rms_back(grad_second, normed, inverse, gain)
    grad_residual_ref[...] = grad_residual
    branch = grad_residual.astype(bf16)
    branch_ref[...] = branch
    own_mout_ref[...] = dot_first(mamba_ref[...], branch).astype(bf16).reshape(OWNERS, 192, D)
    send(own_mout_ref, early_ref.at[:, pl.ds(0, 192)], 3)
    own_aout_ref[...] = dot_first(attended_ref[...], branch).astype(bf16).reshape(OWNERS, 64, D)
    send(own_aout_ref, early_ref.at[:, pl.ds(192, 64)], 4)
    grad_attended_ref[...] = dot_last(branch, aout_ref[...].reshape(Q_WIDTH, D)).astype(bf16)
    for at in range(0, MI, 384):
        cols = slice(at, at + 384)
        w_part = mout_ref[at // 192 : at // 192 + 2].reshape(384, D)
        grad_mamba = dot_last(branch, w_part)
        gating = gating_ref[HALO:, cols]
        logistic = jax.nn.sigmoid(gating)
        grad_ssd_ref[:, cols] = (grad_mamba * (gating * logistic)).astype(bf16)
        slope = logistic * (1.0 + gating * (1.0 - logistic))
        grad_gating_ref[:, cols] = (grad_mamba * ssd_ref[:, cols] * slope).astype(bf16)
    while sending:
        sending.pop().wait()


def middle(
    mamba_in, attended, tokens, grad_out, gain, ssd_out, projected, rest_weights, down_weights
):
    return pl.pallas_call(
        middle_kernel,
        grid=(1,),
        in_specs=[
            whole((ROWS, MI)),
            whole((ROWS, Q_WIDTH)),
            whole((ROWS, D)),
            whole((ROWS, D)),
            whole((1, D)),
            whole((ROWS, MI)),
            whole((ROWS + HALO, MI)),
            pl.BlockSpec(memory_space=pl.ANY),
            pl.BlockSpec(memory_space=pl.ANY),
        ],
        out_specs=(
            whole((ROWS, D)),
            whole((ROWS, D)),
            whole((ROWS, D)),
            whole((8, D)),
            whole((ROWS, Q_WIDTH)),
            whole((ROWS, MI)),
            whole((ROWS, MI)),
            pl.BlockSpec(memory_space=pl.ANY),
        ),
        out_shape=(
            struct((ROWS, D), bf16),
            struct((ROWS, D), f32),
            struct((ROWS, D), bf16),
            struct((8, D), f32),
            struct((ROWS, Q_WIDTH), bf16),
            struct((ROWS, MI), bf16),
            struct((ROWS, MI), bf16),
            struct((OWNERS, D, D), bf16),
        ),
        scratch_shapes=[
            pltpu.VMEM((OWNERS, 192, D), bf16),
            pltpu.VMEM((OWNERS, 64, D), bf16),
            pltpu.VMEM((OWNERS, CTX, 16, 512), bf16),
            pltpu.VMEM((OWNERS, 256, 512), bf16),
            pltpu.VMEM((4, OWNERS, 128, D), bf16),
            pltpu.VMEM((2, OWNERS, 128, D), bf16),
            pltpu.VMEM((4, 256, D), bf16),
            pltpu.VMEM((OWNERS, 192, D), bf16),
            pltpu.VMEM((OWNERS, 64, D), bf16),
            pltpu.SemaphoreType.DMA((8 + OWNERS,)),
            pltpu.SemaphoreType.DMA((5,)),
        ],
        compiler_params=params(),
        name="middle",
    )(
        mamba_in,
        attended,
        tokens,
        grad_out,
        gain,
        ssd_out,
        projected,
        rest_weights,
        down_weights,
    )


def attend_back_kernel(
    first_row_ref,
    query_ref,
    got_ref,
    total_ref,
    grad_attended_ref,
    grad_ssd_ref,
    inputs_c_ref,
    cum_ref,
    grad_query_ref,
    sent_ref,
):
    keys = got_ref[:, STATE_ROWS : STATE_ROWS + ROWS].reshape(KEYS, 128)
    values = got_ref[:, STATE_ROWS + ROWS :].reshape(KEYS, 128)
    allowed = key_mask(first_row_ref[0])
    grad_keys = jnp.zeros((KEYS, 128), f32)
    grad_values = jnp.zeros((KEYS, 128), f32)
    for group in range(KH):
        queries = query_ref[512 * group : 512 * (group + 1)]
        grads = []
        for head in range(4 * group, 4 * group + 4):
            pair = grad_attended_ref[:, 128 * (head // 2) : 128 * (head // 2 + 1)].astype(f32)
            grads.append(half_filled(pair, head))
        grads = jnp.concatenate(grads, axis=0)
        scores = dot_last(keys, queries) * score_scale
        scores = jnp.where(allowed, scores, masked_value)
        probs = jnp.exp(scores - total_ref[group, 0:1, :])
        grad_probs = dot_last(values, grads)
        delta = jnp.sum(probs * grad_probs, axis=0, keepdims=True)
        grad_scores = (probs * (grad_probs - delta)).astype(bf16)
        grad_values = grad_values + dot(probs.astype(bf16), grads)
        grad_keys = grad_keys + dot(grad_scores, queries)
        turned_query = dot_first(keys, grad_scores)[64 * group : 64 * (group + 1)]
        for part in range(2):
            both = [
                turned_query[:, 128 * (2 * part + k) : 128 * (2 * part + k + 1)] for k in range(2)
            ]
            at = 256 * group + 128 * part
            grad_query_ref[:, at : at + 128] = jnp.concatenate(both, axis=0).T
    sent_ref[:, STATE_ROWS : STATE_ROWS + ROWS] = grad_keys.astype(bf16).reshape(CTX, ROWS, 128)
    sent_ref[:, STATE_ROWS + ROWS :] = grad_values.astype(bf16).reshape(CTX, ROWS, 128)

    def store(to, row, value):
        sent_ref[to, row : row + 32] = value

    inputs_c = inputs_c_ref[...]
    reach = jnp.exp(cum_ref[...])
    for pair in range(PAIRS):
        cols = slice(128 * pair, 128 * (pair + 1))
        scale = by_head(*(reach[:, head : head + 1] for head in (2 * pair, 2 * pair + 1)))
        scaled = (grad_ssd_ref[:, cols].astype(f32) * scale).astype(bf16)
        state_pieces((pair, dot_first(scaled, inputs_c).astype(bf16)), store)


def attend_back(first_row, queries, got, total, grad_attended, grad_ssd, activated, cum):
    return pl.pallas_call(
        attend_back_kernel,
        grid=(1,),
        in_specs=[
            pl.BlockSpec(memory_space=pltpu.SMEM),
            whole((QH * ROWS, 128)),
            whole((CTX, SENT_ROWS, 128)),
            whole((KH, 8, 512)),
            whole((ROWS, Q_WIDTH)),
            whole((ROWS, MI)),
            pl.BlockSpec((ROWS, NS), lambda i: (0, (MI + NS) // NS)),
            whole((ROWS, MIXER_HEADS)),
        ],
        out_specs=(whole((ROWS, Q_WIDTH)), whole((CTX, SENT_ROWS, NS))),
        out_shape=(struct((ROWS, Q_WIDTH), f32), struct((CTX, SENT_ROWS, NS), bf16)),
        compiler_params=params(),
        name="attend_back",
    )(first_row, queries, got, total, grad_attended, grad_ssd, activated, cum)


def ssd_back_kernel(
    grad_ssd_ref,
    act_ref,
    conv_out_ref,
    cum_ref,
    cum_t_ref,
    gate_ref,
    starts_ref,
    ends_ref,
    grad_query_ref,
    got_ref,
    cos_ref,
    sin_ref,
    grad_conv_ref,
    grad_a_ref,
):
    inputs_b = act_ref[:, MI : MI + NS]
    inputs_c = act_ref[:, MI + NS :]
    products = dot_last(inputs_b, inputs_c)
    row_ids = lax.broadcasted_iota(jnp.int32, (ROWS, ROWS), 0)
    causal = row_ids <= lanes()
    cum = cum_ref[...]
    reach = jnp.exp(cum)
    gates = gate_ref[...]
    remain_all = jnp.exp(cum[ROWS - 1 : ROWS] - cum) * gates
    starts = starts_ref[...].reshape(MI, NS)
    ends = ends_ref[...].reshape(MI, NS)
    grad_products = jnp.zeros((ROWS, ROWS), f32)
    grad_b = jnp.zeros((ROWS, NS), f32)
    grad_c = jnp.zeros((ROWS, NS), f32)

    def through(conv, grad):
        logistic = jax.nn.sigmoid(conv)
        return (grad * (logistic * (1.0 + conv * (1.0 - logistic)))).astype(bf16)

    for pair in range(PAIRS):
        cols = slice(128 * pair, 128 * (pair + 1))
        heads = (2 * pair, 2 * pair + 1)
        inputs_x = act_ref[:, cols]
        grads = grad_ssd_ref[:, cols]
        wide_x = inputs_x.astype(f32)
        back = []
        for side, head in enumerate(heads):
            spread = cum_t_ref[head : head + 1, :] - cum[:, head : head + 1]
            weights = jnp.exp(jnp.where(causal, spread, masked_value)) * gates[:, head : head + 1]
            back.append(dot((weights * products).astype(bf16), grads))
            own = jnp.where(lanes() // MP == side, wide_x, 0.0).astype(bf16)
            grad_products = grad_products + weights * dot_last(own, grads)
        remain = by_head(*(remain_all[:, head : head + 1] for head in heads))
        scale = by_head(*(reach[:, head : head + 1] for head in heads))
        grad_x = by_head(*back) + remain * dot_last(inputs_b, ends[cols])
        grad_conv_ref[:, cols] = through(conv_out_ref[:, cols], grad_x)
        grad_b = grad_b + dot((wide_x * remain).astype(bf16), ends[cols])
        grad_c = grad_c + dot((grads.astype(f32) * scale).astype(bf16), starts[cols])
    low = grad_products.astype(bf16)
    grad_b = grad_b + dot(low, inputs_c)
    grad_c = grad_c + dot_first(low, inputs_b)
    grad_conv_ref[:, MI : MI + NS] = through(conv_out_ref[:, MI : MI + NS], grad_b)
    grad_conv_ref[:, MI + NS :] = through(conv_out_ref[:, MI + NS :], grad_c)

    cos, sin = cos_ref[...], sin_ref[...]
    for part in range(QKV // 128):
        if part < 4:
            values = grad_query_ref[:, 128 * part : 128 * (part + 1)]
        else:
            begin = STATE_ROWS + ROWS * (part - 4)
            values = jnp.sum(got_ref[:, begin : begin + ROWS].astype(f32), axis=0)
        if part < 5:
            values = (values * cos - turned(values) * sin) * score_scale
        grad_a_ref[:, 128 * part : 128 * (part + 1)] = values.astype(bf16)


def ssd_back(grad_ssd, activated, conv_out, cum, gates, starts, ends, grad_query, got, cos, sin):
    return pl.pallas_call(
        ssd_back_kernel,
        out_shape=(struct((ROWS, XBC), bf16), struct((ROWS, QKV), bf16)),
        compiler_params=params(),
        name="ssd_back",
    )(grad_ssd, activated, conv_out, cum, cum.T, gates, starts, ends, grad_query, got, cos, sin)


def conv_back_kernel(grad_ref, ahead_ref, conv_in_ref, taps_ref, out_ref, grad_taps_ref, ext_ref, in_ref):
    for at in range(0, XBC, 256):
        cols = slice(at, at + 256)
        grads = grad_ref[:, cols].astype(f32)
        ext_ref[:ROWS] = grads
        ext_ref[ROWS:] = ahead_ref[:, cols].astype(f32)
        in_ref[...] = conv_in_ref[:, cols].astype(f32)
        total = jnp.zeros((ROWS, 256), f32)
        for tap in range(CONV):
            lead = CONV - 1 - tap
            total = total + ext_ref[lead : lead + ROWS, :] * taps_ref[tap : tap + 1, cols]
            start = HALO - lead
            grad_taps_ref[tap : tap + 1, cols] = jnp.sum(
                grads * in_ref[start : start + ROWS, :], axis=0, keepdims=True
            )
        out_ref[:, cols] = total.astype(bf16)


def conv_back(grad_conv_out, ahead, conv_in, taps):
    return pl.pallas_call(
        conv_back_kernel,
        out_shape=(struct((ROWS, XBC), bf16), struct((CONV, XBC), f32)),
        scratch_shapes=[pltpu.VMEM((ROWS + HALO, 256), f32), pltpu.VMEM((ROWS + HALO, 256), f32)],
        compiler_params=params(),
        name="conv_back",
    )(grad_conv_out, ahead, conv_in, taps)


def late_grads_kernel(shared_ref, grad_ref, out_ref):
    for block in range(4):
        part = dot_first(shared_ref[...], grad_ref[:, D * block : D * (block + 1)]).astype(bf16)
        for owner in range(2):
            out_ref[owner, 128 * block : 128 * (block + 1)] = part[128 * owner : 128 * (owner + 1)]


def late_grads(shared, grad_proj):
    return pl.pallas_call(
        late_grads_kernel,
        grid=(OWNERS // 2,),
        in_specs=[pl.BlockSpec((ROWS, 256), lambda f: (0, f)), whole((ROWS, 4 * D))],
        out_specs=pl.BlockSpec((2, 512, D), lambda f: (f, 0, 0)),
        out_shape=struct((OWNERS, 512, D), bf16),
        compiler_params=params(),
        name="late_grads",
    )(shared, grad_proj)


def fold_kernel(parts_ref, out_ref):
    total = parts_ref[0].astype(f32)
    for part in range(1, CTX):
        total = total + parts_ref[part].astype(f32)
    low = total.astype(bf16)
    for to in range(CTX):
        out_ref[to] = low


def fold(parts):
    rows = parts.shape[1]
    return pl.pallas_call(
        fold_kernel,
        grid=(rows // 16,),
        in_specs=[pl.BlockSpec((CTX, 16, D), lambda i: (0, i, 0))],
        out_specs=pl.BlockSpec((CTX, 16, D), lambda i: (0, i, 0)),
        out_shape=struct(parts.shape, bf16),
        compiler_params=params(),
        name="fold",
    )(parts)


def spread_kernel(parts_ref, mamba_ref, qkv_ref):
    for block in range(4):
        part = parts_ref[4 * block : 4 * (block + 1)].reshape(ROWS, D).astype(f32)
        if block < 3:
            mamba_ref[:, D * block : D * (block + 1)] = part
        else:
            mamba_ref[:, 3 * D :] = part[:, :256]
            qkv_ref[...] = part[:, 256:]


def spread(parts):
    return pl.pallas_call(
        spread_kernel,
        out_shape=(struct((ROWS, MI + XBC), f32), struct((ROWS, QKV), f32)),
        compiler_params=params(),
        name="spread",
    )(parts)


def widened(blocks):
    return blocks.reshape(4, ROWS, D).transpose(1, 0, 2).reshape(ROWS, 4 * D)


def on_device(
    tokens,
    gain_one,
    w_mamba_in,
    conv_weight,
    w_mamba_out,
    w_qkv,
    w_attn_out,
    gain_two,
    w_gate_up,
    w_down,
    decays,
    input_gates,
    grad_out,
):
    tokens = tokens[0]
    decays = decays[0]
    input_gates = input_gates[0]
    grad_out = grad_out[0]
    ctx_index = lax.axis_index("ctx")
    offset = ctx_index * ROWS
    first_row = offset.astype(jnp.int32).reshape(1)

    first_weights = lax.all_gather(
        jnp.concatenate([w_mamba_in, w_qkv], axis=1), "fsdp", axis=0, tiled=True
    )
    rest = jnp.concatenate(
        [
            w_mamba_out,
            w_attn_out,
            jnp.concatenate([w_down[:128, 512:], w_down[128:, 512:]], axis=1),
        ]
        + [w_gate_up[:, D * block : D * (block + 1)] for block in range(4)],
        axis=0,
    )
    small = jnp.concatenate(
        [gain_one, gain_two, conv_weight.T.reshape(-1), jnp.zeros((7 * D - 128,), bf16)]
    )
    piece = lax.dynamic_slice(w_down, (ctx_index * 16, 0), (16, 512))
    piece = jnp.concatenate([piece, small.reshape(16, 512)], axis=0)
    pieces = swap(jnp.broadcast_to(piece[None], (OWNERS, 32, 512)), "fsdp")
    small_all = pieces[:, 16:19].reshape(OWNERS, 3 * 512)[:, :1152]
    gain_first = small_all[:, :128].reshape(1, D).astype(f32)
    gain_second = small_all[:, 128:256].reshape(1, D).astype(f32)
    conv_taps = small_all[:, 256:].reshape(OWNERS, CONV, XBC // OWNERS).transpose(1, 0, 2)
    conv_taps = conv_taps.reshape(CONV, XBC).astype(f32)

    cumulative = jnp.cumsum(jnp.log(decays), axis=0)
    whole_decay = jnp.exp(cumulative[-1:])
    decay_parts = []
    for _ in range(3):
        decay_parts.append(whole_decay.astype(bf16))
        whole_decay = whole_decay - decay_parts[-1].astype(f32)
    decay_parts = jnp.pad(jnp.concatenate(decay_parts, axis=1), ((0, 15), (0, 512 - 72)))
    sent_down = jnp.concatenate([pieces[:, :16].reshape(ROWS, 512), decay_parts], axis=0)
    down_weights = swap(jnp.broadcast_to(sent_down[None], (CTX, ROWS + 16, 512)), "ctx")
    decay_parts = down_weights[:, ROWS, :72].astype(f32)
    decays_all = decay_parts[:, :24] + decay_parts[:, 24:48] + decay_parts[:, 48:]
    decay_rows = lax.dynamic_slice_in_dim(
        jnp.repeat(decays_all, MP, axis=1), ctx_index * STATE_ROWS, STATE_ROWS, 1
    )[:, :, None]

    halo = passed_along(tokens[ROWS - HALO :], "ctx", 1)
    hidden_ext = jnp.concatenate([halo, tokens], axis=0).astype(f32)
    inverse_ext = lax.rsqrt(jnp.mean(hidden_ext * hidden_ext, axis=-1, keepdims=True) + epsilon)
    normed_ext = hidden_ext * inverse_ext
    shared_ext = (normed_ext * gain_first).astype(bf16)
    inverse_one = inverse_ext[HALO:]
    normed, shared = normed_ext[HALO:], shared_ext[HALO:]

    half_dim = HD // 2
    frequency = jnp.exp(-jnp.log(rope_base) * (2.0 * jnp.arange(half_dim).astype(f32) / HD))
    positions = (offset + jnp.arange(ROWS)).astype(f32)
    angles = jnp.tile(positions[:, None] * frequency[None, :], (1, 4))
    cosine, sine = jnp.cos(angles), jnp.sin(angles)

    (
        first_weights,
        decay_rows,
        shared_ext,
        cosine,
        sine,
        conv_taps,
        cumulative,
        rest,
        down_weights,
    ) = lax.optimization_barrier(
        (
            first_weights,
            decay_rows,
            shared_ext,
            cosine,
            sine,
            conv_taps,
            cumulative,
            rest,
            down_weights,
        )
    )
    rest_weights = lax.all_gather(rest, "fsdp", axis=0, tiled=False)
    projected = dot(shared_ext, first_weights)
    conv_in, conv_out, activated, local_out, queries, sent = enter(
        projected, conv_taps, cumulative, input_gates, cosine, sine
    )
    got = swap(sent, "ctx")
    starts = swap(prefix(got, decay_rows, False), "ctx")
    attended, total = attend(first_row, queries, got)
    ssd_out, mamba_in = leave(local_out, starts, activated, cumulative, projected)
    (
        output,
        grad_residual,
        branch_grad,
        grad_g_two,
        grad_attended,
        grad_ssd,
        grad_gating,
        early,
    ) = middle(
        mamba_in,
        attended,
        tokens,
        grad_out,
        gain_second,
        ssd_out,
        projected,
        rest_weights,
        down_weights,
    )
    early_share = lax.psum_scatter(
        early, "fsdp", scatter_dimension=0, tiled=True
    )[0]
    grad_query, sent_back = attend_back(
        first_row, queries, got, total, grad_attended, grad_ssd, activated, cumulative
    )
    got_back = swap(sent_back, "ctx")
    ends = swap(prefix(got_back, decay_rows, True), "ctx")
    grad_conv_out, grad_proj_a = ssd_back(
        grad_ssd,
        activated,
        conv_out,
        cumulative,
        input_gates,
        starts,
        ends,
        grad_query,
        got_back,
        cosine,
        sine,
    )
    ahead = passed_along(grad_conv_out[:HALO], "ctx", -1)
    grad_conv_in, grad_conv = conv_back(grad_conv_out, ahead, conv_in, conv_taps)
    grad_proj = jnp.concatenate([grad_gating, grad_conv_in, grad_proj_a], axis=1)
    grad_shared = dot_last(grad_proj, first_weights)
    grad_g_one = jnp.sum(grad_shared * normed, axis=0)
    grad_tokens = grad_residual + rms_back(grad_shared, normed, inverse_one, gain_first)

    conv_owned = grad_conv.reshape(CONV, OWNERS, XBC // OWNERS).transpose(1, 0, 2)
    small_grads = jnp.concatenate(
        [
            grad_g_one.reshape(OWNERS, 128),
            conv_owned.reshape(OWNERS, 896),
            grad_g_two[0].reshape(OWNERS, 128),
            jnp.zeros((OWNERS, 896), f32),
        ],
        axis=1,
    ).astype(bf16).reshape(OWNERS, 2, D)
    small_got = jnp.sum(swap(small_grads, "fsdp").astype(f32), axis=0).astype(bf16)
    small_got, grad_proj = lax.optimization_barrier((small_got, grad_proj))
    small_sum = swap(jnp.broadcast_to(small_got[None], (CTX, 2, D)), "ctx").astype(f32)
    late_share = lax.psum_scatter(
        late_grads(shared, grad_proj), "fsdp", scatter_dimension=0, tiled=True
    )[0]
    early_share, small_sum = lax.optimization_barrier((early_share, jnp.sum(small_sum, axis=0)))
    early_got = swap(early_share.reshape(CTX, 64, D), "ctx")
    early_sum = swap(fold(early_got), "ctx")
    late_share, early_sum = lax.optimization_barrier((late_share, early_sum))
    late_sum = swap(fold(swap(late_share.reshape(CTX, 32, D), "ctx")), "ctx")
    grad_in, grad_qkv = spread(late_sum)
    early_sum = early_sum.reshape(D, D).astype(f32)
    return (
        output[None],
        grad_tokens[None],
        small_sum[0, :128],
        grad_in,
        small_sum[0, 128:].reshape(CONV, XBC // OWNERS).T,
        early_sum[:192],
        grad_qkv,
        early_sum[192:256],
        small_sum[1, :128],
        widened(early_sum[512:]),
        early_sum[256:512],
    )


def solution(mesh):
    in_specs = (
        P("fsdp", "ctx", None),
        P("fsdp"),
        P("fsdp", None),
        P("fsdp", None),
        P("fsdp", None),
        P("fsdp", None),
        P("fsdp", None),
        P("fsdp"),
        P("fsdp", None),
        P("fsdp", None),
        P("fsdp", "ctx", None),
        P("fsdp", "ctx", None),
        P("fsdp", "ctx", None),
    )
    out_specs = (
        P("fsdp", "ctx", None),
        P("fsdp", "ctx", None),
        P("fsdp"),
        P("fsdp", None),
        P("fsdp", None),
        P("fsdp", None),
        P("fsdp", None),
        P("fsdp", None),
        P("fsdp"),
        P("fsdp", None),
        P("fsdp", None),
    )
    return jax.shard_map(
        on_device, mesh=mesh, in_specs=in_specs, out_specs=out_specs, check_vma=False
    )
```

```python
import functools

import jax
import jax.numpy as jnp
from jax import lax
from jax.experimental import pallas as pl
from jax.experimental.pallas import tpu as pltpu
from jax.sharding import PartitionSpec as P

D = 1024
QH = 8
KH = 2
HD = 64
MIXER_HEADS = 24
MP = 64
NS = 128
CONV = 4
FF = 2048
MI = MIXER_HEADS * MP
XBC = MI + 2 * NS
Q_WIDTH = QH * HD
KV_WIDTH = KH * HD
QKV = Q_WIDTH + 2 * KV_WIDTH
CTX = 16
OWNERS = 8
ROWS = 128
KEYS = CTX * ROWS
HALO = 16
PAIRS = MIXER_HEADS // 2
STATE_ROWS = MI // CTX
SENT_ROWS = STATE_ROWS + 2 * ROWS

epsilon = 1e-05
rope_base = 10000.0
masked_value = -1e30
score_scale = HD ** (-0.5)
bf16 = jnp.bfloat16
f32 = jnp.float32


def passed_along(value, axis, steps):
    count = lax.axis_size(axis)
    leading, last = (max(0, -steps), min(count, count - steps))
    return lax.ppermute(value, axis, [(source, source + steps) for source in range(leading, last)])


def swap(value, axis):
    return lax.all_to_all(value, axis, 0, 0, tiled=True)


def rms_back(grad_normed, normed, inverse, gain):
    scaled = grad_normed * gain
    return inverse * (scaled - normed * jnp.mean(scaled * normed, axis=-1, keepdims=True))


def params():
    return pltpu.CompilerParams(vmem_limit_bytes=60 * 1024 * 1024)


def whole(shape):
    return pl.BlockSpec(shape, lambda *_: (0,) * len(shape))


def struct(shape, dtype):
    return jax.ShapeDtypeStruct(shape, dtype)


def dot(left, right):
    return jnp.dot(left, right, preferred_element_type=f32)


def dot_last(left, right):
    return lax.dot_general(left, right, (((1,), (1,)), ((), ())), preferred_element_type=f32)


def dot_first(left, right):
    return lax.dot_general(left, right, (((0,), (0,)), ((), ())), preferred_element_type=f32)


def lanes(rows=ROWS):
    return lax.broadcasted_iota(jnp.int32, (rows, 128), 1)


def by_head(first, second):
    return jnp.where(lanes() < MP, first, second)


def turned(values):
    ahead = pltpu.roll(values, 96, 1)
    behind = pltpu.roll(values, 32, 1)
    return jnp.where(lax.rem(lanes(), HD) < HD // 2, -ahead, behind)


def half_filled(pair, head):
    group = head // (QH // KH)
    placed = pair if head % 2 == group else pltpu.roll(pair, 64, 1)
    return jnp.where(lanes() // HD == group, placed, 0.0).astype(bf16)


def state_pieces(block, store):
    for piece in range(4):
        row = ROWS * block[0] + 32 * piece
        store(row // STATE_ROWS, row % STATE_ROWS, block[1][32 * piece : 32 * (piece + 1)])


def pack_rest_kernel(mout_ref, aout_ref, down_ref, gu_ref, out_ref):
    out_ref[:192] = mout_ref[...]
    out_ref[192:256] = aout_ref[...]
    for block in range(3):
        for part in range(8):
            rows = slice(256 + 32 * block, 288 + 32 * block)
            out_ref[rows, 128 * part : 128 * (part + 1)] = down_ref[
                32 * part : 32 * (part + 1), 640 + 128 * block : 768 + 128 * block
            ]
    for block in range(4):
        rows = slice(352 + 128 * block, 480 + 128 * block)
        out_ref[rows] = gu_ref[:, D * block : D * (block + 1)]


def pack_rest(w_mamba_out, w_attn_out, w_down, w_gate_up):
    return pl.pallas_call(
        pack_rest_kernel,
        out_shape=struct((864, D), bf16),
        compiler_params=params(),
        name="pack_rest",
    )(w_mamba_out, w_attn_out, w_down, w_gate_up)


def enter_kernel(
    proj_ref,
    taps_ref,
    cum_t_ref,
    gate_t_ref,
    cos_ref,
    sin_ref,
    conv_in_ref,
    conv_out_ref,
    act_ref,
    local_ref,
    query_ref,
    sent_ref,
    ext_ref,
):
    for at in range(0, XBC, 256):
        cols = slice(at, at + 256)
        low = proj_ref[:, MI + at : MI + at + 256].astype(bf16)
        conv_in_ref[:, cols] = low
        ext_ref[...] = low.astype(f32)
        conv = jnp.zeros((ROWS, 256), f32)
        for tap in range(CONV):
            start = HALO - (CONV - 1) + tap
            conv = conv + ext_ref[start : start + ROWS, :] * taps_ref[tap : tap + 1, cols]
        conv_out_ref[:, cols] = conv
        act_ref[:, cols] = (conv * jax.nn.sigmoid(conv)).astype(bf16)

    cos, sin = cos_ref[...], sin_ref[...]
    for part in range(QKV // 128):
        at = MI + XBC + 128 * part
        values = proj_ref[HALO:, at : at + 128]
        if part < 5:
            values = values * cos + turned(values) * sin
        if part < 4:
            for head in (2 * part, 2 * part + 1):
                query_ref[head * ROWS : (head + 1) * ROWS] = half_filled(values, head)
        else:
            begin = STATE_ROWS + ROWS * (part - 4)
            low = values.astype(bf16)
            for to in range(CTX):
                sent_ref[to, begin : begin + ROWS] = low

    inputs_b = act_ref[:, MI : MI + NS]
    inputs_c = act_ref[:, MI + NS :]
    products = dot_last(inputs_c, inputs_b)
    row_ids = lax.broadcasted_iota(jnp.int32, (ROWS, ROWS), 0)
    causal = lanes() <= row_ids
    cum = cum_t_ref[...].T
    remain_all = jnp.exp(cum[ROWS - 1 : ROWS] - cum) * gate_t_ref[...].T

    def store(to, row, value):
        sent_ref[to, row : row + 32] = value

    for pair in range(PAIRS):
        cols = slice(128 * pair, 128 * (pair + 1))
        inputs_x = act_ref[:, cols]
        outs = []
        for head in (2 * pair, 2 * pair + 1):
            spread = cum[:, head : head + 1] - cum_t_ref[head : head + 1, :]
            weights = jnp.exp(jnp.where(causal, spread, masked_value))
            mixing = weights * products * gate_t_ref[head : head + 1, :]
            outs.append(dot(mixing.astype(bf16), inputs_x))
        local_ref[:, cols] = by_head(*outs)
        remain = by_head(*(remain_all[:, head : head + 1] for head in (2 * pair, 2 * pair + 1)))
        state = dot_first((inputs_x.astype(f32) * remain).astype(bf16), inputs_b).astype(bf16)
        state_pieces((pair, state), store)


def enter(projected, taps, cum_t, gate_t, cos, sin):
    return pl.pallas_call(
        enter_kernel,
        out_shape=(
            struct((ROWS + HALO, XBC), bf16),
            struct((ROWS, XBC), f32),
            struct((ROWS, XBC), bf16),
            struct((ROWS, MI), f32),
            struct((QH * ROWS, 128), bf16),
            struct((CTX, SENT_ROWS, NS), bf16),
        ),
        scratch_shapes=[pltpu.VMEM((ROWS + HALO, 256), f32)],
        compiler_params=params(),
        name="enter",
    )(projected, taps, cum_t, gate_t, cos, sin)


def prefix_kernel(reverse, parts_ref, decay_ref, out_ref):
    running = jnp.zeros(out_ref.shape[1:], f32)
    for at in range(CTX - 1, -1, -1) if reverse else range(CTX):
        out_ref[at] = running.astype(bf16)
        running = decay_ref[at] * running + parts_ref[at].astype(f32)


def prefix(got, decay_rows, reverse):
    return pl.pallas_call(
        functools.partial(prefix_kernel, reverse),
        grid=(1,),
        in_specs=[whole((CTX, STATE_ROWS, NS)), whole((CTX, STATE_ROWS, 1))],
        out_specs=whole((CTX, STATE_ROWS, NS)),
        out_shape=struct((CTX, STATE_ROWS, NS), bf16),
        compiler_params=params(),
        name="state_prefix",
    )(got, decay_rows)


def key_mask(first_row):
    keys = lax.broadcasted_iota(jnp.int32, (KEYS, 4 * ROWS), 0)
    queries = lax.rem(lax.broadcasted_iota(jnp.int32, (KEYS, 4 * ROWS), 1), ROWS)
    return keys <= queries + first_row


def attend_kernel(first_row_ref, query_ref, got_ref, attended_ref, total_ref):
    keys = got_ref[:, STATE_ROWS : STATE_ROWS + ROWS].reshape(KEYS, 128)
    values = got_ref[:, STATE_ROWS + ROWS :].reshape(KEYS, 128)
    allowed = key_mask(first_row_ref[0])
    for group in range(KH):
        queries = query_ref[512 * group : 512 * (group + 1)]
        scores = dot_last(keys, queries) * score_scale
        scores = jnp.where(allowed, scores, masked_value)
        top = jnp.max(scores, axis=0, keepdims=True)
        exponent = jnp.exp(scores - top)
        total = jnp.sum(exponent, axis=0, keepdims=True)
        probs = (exponent * (1.0 / total)).astype(bf16)
        total_ref[group] = jnp.broadcast_to(top + jnp.log(total), (8, 512))
        mixed = dot_first(values, probs)[64 * group : 64 * (group + 1)]
        for part in range(2):
            both = [mixed[:, 128 * (2 * part + k) : 128 * (2 * part + k + 1)] for k in range(2)]
            at = 256 * group + 128 * part
            attended_ref[:, at : at + 128] = jnp.concatenate(both, axis=0).T.astype(bf16)


def attend(first_row, queries, got):
    return pl.pallas_call(
        attend_kernel,
        in_specs=[
            pl.BlockSpec(memory_space=pltpu.SMEM),
            pl.BlockSpec(memory_space=pltpu.VMEM),
            pl.BlockSpec(memory_space=pltpu.VMEM),
        ],
        out_shape=(struct((ROWS, Q_WIDTH), bf16), struct((KH, 8, 512), f32)),
        compiler_params=params(),
        name="attend",
    )(first_row, queries, got)


def leave_kernel(local_ref, starts_ref, act_ref, cum_t_ref, gating_ref, ssd_ref, mamba_ref):
    inputs_c = act_ref[...]
    reach = jnp.exp(cum_t_ref[...]).T
    starts = starts_ref[...].reshape(MI, NS)
    for pair in range(PAIRS):
        cols = slice(128 * pair, 128 * (pair + 1))
        scale = by_head(*(reach[:, head : head + 1] for head in (2 * pair, 2 * pair + 1)))
        out = local_ref[:, cols] + scale * dot_last(inputs_c, starts[cols])
        ssd_ref[:, cols] = out
        gating = gating_ref[HALO:, cols]
        mamba_ref[:, cols] = (out * (gating * jax.nn.sigmoid(gating))).astype(bf16)


def leave(local_out, starts, activated, cum, projected):
    return pl.pallas_call(
        leave_kernel,
        grid=(1,),
        in_specs=[
            whole((ROWS, MI)),
            whole((CTX, STATE_ROWS, NS)),
            pl.BlockSpec((ROWS, NS), lambda i: (0, (MI + NS) // NS)),
            whole((MIXER_HEADS, ROWS)),
            whole((ROWS + HALO, MI)),
        ],
        out_specs=(whole((ROWS, MI)), whole((ROWS, MI))),
        out_shape=(struct((ROWS, MI), f32), struct((ROWS, MI), bf16)),
        compiler_params=params(),
        name="leave",
    )(local_out, starts, activated, cum, projected)


def middle_kernel(
    mamba_ref,
    attended_ref,
    tokens_ref,
    grad_out_ref,
    gain_ref,
    ssd_ref,
    gating_ref,
    rest_ref,
    down_hbm_ref,
    middle_hbm_ref,
    output_ref,
    grad_residual_ref,
    branch_ref,
    grad_gain_ref,
    grad_attended_ref,
    grad_ssd_ref,
    grad_gating_ref,
    early_ref,
    mout_ref,
    aout_ref,
    left_ref,
    mid_ref,
    right_ref,
    gu_ref,
    own_gu_ref,
    own_down_ref,
    own_mout_ref,
    own_aout_ref,
    sems,
    own_sems,
):
    def fetch(begin, rows, target, sem):
        copy = pltpu.make_async_copy(rest_ref.at[:, pl.ds(begin, rows)], target, sems.at[sem])
        copy.start()
        return copy

    get_mout = fetch(0, 192, mout_ref, 0)
    get_aout = fetch(192, 64, aout_ref, 1)
    get_gu = {}
    for order, block in enumerate((0, 2)):
        get_gu[block] = fetch(352 + 128 * block, 128, gu_ref.at[block], 2 + order)
    get_down = []
    for owner in range(OWNERS):
        source = down_hbm_ref.at[:, pl.ds(16 * owner, 16)]
        get_down.append(pltpu.make_async_copy(source, left_ref.at[owner], sems.at[6 + owner]))
        source = middle_hbm_ref.at[:, pl.ds(16 * owner, 16)]
        get_down.append(pltpu.make_async_copy(source, mid_ref.at[owner], sems.at[14 + owner]))
    for block in range(3):
        for part in range(8):
            source = rest_ref.at[:, pl.ds(256 + 32 * block, 32), pl.ds(128 * part, 128)]
            target = right_ref.at[:, pl.ds(32 * part, 32), pl.ds(128 * block, 128)]
            sem = sems.at[22 + 8 * block + part]
            get_down.append(pltpu.make_async_copy(source, target, sem))
    for copy in get_down:
        copy.start()
    for order, block in enumerate((1, 3)):
        get_gu[block] = fetch(352 + 128 * block, 128, gu_ref.at[block], 4 + order)

    get_mout.wait()
    mamba_out = dot(mamba_ref[...], mout_ref[...].reshape(MI, D))
    get_aout.wait()
    attn_out = dot(attended_ref[...], aout_ref[...].reshape(Q_WIDTH, D))
    residual = tokens_ref[...].astype(f32) + attn_out + mamba_out
    inverse = lax.rsqrt(jnp.mean(residual * residual, axis=-1, keepdims=True) + epsilon)
    normed = residual * inverse
    gain = gain_ref[...]
    second = (normed * gain).astype(bf16)
    second_turned = second.T
    sending = []

    def send(source, target, sem):
        copy = pltpu.make_async_copy(source, target, own_sems.at[sem])
        copy.start()
        sending.append(copy)

    grad_out = grad_out_ref[...]
    result = jnp.zeros((ROWS, D), f32)
    grad_second = jnp.zeros((ROWS, D), f32)
    for half in range(2):
        get_gu[half].wait()
        get_gu[2 + half].wait()
        w_gate = gu_ref[half].reshape(D, D)
        w_up = gu_ref[2 + half].reshape(D, D)
        gate = dot(second, w_gate)
        up = dot(second, w_up)
        logistic = jax.nn.sigmoid(gate)
        active = gate * logistic
        hidden = (active * up).astype(bf16)
        if half == 0:
            for copy in get_down:
                copy.wait()
        w_left = left_ref[4 * half : 4 * (half + 1)].reshape(D, 384)
        w_right = right_ref[4 * half : 4 * (half + 1)].reshape(D, 384)
        w_mid = mid_ref[4 * half : 4 * (half + 1)].reshape(D, 256)
        result = result + jnp.concatenate(
            [dot(hidden, w_left), dot(hidden, w_mid), dot(hidden, w_right)], axis=1
        )
        grad_hidden = (
            dot_last(grad_out[:, :384], w_left)
            + dot_last(grad_out[:, 384:640], w_mid)
            + dot_last(grad_out[:, 640:], w_right)
        )
        slope = logistic * (1.0 + gate * (1.0 - logistic))
        grad_gate = (grad_hidden * up * slope).astype(bf16)
        grad_up = (grad_hidden * active).astype(bf16)
        grad_second = grad_second + dot_last(grad_gate, w_gate) + dot_last(grad_up, w_up)
        while sending:
            sending.pop().wait()
        for side, grads in enumerate((grad_gate, grad_up)):
            own_gu_ref[side] = dot(second_turned, grads).astype(bf16).reshape(OWNERS, 128, D)
            begin = 512 + 128 * (half + 2 * side)
            send(own_gu_ref.at[side], early_ref.at[:, pl.ds(begin, 128)], side)
        own_down_ref[...] = dot_first(hidden, grad_out).astype(bf16).reshape(4, 256, D)
        send(own_down_ref, early_ref.at[pl.ds(4 * half, 4), pl.ds(256, 256)], 2)
    output_ref[...] = (residual + result).astype(bf16)
    grad_gain_ref[...] = jnp.broadcast_to(
        jnp.sum(grad_second * normed, axis=0, keepdims=True), (8, D)
    )
    grad_residual = grad_out.astype(f32) + rms_back(grad_second, normed, inverse, gain)
    grad_residual_ref[...] = grad_residual
    branch = grad_residual.astype(bf16)
    branch_ref[...] = branch
    own_mout_ref[...] = dot_first(mamba_ref[...], branch).astype(bf16).reshape(OWNERS, 192, D)
    send(own_mout_ref, early_ref.at[:, pl.ds(0, 192)], 3)
    own_aout_ref[...] = dot_first(attended_ref[...], branch).astype(bf16).reshape(OWNERS, 64, D)
    send(own_aout_ref, early_ref.at[:, pl.ds(192, 64)], 4)
    grad_attended_ref[...] = dot_last(branch, aout_ref[...].reshape(Q_WIDTH, D)).astype(bf16)
    for at in range(0, MI, 384):
        cols = slice(at, at + 384)
        w_part = mout_ref[at // 192 : at // 192 + 2].reshape(384, D)
        grad_mamba = dot_last(branch, w_part)
        gating = gating_ref[HALO:, cols]
        logistic = jax.nn.sigmoid(gating)
        grad_ssd_ref[:, cols] = (grad_mamba * (gating * logistic)).astype(bf16)
        slope = logistic * (1.0 + gating * (1.0 - logistic))
        grad_gating_ref[:, cols] = (grad_mamba * ssd_ref[:, cols] * slope).astype(bf16)
    while sending:
        sending.pop().wait()


def middle(
    mamba_in,
    attended,
    tokens,
    grad_out,
    gain,
    ssd_out,
    projected,
    rest_weights,
    down_weights,
    middle_weights,
):
    return pl.pallas_call(
        middle_kernel,
        grid=(1,),
        in_specs=[
            whole((ROWS, MI)),
            whole((ROWS, Q_WIDTH)),
            whole((ROWS, D)),
            whole((ROWS, D)),
            whole((1, D)),
            whole((ROWS, MI)),
            whole((ROWS + HALO, MI)),
            pl.BlockSpec(memory_space=pl.ANY),
            pl.BlockSpec(memory_space=pl.ANY),
            pl.BlockSpec(memory_space=pl.ANY),
        ],
        out_specs=(
            whole((ROWS, D)),
            whole((ROWS, D)),
            whole((ROWS, D)),
            whole((8, D)),
            whole((ROWS, Q_WIDTH)),
            whole((ROWS, MI)),
            whole((ROWS, MI)),
            pl.BlockSpec(memory_space=pl.ANY),
        ),
        out_shape=(
            struct((ROWS, D), bf16),
            struct((ROWS, D), f32),
            struct((ROWS, D), bf16),
            struct((8, D), f32),
            struct((ROWS, Q_WIDTH), bf16),
            struct((ROWS, MI), bf16),
            struct((ROWS, MI), bf16),
            struct((OWNERS, D, D), bf16),
        ),
        scratch_shapes=[
            pltpu.VMEM((OWNERS, 192, D), bf16),
            pltpu.VMEM((OWNERS, 64, D), bf16),
            pltpu.VMEM((OWNERS, CTX, 16, 384), bf16),
            pltpu.VMEM((OWNERS, CTX, 16, 256), bf16),
            pltpu.VMEM((OWNERS, 256, 384), bf16),
            pltpu.VMEM((4, OWNERS, 128, D), bf16),
            pltpu.VMEM((2, OWNERS, 128, D), bf16),
            pltpu.VMEM((4, 256, D), bf16),
            pltpu.VMEM((OWNERS, 192, D), bf16),
            pltpu.VMEM((OWNERS, 64, D), bf16),
            pltpu.SemaphoreType.DMA((46,)),
            pltpu.SemaphoreType.DMA((5,)),
        ],
        compiler_params=params(),
        name="middle",
    )(
        mamba_in,
        attended,
        tokens,
        grad_out,
        gain,
        ssd_out,
        projected,
        rest_weights,
        down_weights,
        middle_weights,
    )


def attend_back_kernel(
    first_row_ref,
    query_ref,
    got_ref,
    total_ref,
    grad_attended_ref,
    grad_ssd_ref,
    inputs_c_ref,
    cum_t_ref,
    grad_query_ref,
    sent_ref,
):
    keys = got_ref[:, STATE_ROWS : STATE_ROWS + ROWS].reshape(KEYS, 128)
    values = got_ref[:, STATE_ROWS + ROWS :].reshape(KEYS, 128)
    allowed = key_mask(first_row_ref[0])
    grad_keys = jnp.zeros((KEYS, 128), f32)
    grad_values = jnp.zeros((KEYS, 128), f32)
    for group in range(KH):
        queries = query_ref[512 * group : 512 * (group + 1)]
        grads = []
        for head in range(4 * group, 4 * group + 4):
            pair = grad_attended_ref[:, 128 * (head // 2) : 128 * (head // 2 + 1)].astype(f32)
            grads.append(half_filled(pair, head))
        grads = jnp.concatenate(grads, axis=0)
        scores = dot_last(keys, queries) * score_scale
        scores = jnp.where(allowed, scores, masked_value)
        probs = jnp.exp(scores - total_ref[group, 0:1, :])
        grad_probs = dot_last(values, grads)
        delta = jnp.sum(probs * grad_probs, axis=0, keepdims=True)
        grad_scores = (probs * (grad_probs - delta)).astype(bf16)
        grad_values = grad_values + dot(probs.astype(bf16), grads)
        grad_keys = grad_keys + dot(grad_scores, queries)
        turned_query = dot_first(keys, grad_scores)[64 * group : 64 * (group + 1)]
        for part in range(2):
            both = [
                turned_query[:, 128 * (2 * part + k) : 128 * (2 * part + k + 1)] for k in range(2)
            ]
            at = 256 * group + 128 * part
            grad_query_ref[:, at : at + 128] = jnp.concatenate(both, axis=0).T
    sent_ref[:, STATE_ROWS : STATE_ROWS + ROWS] = grad_keys.astype(bf16).reshape(CTX, ROWS, 128)
    sent_ref[:, STATE_ROWS + ROWS :] = grad_values.astype(bf16).reshape(CTX, ROWS, 128)

    def store(to, row, value):
        sent_ref[to, row : row + 32] = value

    inputs_c = inputs_c_ref[...]
    reach = jnp.exp(cum_t_ref[...]).T
    for pair in range(PAIRS):
        cols = slice(128 * pair, 128 * (pair + 1))
        scale = by_head(*(reach[:, head : head + 1] for head in (2 * pair, 2 * pair + 1)))
        scaled = (grad_ssd_ref[:, cols].astype(f32) * scale).astype(bf16)
        state_pieces((pair, dot_first(scaled, inputs_c).astype(bf16)), store)


def attend_back(first_row, queries, got, total, grad_attended, grad_ssd, activated, cum):
    return pl.pallas_call(
        attend_back_kernel,
        grid=(1,),
        in_specs=[
            pl.BlockSpec(memory_space=pltpu.SMEM),
            whole((QH * ROWS, 128)),
            whole((CTX, SENT_ROWS, 128)),
            whole((KH, 8, 512)),
            whole((ROWS, Q_WIDTH)),
            whole((ROWS, MI)),
            pl.BlockSpec((ROWS, NS), lambda i: (0, (MI + NS) // NS)),
            whole((MIXER_HEADS, ROWS)),
        ],
        out_specs=(whole((ROWS, Q_WIDTH)), whole((CTX, SENT_ROWS, NS))),
        out_shape=(struct((ROWS, Q_WIDTH), f32), struct((CTX, SENT_ROWS, NS), bf16)),
        compiler_params=params(),
        name="attend_back",
    )(first_row, queries, got, total, grad_attended, grad_ssd, activated, cum)


def ssd_back_kernel(
    grad_ssd_ref,
    act_ref,
    conv_out_ref,
    cum_t_ref,
    gate_t_ref,
    starts_ref,
    ends_ref,
    grad_query_ref,
    got_ref,
    cos_ref,
    sin_ref,
    grad_conv_ref,
    grad_a_ref,
):
    inputs_b = act_ref[:, MI : MI + NS]
    inputs_c = act_ref[:, MI + NS :]
    products = dot_last(inputs_b, inputs_c)
    row_ids = lax.broadcasted_iota(jnp.int32, (ROWS, ROWS), 0)
    causal = row_ids <= lanes()
    cum = cum_t_ref[...].T
    reach = jnp.exp(cum)
    gates = gate_t_ref[...].T
    remain_all = jnp.exp(cum[ROWS - 1 : ROWS] - cum) * gates
    starts = starts_ref[...].reshape(MI, NS)
    ends = ends_ref[...].reshape(MI, NS)
    grad_products = jnp.zeros((ROWS, ROWS), f32)
    grad_b = jnp.zeros((ROWS, NS), f32)
    grad_c = jnp.zeros((ROWS, NS), f32)

    def through(conv, grad):
        logistic = jax.nn.sigmoid(conv)
        return (grad * (logistic * (1.0 + conv * (1.0 - logistic)))).astype(bf16)

    for pair in range(PAIRS):
        cols = slice(128 * pair, 128 * (pair + 1))
        heads = (2 * pair, 2 * pair + 1)
        inputs_x = act_ref[:, cols]
        grads = grad_ssd_ref[:, cols]
        wide_x = inputs_x.astype(f32)
        back = []
        for side, head in enumerate(heads):
            spread = cum_t_ref[head : head + 1, :] - cum[:, head : head + 1]
            weights = jnp.exp(jnp.where(causal, spread, masked_value)) * gates[:, head : head + 1]
            back.append(dot((weights * products).astype(bf16), grads))
            own = jnp.where(lanes() // MP == side, wide_x, 0.0).astype(bf16)
            grad_products = grad_products + weights * dot_last(own, grads)
        remain = by_head(*(remain_all[:, head : head + 1] for head in heads))
        scale = by_head(*(reach[:, head : head + 1] for head in heads))
        grad_x = by_head(*back) + remain * dot_last(inputs_b, ends[cols])
        grad_conv_ref[:, cols] = through(conv_out_ref[:, cols], grad_x)
        grad_b = grad_b + dot((wide_x * remain).astype(bf16), ends[cols])
        grad_c = grad_c + dot((grads.astype(f32) * scale).astype(bf16), starts[cols])
    low = grad_products.astype(bf16)
    grad_b = grad_b + dot(low, inputs_c)
    grad_c = grad_c + dot_first(low, inputs_b)
    grad_conv_ref[:, MI : MI + NS] = through(conv_out_ref[:, MI : MI + NS], grad_b)
    grad_conv_ref[:, MI + NS :] = through(conv_out_ref[:, MI + NS :], grad_c)

    cos, sin = cos_ref[...], sin_ref[...]
    for part in range(QKV // 128):
        if part < 4:
            values = grad_query_ref[:, 128 * part : 128 * (part + 1)]
        else:
            begin = STATE_ROWS + ROWS * (part - 4)
            values = jnp.sum(got_ref[:, begin : begin + ROWS].astype(f32), axis=0)
        if part < 5:
            values = (values * cos - turned(values) * sin) * score_scale
        grad_a_ref[:, 128 * part : 128 * (part + 1)] = values.astype(bf16)


def ssd_back(
    grad_ssd, activated, conv_out, cum_t, gate_t, starts, ends, grad_query, got, cos, sin
):
    return pl.pallas_call(
        ssd_back_kernel,
        out_shape=(struct((ROWS, XBC), bf16), struct((ROWS, QKV), bf16)),
        compiler_params=params(),
        name="ssd_back",
    )(grad_ssd, activated, conv_out, cum_t, gate_t, starts, ends, grad_query, got, cos, sin)


def conv_back_kernel(grad_ref, ahead_ref, conv_in_ref, taps_ref, out_ref, grad_taps_ref, ext_ref, in_ref):
    for at in range(0, XBC, 256):
        cols = slice(at, at + 256)
        grads = grad_ref[:, cols].astype(f32)
        ext_ref[:ROWS] = grads
        ext_ref[ROWS:] = ahead_ref[:, cols].astype(f32)
        in_ref[...] = conv_in_ref[:, cols].astype(f32)
        total = jnp.zeros((ROWS, 256), f32)
        for tap in range(CONV):
            lead = CONV - 1 - tap
            total = total + ext_ref[lead : lead + ROWS, :] * taps_ref[tap : tap + 1, cols]
            start = HALO - lead
            grad_taps_ref[tap : tap + 1, cols] = jnp.sum(
                grads * in_ref[start : start + ROWS, :], axis=0, keepdims=True
            )
        out_ref[:, cols] = total.astype(bf16)


def conv_back(grad_conv_out, ahead, conv_in, taps):
    return pl.pallas_call(
        conv_back_kernel,
        out_shape=(struct((ROWS, XBC), bf16), struct((CONV, XBC), f32)),
        scratch_shapes=[pltpu.VMEM((ROWS + HALO, 256), f32), pltpu.VMEM((ROWS + HALO, 256), f32)],
        compiler_params=params(),
        name="conv_back",
    )(grad_conv_out, ahead, conv_in, taps)


def late_grads_kernel(shared_ref, grad_ref, out_ref):
    for block in range(4):
        part = dot_first(shared_ref[...], grad_ref[:, D * block : D * (block + 1)]).astype(bf16)
        for owner in range(2):
            out_ref[owner, 128 * block : 128 * (block + 1)] = part[128 * owner : 128 * (owner + 1)]


def late_grads(shared, grad_proj):
    return pl.pallas_call(
        late_grads_kernel,
        grid=(OWNERS // 2,),
        in_specs=[pl.BlockSpec((ROWS, 256), lambda f: (0, f)), whole((ROWS, 4 * D))],
        out_specs=pl.BlockSpec((2, 512, D), lambda f: (f, 0, 0)),
        out_shape=struct((OWNERS, 512, D), bf16),
        compiler_params=params(),
        name="late_grads",
    )(shared, grad_proj)


def summed(parts_ref):
    total = parts_ref[0].astype(f32)
    for part in range(1, CTX):
        total = total + parts_ref[part].astype(f32)
    return total.astype(bf16)


def early_fold_kernel(parts_ref, small_ref, out_ref):
    out_ref[:64] = summed(parts_ref)
    out_ref[64:] = small_ref[...]


def early_fold(parts, small):
    return pl.pallas_call(
        early_fold_kernel,
        out_shape=struct((80, D), bf16),
        compiler_params=params(),
        name="early_fold",
    )(parts, small)


def fold_kernel(parts_ref, out_ref):
    low = summed(parts_ref)
    for to in range(CTX):
        out_ref[to] = low


def fold(parts):
    return pl.pallas_call(
        fold_kernel,
        out_shape=struct(parts.shape, bf16),
        compiler_params=params(),
        name="fold",
    )(parts)


def early_spread_kernel(parts_ref, mout_ref, aout_ref, down_ref, gu_ref, small_ref):
    for part in range(CTX):
        values = parts_ref[part, :64].astype(f32)
        if part < 3:
            mout_ref[64 * part : 64 * (part + 1)] = values
        elif part < 4:
            aout_ref[...] = values
        elif part < 8:
            down_ref[64 * (part - 4) : 64 * (part - 3)] = values
        else:
            at = D * ((part - 8) // 2)
            row = 64 * (part % 2)
            gu_ref[row : row + 64, at : at + D] = values
    total = parts_ref[0, 64:].astype(f32)
    for part in range(1, CTX):
        total = total + parts_ref[part, 64:].astype(f32)
    small_ref[...] = total


def early_spread(parts):
    return pl.pallas_call(
        early_spread_kernel,
        out_shape=(
            struct((192, D), f32),
            struct((64, D), f32),
            struct((256, D), f32),
            struct((ROWS, 2 * FF), f32),
            struct((16, D), f32),
        ),
        compiler_params=params(),
        name="early_spread",
    )(parts)


def spread_kernel(parts_ref, mamba_ref, qkv_ref):
    for block in range(4):
        part = parts_ref[4 * block : 4 * (block + 1)].reshape(ROWS, D).astype(f32)
        if block < 3:
            mamba_ref[:, D * block : D * (block + 1)] = part
        else:
            mamba_ref[:, 3 * D :] = part[:, :256]
            qkv_ref[...] = part[:, 256:]


def spread(parts):
    return pl.pallas_call(
        spread_kernel,
        out_shape=(struct((ROWS, MI + XBC), f32), struct((ROWS, QKV), f32)),
        compiler_params=params(),
        name="spread",
    )(parts)


def on_device(
    tokens,
    gain_one,
    w_mamba_in,
    conv_weight,
    w_mamba_out,
    w_qkv,
    w_attn_out,
    gain_two,
    w_gate_up,
    w_down,
    decays,
    input_gates,
    grad_out,
):
    tokens = tokens[0]
    decays = decays[0].T
    input_gates = input_gates[0].T
    grad_out = grad_out[0]
    ctx_index = lax.axis_index("ctx")
    offset = ctx_index * ROWS
    first_row = offset.astype(jnp.int32).reshape(1)

    first_weights = lax.all_gather(
        jnp.concatenate([w_mamba_in, w_qkv], axis=1), "fsdp", axis=0, tiled=True
    )
    rest = pack_rest(w_mamba_out, w_attn_out, w_down, w_gate_up)
    small = jnp.concatenate(
        [gain_one, gain_two, conv_weight.T.reshape(-1), jnp.zeros((16 * 640 - 1152,), bf16)]
    )
    piece = lax.dynamic_slice(w_down, (ctx_index * 16, 0), (16, 640))
    piece = jnp.concatenate([piece, small.reshape(16, 640)], axis=0)
    pieces = swap(jnp.broadcast_to(piece[None], (OWNERS, 32, 640)), "fsdp")
    small_all = pieces[:, 16:18].reshape(OWNERS, 1280)[:, :1152]
    gain_first = small_all[:, :128].reshape(1, D).astype(f32)
    gain_second = small_all[:, 128:256].reshape(1, D).astype(f32)
    conv_taps = small_all[:, 256:].reshape(OWNERS, CONV, XBC // OWNERS).transpose(1, 0, 2)
    conv_taps = conv_taps.reshape(CONV, XBC).astype(f32)

    cumulative = jnp.cumsum(jnp.log(decays), axis=1)
    whole_decay = jnp.exp(cumulative[:, -1])[None]
    decay_parts = []
    for _ in range(3):
        decay_parts.append(whole_decay.astype(bf16))
        whole_decay = whole_decay - decay_parts[-1].astype(f32)
    decay_parts = jnp.pad(jnp.concatenate(decay_parts, axis=1), ((0, 15), (0, 384 - 72)))
    sent_down = jnp.concatenate([pieces[:, :16, :384].reshape(ROWS, 384), decay_parts], axis=0)
    down_weights = swap(jnp.broadcast_to(sent_down[None], (CTX, ROWS + 16, 384)), "ctx")
    decay_parts = down_weights[:, ROWS, :72].astype(f32)
    decays_all = decay_parts[:, :24] + decay_parts[:, 24:48] + decay_parts[:, 48:]
    decay_rows = lax.dynamic_slice_in_dim(
        jnp.repeat(decays_all, MP, axis=1), ctx_index * STATE_ROWS, STATE_ROWS, 1
    )[:, :, None]

    halo = passed_along(tokens[ROWS - HALO :], "ctx", 1)
    hidden_ext = jnp.concatenate([halo, tokens], axis=0).astype(f32)
    inverse_ext = lax.rsqrt(jnp.mean(hidden_ext * hidden_ext, axis=-1, keepdims=True) + epsilon)
    normed_ext = hidden_ext * inverse_ext
    shared_ext = (normed_ext * gain_first).astype(bf16)
    inverse_one = inverse_ext[HALO:]
    normed, shared = normed_ext[HALO:], shared_ext[HALO:]

    pair_index = jnp.remainder(jnp.arange(128), HD // 2).astype(f32)
    frequency = jnp.exp(-jnp.log(rope_base) * (2.0 * pair_index / HD))
    positions = (offset + jnp.arange(ROWS)).astype(f32)
    angles = positions[:, None] * frequency[None, :]
    cosine, sine = jnp.cos(angles), jnp.sin(angles)

    (
        first_weights,
        decay_rows,
        shared_ext,
        cosine,
        sine,
        conv_taps,
        cumulative,
        rest,
        down_weights,
        pieces,
    ) = lax.optimization_barrier(
        (
            first_weights,
            decay_rows,
            shared_ext,
            cosine,
            sine,
            conv_taps,
            cumulative,
            rest,
            down_weights,
            pieces,
        )
    )
    sent_middle = jnp.broadcast_to(pieces[None, :, :16, 384:], (CTX, OWNERS, 16, 256))
    middle_weights = swap(sent_middle.reshape(CTX, ROWS, 256), "ctx")
    rest_weights = lax.all_gather(rest, "fsdp", axis=0, tiled=False)
    projected = dot(shared_ext, first_weights)
    conv_in, conv_out, activated, local_out, queries, sent = enter(
        projected, conv_taps, cumulative, input_gates, cosine, sine
    )
    got = swap(sent, "ctx")
    starts = swap(prefix(got, decay_rows, False), "ctx")
    attended, total = attend(first_row, queries, got)
    ssd_out, mamba_in = leave(local_out, starts, activated, cumulative, projected)
    (
        output,
        grad_residual,
        branch_grad,
        grad_g_two,
        grad_attended,
        grad_ssd,
        grad_gating,
        early,
    ) = middle(
        mamba_in,
        attended,
        tokens,
        grad_out,
        gain_second,
        ssd_out,
        projected,
        rest_weights,
        down_weights,
        middle_weights,
    )
    early_share = lax.psum_scatter(
        early, "fsdp", scatter_dimension=0, tiled=True
    )[0]
    grad_query, sent_back = attend_back(
        first_row, queries, got, total, grad_attended, grad_ssd, activated, cumulative
    )
    got_back = swap(sent_back, "ctx")
    ends = swap(prefix(got_back, decay_rows, True), "ctx")
    grad_conv_out, grad_proj_a = ssd_back(
        grad_ssd,
        activated,
        conv_out,
        cumulative,
        input_gates,
        starts,
        ends,
        grad_query,
        got_back,
        cosine,
        sine,
    )
    ahead = passed_along(grad_conv_out[:HALO], "ctx", -1)
    grad_conv_in, grad_conv = conv_back(grad_conv_out, ahead, conv_in, conv_taps)
    grad_proj = jnp.concatenate([grad_gating, grad_conv_in, grad_proj_a], axis=1)
    grad_shared = dot_last(grad_proj, first_weights)
    grad_g_one = jnp.sum(grad_shared * normed, axis=0)
    grad_tokens = grad_residual + rms_back(grad_shared, normed, inverse_one, gain_first)

    conv_owned = grad_conv.reshape(CONV, OWNERS, XBC // OWNERS).transpose(1, 0, 2)
    small_grads = jnp.concatenate(
        [
            grad_g_one.reshape(OWNERS, 128),
            conv_owned.reshape(OWNERS, 896),
            grad_g_two[0].reshape(OWNERS, 128),
            jnp.zeros((OWNERS, 896), f32),
        ],
        axis=1,
    ).astype(bf16).reshape(OWNERS, 2, D)
    small_got = jnp.sum(swap(small_grads, "fsdp").astype(f32), axis=0).astype(bf16)
    late_share = lax.psum_scatter(
        late_grads(shared, grad_proj), "fsdp", scatter_dimension=0, tiled=True
    )[0]
    early_share, small_got = lax.optimization_barrier((early_share, small_got))
    early_got = swap(early_share.reshape(CTX, 64, D), "ctx")
    small_rows = jnp.concatenate([small_got, jnp.zeros((14, D), bf16)], axis=0)
    early_mine = early_fold(early_got, small_rows)
    late_share, early_mine = lax.optimization_barrier((late_share, early_mine))
    early_sum = lax.all_gather(early_mine, "ctx", axis=0, tiled=False)
    late_sum = swap(fold(swap(late_share.reshape(CTX, 32, D), "ctx")), "ctx")
    grad_mout, grad_aout, grad_down, grad_gate_up, small_sum = early_spread(early_sum)
    grad_in, grad_qkv = spread(late_sum)
    return (
        output[None],
        grad_tokens[None],
        small_sum[0, :128],
        grad_in,
        small_sum[0, 128:].reshape(CONV, XBC // OWNERS).T,
        grad_mout,
        grad_qkv,
        grad_aout,
        small_sum[1, :128],
        grad_gate_up,
        grad_down,
    )


def solution(mesh):
    in_specs = (
        P("fsdp", "ctx", None),
        P("fsdp"),
        P("fsdp", None),
        P("fsdp", None),
        P("fsdp", None),
        P("fsdp", None),
        P("fsdp", None),
        P("fsdp"),
        P("fsdp", None),
        P("fsdp", None),
        P("fsdp", "ctx", None),
        P("fsdp", "ctx", None),
        P("fsdp", "ctx", None),
    )
    out_specs = (
        P("fsdp", "ctx", None),
        P("fsdp", "ctx", None),
        P("fsdp"),
        P("fsdp", None),
        P("fsdp", None),
        P("fsdp", None),
        P("fsdp", None),
        P("fsdp", None),
        P("fsdp"),
        P("fsdp", None),
        P("fsdp", None),
    )
    return jax.shard_map(
        on_device, mesh=mesh, in_specs=in_specs, out_specs=out_specs, check_vma=False
    )
```

```python
import functools

import jax
import jax.numpy as jnp
from jax import lax
from jax.experimental import pallas as pl
from jax.experimental.pallas import tpu as pltpu
from jax.sharding import PartitionSpec as P

D = 1024
QH = 8
KH = 2
HD = 64
MIXER_HEADS = 24
MP = 64
NS = 128
CONV = 4
FF = 2048
MI = MIXER_HEADS * MP
XBC = MI + 2 * NS
Q_WIDTH = QH * HD
KV_WIDTH = KH * HD
QKV = Q_WIDTH + 2 * KV_WIDTH
CTX = 16
OWNERS = 8
ROWS = 128
KEYS = CTX * ROWS
HALO = 16
PAIRS = MIXER_HEADS // 2
STATE_ROWS = MI // CTX
SENT_ROWS = STATE_ROWS + 2 * ROWS

epsilon = 1e-05
rope_base = 10000.0
masked_value = -1e30
score_scale = HD ** (-0.5)
bf16 = jnp.bfloat16
f32 = jnp.float32


def passed_along(value, axis, steps):
    count = lax.axis_size(axis)
    leading, last = (max(0, -steps), min(count, count - steps))
    return lax.ppermute(value, axis, [(source, source + steps) for source in range(leading, last)])


def swap(value, axis):
    return lax.all_to_all(value, axis, 0, 0, tiled=True)


def rms_back(grad_normed, normed, inverse, gain):
    scaled = grad_normed * gain
    return inverse * (scaled - normed * jnp.mean(scaled * normed, axis=-1, keepdims=True))


def params():
    return pltpu.CompilerParams(vmem_limit_bytes=60 * 1024 * 1024)


def whole(shape):
    return pl.BlockSpec(shape, lambda *_: (0,) * len(shape))


def struct(shape, dtype):
    return jax.ShapeDtypeStruct(shape, dtype)


def dot(left, right):
    return jnp.dot(left, right, preferred_element_type=f32)


def dot_last(left, right):
    return lax.dot_general(left, right, (((1,), (1,)), ((), ())), preferred_element_type=f32)


def dot_first(left, right):
    return lax.dot_general(left, right, (((0,), (0,)), ((), ())), preferred_element_type=f32)


def lanes(rows=ROWS):
    return lax.broadcasted_iota(jnp.int32, (rows, 128), 1)


def by_head(first, second):
    return jnp.where(lanes() < MP, first, second)


def turned(values):
    ahead = pltpu.roll(values, 96, 1)
    behind = pltpu.roll(values, 32, 1)
    return jnp.where(lax.rem(lanes(), HD) < HD // 2, -ahead, behind)


def half_filled(pair, head):
    group = head // (QH // KH)
    placed = pair if head % 2 == group else pltpu.roll(pair, 64, 1)
    return jnp.where(lanes() // HD == group, placed, 0.0).astype(bf16)


def state_pieces(block, store):
    for piece in range(4):
        row = ROWS * block[0] + 32 * piece
        store(row // STATE_ROWS, row % STATE_ROWS, block[1][32 * piece : 32 * (piece + 1)])


def pack_rest_kernel(mout_ref, aout_ref, down_ref, gu_ref, out_ref):
    out_ref[:192] = mout_ref[...]
    out_ref[192:256] = aout_ref[...]
    for block in range(3):
        for part in range(8):
            rows = slice(256 + 32 * block, 288 + 32 * block)
            out_ref[rows, 128 * part : 128 * (part + 1)] = down_ref[
                32 * part : 32 * (part + 1), 640 + 128 * block : 768 + 128 * block
            ]
    for block in range(4):
        rows = slice(352 + 128 * block, 480 + 128 * block)
        out_ref[rows] = gu_ref[:, D * block : D * (block + 1)]


def pack_rest(w_mamba_out, w_attn_out, w_down, w_gate_up):
    return pl.pallas_call(
        pack_rest_kernel,
        out_shape=struct((864, D), bf16),
        compiler_params=params(),
        name="pack_rest",
    )(w_mamba_out, w_attn_out, w_down, w_gate_up)


def enter_kernel(
    proj_ref,
    taps_ref,
    cum_t_ref,
    gate_t_ref,
    cos_ref,
    sin_ref,
    conv_in_ref,
    conv_out_ref,
    act_ref,
    local_ref,
    query_ref,
    sent_ref,
    ext_ref,
):
    for at in range(0, XBC, 256):
        cols = slice(at, at + 256)
        low = proj_ref[:, MI + at : MI + at + 256].astype(bf16)
        conv_in_ref[:, cols] = low
        ext_ref[...] = low.astype(f32)
        conv = jnp.zeros((ROWS, 256), f32)
        for tap in range(CONV):
            start = HALO - (CONV - 1) + tap
            conv = conv + ext_ref[start : start + ROWS, :] * taps_ref[tap : tap + 1, cols]
        conv_out_ref[:, cols] = conv
        act_ref[:, cols] = (conv * jax.nn.sigmoid(conv)).astype(bf16)

    cos, sin = cos_ref[...], sin_ref[...]
    for part in range(QKV // 128):
        at = MI + XBC + 128 * part
        values = proj_ref[HALO:, at : at + 128]
        if part < 5:
            values = values * cos + turned(values) * sin
        if part < 4:
            for head in (2 * part, 2 * part + 1):
                query_ref[head * ROWS : (head + 1) * ROWS] = half_filled(values, head)
        else:
            begin = STATE_ROWS + ROWS * (part - 4)
            low = values.astype(bf16)
            for to in range(CTX):
                sent_ref[to, begin : begin + ROWS] = low

    inputs_b = act_ref[:, MI : MI + NS]
    inputs_c = act_ref[:, MI + NS :]
    products = dot_last(inputs_c, inputs_b)
    row_ids = lax.broadcasted_iota(jnp.int32, (ROWS, ROWS), 0)
    causal = lanes() <= row_ids
    cum = cum_t_ref[...].T
    remain_all = jnp.exp(cum[ROWS - 1 : ROWS] - cum) * gate_t_ref[...].T

    def store(to, row, value):
        sent_ref[to, row : row + 32] = value

    for pair in range(PAIRS):
        cols = slice(128 * pair, 128 * (pair + 1))
        inputs_x = act_ref[:, cols]
        outs = []
        for head in (2 * pair, 2 * pair + 1):
            spread = cum[:, head : head + 1] - cum_t_ref[head : head + 1, :]
            weights = jnp.exp(jnp.where(causal, spread, masked_value))
            mixing = weights * products * gate_t_ref[head : head + 1, :]
            outs.append(dot(mixing.astype(bf16), inputs_x))
        local_ref[:, cols] = by_head(*outs)
        remain = by_head(*(remain_all[:, head : head + 1] for head in (2 * pair, 2 * pair + 1)))
        state = dot_first((inputs_x.astype(f32) * remain).astype(bf16), inputs_b).astype(bf16)
        state_pieces((pair, state), store)


def enter(projected, taps, cum_t, gate_t, cos, sin):
    return pl.pallas_call(
        enter_kernel,
        out_shape=(
            struct((ROWS + HALO, XBC), bf16),
            struct((ROWS, XBC), f32),
            struct((ROWS, XBC), bf16),
            struct((ROWS, MI), f32),
            struct((QH * ROWS, 128), bf16),
            struct((CTX, SENT_ROWS, NS), bf16),
        ),
        scratch_shapes=[pltpu.VMEM((ROWS + HALO, 256), f32)],
        compiler_params=params(),
        name="enter",
    )(projected, taps, cum_t, gate_t, cos, sin)


def prefix_kernel(reverse, parts_ref, decay_ref, out_ref):
    running = jnp.zeros(out_ref.shape[1:], f32)
    for at in range(CTX - 1, -1, -1) if reverse else range(CTX):
        out_ref[at] = running.astype(bf16)
        running = decay_ref[at] * running + parts_ref[at].astype(f32)


def prefix(got, decay_rows, reverse):
    return pl.pallas_call(
        functools.partial(prefix_kernel, reverse),
        grid=(1,),
        in_specs=[whole((CTX, STATE_ROWS, NS)), whole((CTX, STATE_ROWS, 1))],
        out_specs=whole((CTX, STATE_ROWS, NS)),
        out_shape=struct((CTX, STATE_ROWS, NS), bf16),
        compiler_params=params(),
        name="state_prefix",
    )(got, decay_rows)


def key_mask(first_row):
    keys = lax.broadcasted_iota(jnp.int32, (KEYS, 4 * ROWS), 0)
    queries = lax.rem(lax.broadcasted_iota(jnp.int32, (KEYS, 4 * ROWS), 1), ROWS)
    return keys <= queries + first_row


def attend_kernel(first_row_ref, query_ref, got_ref, attended_ref, total_ref):
    keys = got_ref[:, STATE_ROWS : STATE_ROWS + ROWS].reshape(KEYS, 128)
    values = got_ref[:, STATE_ROWS + ROWS :].reshape(KEYS, 128)
    allowed = key_mask(first_row_ref[0])
    for group in range(KH):
        queries = query_ref[512 * group : 512 * (group + 1)]
        scores = dot_last(keys, queries) * score_scale
        scores = jnp.where(allowed, scores, masked_value)
        top = jnp.max(scores, axis=0, keepdims=True)
        exponent = jnp.exp(scores - top)
        total = jnp.sum(exponent, axis=0, keepdims=True)
        probs = (exponent * (1.0 / total)).astype(bf16)
        total_ref[group] = jnp.broadcast_to(top + jnp.log(total), (8, 512))
        mixed = dot_first(values, probs)[64 * group : 64 * (group + 1)]
        for part in range(2):
            both = [mixed[:, 128 * (2 * part + k) : 128 * (2 * part + k + 1)] for k in range(2)]
            at = 256 * group + 128 * part
            attended_ref[:, at : at + 128] = jnp.concatenate(both, axis=0).T.astype(bf16)


def attend(first_row, queries, got):
    return pl.pallas_call(
        attend_kernel,
        in_specs=[
            pl.BlockSpec(memory_space=pltpu.SMEM),
            pl.BlockSpec(memory_space=pltpu.VMEM),
            pl.BlockSpec(memory_space=pltpu.VMEM),
        ],
        out_shape=(struct((ROWS, Q_WIDTH), bf16), struct((KH, 8, 512), f32)),
        compiler_params=params(),
        name="attend",
    )(first_row, queries, got)


def leave_kernel(local_ref, starts_ref, act_ref, cum_t_ref, gating_ref, ssd_ref, mamba_ref):
    inputs_c = act_ref[...]
    reach = jnp.exp(cum_t_ref[...]).T
    starts = starts_ref[...].reshape(MI, NS)
    for pair in range(PAIRS):
        cols = slice(128 * pair, 128 * (pair + 1))
        scale = by_head(*(reach[:, head : head + 1] for head in (2 * pair, 2 * pair + 1)))
        out = local_ref[:, cols] + scale * dot_last(inputs_c, starts[cols])
        ssd_ref[:, cols] = out
        gating = gating_ref[HALO:, cols]
        mamba_ref[:, cols] = (out * (gating * jax.nn.sigmoid(gating))).astype(bf16)


def leave(local_out, starts, activated, cum, projected):
    return pl.pallas_call(
        leave_kernel,
        grid=(1,),
        in_specs=[
            whole((ROWS, MI)),
            whole((CTX, STATE_ROWS, NS)),
            pl.BlockSpec((ROWS, NS), lambda i: (0, (MI + NS) // NS)),
            whole((MIXER_HEADS, ROWS)),
            whole((ROWS + HALO, MI)),
        ],
        out_specs=(whole((ROWS, MI)), whole((ROWS, MI))),
        out_shape=(struct((ROWS, MI), f32), struct((ROWS, MI), bf16)),
        compiler_params=params(),
        name="leave",
    )(local_out, starts, activated, cum, projected)


def middle_kernel(
    mamba_ref,
    attended_ref,
    tokens_ref,
    grad_out_ref,
    gain_ref,
    rest_ref,
    down_hbm_ref,
    middle_hbm_ref,
    residual_ref,
    hidden_ref,
    grad_residual_ref,
    branch_ref,
    grad_gain_ref,
    early_ref,
    mout_ref,
    aout_ref,
    left_ref,
    mid_ref,
    right_ref,
    gu_ref,
    own_gu_ref,
    own_down_ref,
    own_mout_ref,
    own_aout_ref,
    sems,
    own_sems,
):
    def fetch(begin, rows, target, sem):
        copy = pltpu.make_async_copy(rest_ref.at[:, pl.ds(begin, rows)], target, sems.at[sem])
        copy.start()
        return copy

    get_mout = fetch(0, 192, mout_ref, 0)
    get_aout = fetch(192, 64, aout_ref, 1)
    get_gu = {}
    for order, block in enumerate((0, 2)):
        get_gu[block] = fetch(352 + 128 * block, 128, gu_ref.at[block], 2 + order)
    get_down = []
    for owner in range(OWNERS):
        source = down_hbm_ref.at[:, pl.ds(16 * owner, 16)]
        get_down.append(pltpu.make_async_copy(source, left_ref.at[owner], sems.at[6 + owner]))
        source = middle_hbm_ref.at[:, pl.ds(16 * owner, 16)]
        get_down.append(pltpu.make_async_copy(source, mid_ref.at[owner], sems.at[14 + owner]))
    for block in range(3):
        for part in range(8):
            source = rest_ref.at[:, pl.ds(256 + 32 * block, 32), pl.ds(128 * part, 128)]
            target = right_ref.at[:, pl.ds(32 * part, 32), pl.ds(128 * block, 128)]
            sem = sems.at[22 + 8 * block + part]
            get_down.append(pltpu.make_async_copy(source, target, sem))
    for copy in get_down:
        copy.start()
    for order, block in enumerate((1, 3)):
        get_gu[block] = fetch(352 + 128 * block, 128, gu_ref.at[block], 4 + order)

    get_mout.wait()
    mamba_out = dot(mamba_ref[...], mout_ref[...].reshape(MI, D))
    get_aout.wait()
    attn_out = dot(attended_ref[...], aout_ref[...].reshape(Q_WIDTH, D))
    residual = tokens_ref[...].astype(f32) + attn_out + mamba_out
    inverse = lax.rsqrt(jnp.mean(residual * residual, axis=-1, keepdims=True) + epsilon)
    normed = residual * inverse
    gain = gain_ref[...]
    second = (normed * gain).astype(bf16)
    second_turned = second.T
    sending = []

    def send(source, target, sem):
        copy = pltpu.make_async_copy(source, target, own_sems.at[sem])
        copy.start()
        sending.append(copy)

    grad_out = grad_out_ref[...]
    residual_ref[...] = residual
    grad_second = jnp.zeros((ROWS, D), f32)
    for half in range(2):
        get_gu[half].wait()
        get_gu[2 + half].wait()
        w_gate = gu_ref[half].reshape(D, D)
        w_up = gu_ref[2 + half].reshape(D, D)
        gate = dot(second, w_gate)
        up = dot(second, w_up)
        logistic = jax.nn.sigmoid(gate)
        active = gate * logistic
        hidden = (active * up).astype(bf16)
        if half == 0:
            for copy in get_down:
                copy.wait()
        w_left = left_ref[4 * half : 4 * (half + 1)].reshape(D, 384)
        w_right = right_ref[4 * half : 4 * (half + 1)].reshape(D, 384)
        w_mid = mid_ref[4 * half : 4 * (half + 1)].reshape(D, 256)
        hidden_ref[:, D * half : D * (half + 1)] = hidden
        grad_hidden = (
            dot_last(grad_out[:, :384], w_left)
            + dot_last(grad_out[:, 384:640], w_mid)
            + dot_last(grad_out[:, 640:], w_right)
        )
        slope = logistic * (1.0 + gate * (1.0 - logistic))
        grad_gate = (grad_hidden * up * slope).astype(bf16)
        grad_up = (grad_hidden * active).astype(bf16)
        grad_second = grad_second + dot_last(grad_gate, w_gate) + dot_last(grad_up, w_up)
        while sending:
            sending.pop().wait()
        for side, grads in enumerate((grad_gate, grad_up)):
            own_gu_ref[side] = dot(second_turned, grads).astype(bf16).reshape(OWNERS, 128, D)
            begin = 512 + 128 * (half + 2 * side)
            send(own_gu_ref.at[side], early_ref.at[:, pl.ds(begin, 128)], side)
        own_down_ref[...] = dot_first(hidden, grad_out).astype(bf16).reshape(4, 256, D)
        send(own_down_ref, early_ref.at[pl.ds(4 * half, 4), pl.ds(256, 256)], 2)
    grad_gain_ref[...] = jnp.broadcast_to(
        jnp.sum(grad_second * normed, axis=0, keepdims=True), (8, D)
    )
    grad_residual = grad_out.astype(f32) + rms_back(grad_second, normed, inverse, gain)
    grad_residual_ref[...] = grad_residual
    branch = grad_residual.astype(bf16)
    branch_ref[...] = branch
    own_mout_ref[...] = dot_first(mamba_ref[...], branch).astype(bf16).reshape(OWNERS, 192, D)
    send(own_mout_ref, early_ref.at[:, pl.ds(0, 192)], 3)
    own_aout_ref[...] = dot_first(attended_ref[...], branch).astype(bf16).reshape(OWNERS, 64, D)
    send(own_aout_ref, early_ref.at[:, pl.ds(192, 64)], 4)
    while sending:
        sending.pop().wait()


def middle(
    mamba_in,
    attended,
    tokens,
    grad_out,
    gain,
    rest_weights,
    down_weights,
    middle_weights,
):
    return pl.pallas_call(
        middle_kernel,
        grid=(1,),
        in_specs=[
            whole((ROWS, MI)),
            whole((ROWS, Q_WIDTH)),
            whole((ROWS, D)),
            whole((ROWS, D)),
            whole((1, D)),
            pl.BlockSpec(memory_space=pl.ANY),
            pl.BlockSpec(memory_space=pl.ANY),
            pl.BlockSpec(memory_space=pl.ANY),
        ],
        out_specs=(
            whole((ROWS, D)),
            whole((ROWS, FF)),
            whole((ROWS, D)),
            whole((ROWS, D)),
            whole((8, D)),
            pl.BlockSpec(memory_space=pl.ANY),
        ),
        out_shape=(
            struct((ROWS, D), f32),
            struct((ROWS, FF), bf16),
            struct((ROWS, D), f32),
            struct((ROWS, D), bf16),
            struct((8, D), f32),
            struct((OWNERS, D, D), bf16),
        ),
        scratch_shapes=[
            pltpu.VMEM((OWNERS, 192, D), bf16),
            pltpu.VMEM((OWNERS, 64, D), bf16),
            pltpu.VMEM((OWNERS, CTX, 16, 384), bf16),
            pltpu.VMEM((OWNERS, CTX, 16, 256), bf16),
            pltpu.VMEM((OWNERS, 256, 384), bf16),
            pltpu.VMEM((4, OWNERS, 128, D), bf16),
            pltpu.VMEM((2, OWNERS, 128, D), bf16),
            pltpu.VMEM((4, 256, D), bf16),
            pltpu.VMEM((OWNERS, 192, D), bf16),
            pltpu.VMEM((OWNERS, 64, D), bf16),
            pltpu.SemaphoreType.DMA((46,)),
            pltpu.SemaphoreType.DMA((5,)),
        ],
        compiler_params=params(),
        name="middle",
    )(
        mamba_in,
        attended,
        tokens,
        grad_out,
        gain,
        rest_weights,
        down_weights,
        middle_weights,
    )


def branch_back_kernel(
    branch_ref,
    ssd_ref,
    gating_ref,
    rest_ref,
    grad_attended_ref,
    grad_ssd_ref,
    grad_gating_ref,
    mout_ref,
    aout_ref,
    sems,
):
    get_mout = pltpu.make_async_copy(rest_ref.at[:, pl.ds(0, 192)], mout_ref, sems.at[0])
    get_aout = pltpu.make_async_copy(rest_ref.at[:, pl.ds(192, 64)], aout_ref, sems.at[1])
    get_mout.start()
    get_aout.start()
    branch = branch_ref[...]
    get_mout.wait()
    get_aout.wait()
    grad_attended_ref[...] = dot_last(branch, aout_ref[...].reshape(Q_WIDTH, D)).astype(bf16)
    for at in range(0, MI, 384):
        cols = slice(at, at + 384)
        w_part = mout_ref[at // 192 : at // 192 + 2].reshape(384, D)
        grad_mamba = dot_last(branch, w_part)
        gating = gating_ref[HALO:, cols]
        logistic = jax.nn.sigmoid(gating)
        grad_ssd_ref[:, cols] = (grad_mamba * (gating * logistic)).astype(bf16)
        slope = logistic * (1.0 + gating * (1.0 - logistic))
        grad_gating_ref[:, cols] = (grad_mamba * ssd_ref[:, cols] * slope).astype(bf16)


def branch_back(branch_grad, ssd_out, projected, rest_weights):
    return pl.pallas_call(
        branch_back_kernel,
        grid=(1,),
        in_specs=[
            whole((ROWS, D)),
            whole((ROWS, MI)),
            whole((ROWS + HALO, MI)),
            pl.BlockSpec(memory_space=pl.ANY),
        ],
        out_specs=(whole((ROWS, Q_WIDTH)), whole((ROWS, MI)), whole((ROWS, MI))),
        out_shape=(
            struct((ROWS, Q_WIDTH), bf16),
            struct((ROWS, MI), bf16),
            struct((ROWS, MI), bf16),
        ),
        scratch_shapes=[
            pltpu.VMEM((OWNERS, 192, D), bf16),
            pltpu.VMEM((OWNERS, 64, D), bf16),
            pltpu.SemaphoreType.DMA((2,)),
        ],
        compiler_params=params(),
        name="branch_back",
    )(branch_grad, ssd_out, projected, rest_weights)


def finish_kernel(
    hidden_ref,
    residual_ref,
    rest_ref,
    left_hbm_ref,
    mid_hbm_ref,
    output_ref,
    left_ref,
    mid_ref,
    right_ref,
    sems,
):
    copies = []
    for owner in range(OWNERS):
        rows = pl.ds(16 * owner, 16)
        sem = sems.at[owner]
        copies.append(pltpu.make_async_copy(left_hbm_ref.at[:, rows], left_ref.at[owner], sem))
        sem = sems.at[OWNERS + owner]
        copies.append(pltpu.make_async_copy(mid_hbm_ref.at[:, rows], mid_ref.at[owner], sem))
    for block in range(3):
        for part in range(8):
            source = rest_ref.at[:, pl.ds(256 + 32 * block, 32), pl.ds(128 * part, 128)]
            target = right_ref.at[:, pl.ds(32 * part, 32), pl.ds(128 * block, 128)]
            sem = sems.at[2 * OWNERS + 8 * block + part]
            copies.append(pltpu.make_async_copy(source, target, sem))
    for copy in copies:
        copy.start()
    hidden = hidden_ref[...]
    residual = residual_ref[...]
    for copy in copies:
        copy.wait()
    left = dot(hidden, left_ref[...].reshape(FF, 384))
    mid = dot(hidden, mid_ref[...].reshape(FF, 256))
    right = dot(hidden, right_ref[...].reshape(FF, 384))
    output_ref[...] = (residual + jnp.concatenate([left, mid, right], axis=1)).astype(bf16)


def finish(hidden_act, residual, rest_weights, down_weights, middle_weights):
    return pl.pallas_call(
        finish_kernel,
        grid=(1,),
        in_specs=[
            whole((ROWS, FF)),
            whole((ROWS, D)),
            pl.BlockSpec(memory_space=pl.ANY),
            pl.BlockSpec(memory_space=pl.ANY),
            pl.BlockSpec(memory_space=pl.ANY),
        ],
        out_specs=whole((ROWS, D)),
        out_shape=struct((ROWS, D), bf16),
        scratch_shapes=[
            pltpu.VMEM((OWNERS, CTX, 16, 384), bf16),
            pltpu.VMEM((OWNERS, CTX, 16, 256), bf16),
            pltpu.VMEM((OWNERS, 256, 384), bf16),
            pltpu.SemaphoreType.DMA((40,)),
        ],
        compiler_params=params(),
        name="finish",
    )(hidden_act, residual, rest_weights, down_weights, middle_weights)


def attend_back_kernel(
    first_row_ref,
    query_ref,
    got_ref,
    total_ref,
    grad_attended_ref,
    grad_ssd_ref,
    inputs_c_ref,
    cum_t_ref,
    grad_query_ref,
    sent_ref,
):
    keys = got_ref[:, STATE_ROWS : STATE_ROWS + ROWS].reshape(KEYS, 128)
    values = got_ref[:, STATE_ROWS + ROWS :].reshape(KEYS, 128)
    allowed = key_mask(first_row_ref[0])
    grad_keys = jnp.zeros((KEYS, 128), f32)
    grad_values = jnp.zeros((KEYS, 128), f32)
    for group in range(KH):
        queries = query_ref[512 * group : 512 * (group + 1)]
        grads = []
        for head in range(4 * group, 4 * group + 4):
            pair = grad_attended_ref[:, 128 * (head // 2) : 128 * (head // 2 + 1)].astype(f32)
            grads.append(half_filled(pair, head))
        grads = jnp.concatenate(grads, axis=0)
        scores = dot_last(keys, queries) * score_scale
        scores = jnp.where(allowed, scores, masked_value)
        probs = jnp.exp(scores - total_ref[group, 0:1, :])
        grad_probs = dot_last(values, grads)
        delta = jnp.sum(probs * grad_probs, axis=0, keepdims=True)
        grad_scores = (probs * (grad_probs - delta)).astype(bf16)
        grad_values = grad_values + dot(probs.astype(bf16), grads)
        grad_keys = grad_keys + dot(grad_scores, queries)
        turned_query = dot_first(keys, grad_scores)[64 * group : 64 * (group + 1)]
        for part in range(2):
            both = [
                turned_query[:, 128 * (2 * part + k) : 128 * (2 * part + k + 1)] for k in range(2)
            ]
            at = 256 * group + 128 * part
            grad_query_ref[:, at : at + 128] = jnp.concatenate(both, axis=0).T
    sent_ref[:, STATE_ROWS : STATE_ROWS + ROWS] = grad_keys.astype(bf16).reshape(CTX, ROWS, 128)
    sent_ref[:, STATE_ROWS + ROWS :] = grad_values.astype(bf16).reshape(CTX, ROWS, 128)

    def store(to, row, value):
        sent_ref[to, row : row + 32] = value

    inputs_c = inputs_c_ref[...]
    reach = jnp.exp(cum_t_ref[...]).T
    for pair in range(PAIRS):
        cols = slice(128 * pair, 128 * (pair + 1))
        scale = by_head(*(reach[:, head : head + 1] for head in (2 * pair, 2 * pair + 1)))
        scaled = (grad_ssd_ref[:, cols].astype(f32) * scale).astype(bf16)
        state_pieces((pair, dot_first(scaled, inputs_c).astype(bf16)), store)


def attend_back(first_row, queries, got, total, grad_attended, grad_ssd, activated, cum):
    return pl.pallas_call(
        attend_back_kernel,
        grid=(1,),
        in_specs=[
            pl.BlockSpec(memory_space=pltpu.SMEM),
            whole((QH * ROWS, 128)),
            whole((CTX, SENT_ROWS, 128)),
            whole((KH, 8, 512)),
            whole((ROWS, Q_WIDTH)),
            whole((ROWS, MI)),
            pl.BlockSpec((ROWS, NS), lambda i: (0, (MI + NS) // NS)),
            whole((MIXER_HEADS, ROWS)),
        ],
        out_specs=(whole((ROWS, Q_WIDTH)), whole((CTX, SENT_ROWS, NS))),
        out_shape=(struct((ROWS, Q_WIDTH), f32), struct((CTX, SENT_ROWS, NS), bf16)),
        compiler_params=params(),
        name="attend_back",
    )(first_row, queries, got, total, grad_attended, grad_ssd, activated, cum)


def ssd_back_kernel(
    grad_ssd_ref,
    act_ref,
    conv_out_ref,
    cum_t_ref,
    gate_t_ref,
    starts_ref,
    ends_ref,
    grad_query_ref,
    got_ref,
    cos_ref,
    sin_ref,
    grad_conv_ref,
    grad_a_ref,
):
    inputs_b = act_ref[:, MI : MI + NS]
    inputs_c = act_ref[:, MI + NS :]
    products = dot_last(inputs_b, inputs_c)
    row_ids = lax.broadcasted_iota(jnp.int32, (ROWS, ROWS), 0)
    causal = row_ids <= lanes()
    cum = cum_t_ref[...].T
    reach = jnp.exp(cum)
    gates = gate_t_ref[...].T
    remain_all = jnp.exp(cum[ROWS - 1 : ROWS] - cum) * gates
    starts = starts_ref[...].reshape(MI, NS)
    ends = ends_ref[...].reshape(MI, NS)
    grad_products = jnp.zeros((ROWS, ROWS), f32)
    grad_b = jnp.zeros((ROWS, NS), f32)
    grad_c = jnp.zeros((ROWS, NS), f32)

    def through(conv, grad):
        logistic = jax.nn.sigmoid(conv)
        return (grad * (logistic * (1.0 + conv * (1.0 - logistic)))).astype(bf16)

    for pair in range(PAIRS):
        cols = slice(128 * pair, 128 * (pair + 1))
        heads = (2 * pair, 2 * pair + 1)
        inputs_x = act_ref[:, cols]
        grads = grad_ssd_ref[:, cols]
        wide_x = inputs_x.astype(f32)
        back = []
        for side, head in enumerate(heads):
            spread = cum_t_ref[head : head + 1, :] - cum[:, head : head + 1]
            weights = jnp.exp(jnp.where(causal, spread, masked_value)) * gates[:, head : head + 1]
            back.append(dot((weights * products).astype(bf16), grads))
            own = jnp.where(lanes() // MP == side, wide_x, 0.0).astype(bf16)
            grad_products = grad_products + weights * dot_last(own, grads)
        remain = by_head(*(remain_all[:, head : head + 1] for head in heads))
        scale = by_head(*(reach[:, head : head + 1] for head in heads))
        grad_x = by_head(*back) + remain * dot_last(inputs_b, ends[cols])
        grad_conv_ref[:, cols] = through(conv_out_ref[:, cols], grad_x)
        grad_b = grad_b + dot((wide_x * remain).astype(bf16), ends[cols])
        grad_c = grad_c + dot((grads.astype(f32) * scale).astype(bf16), starts[cols])
    low = grad_products.astype(bf16)
    grad_b = grad_b + dot(low, inputs_c)
    grad_c = grad_c + dot_first(low, inputs_b)
    grad_conv_ref[:, MI : MI + NS] = through(conv_out_ref[:, MI : MI + NS], grad_b)
    grad_conv_ref[:, MI + NS :] = through(conv_out_ref[:, MI + NS :], grad_c)

    cos, sin = cos_ref[...], sin_ref[...]
    for part in range(QKV // 128):
        if part < 4:
            values = grad_query_ref[:, 128 * part : 128 * (part + 1)]
        else:
            begin = STATE_ROWS + ROWS * (part - 4)
            values = jnp.sum(got_ref[:, begin : begin + ROWS].astype(f32), axis=0)
        if part < 5:
            values = (values * cos - turned(values) * sin) * score_scale
        grad_a_ref[:, 128 * part : 128 * (part + 1)] = values.astype(bf16)


def ssd_back(
    grad_ssd, activated, conv_out, cum_t, gate_t, starts, ends, grad_query, got, cos, sin
):
    return pl.pallas_call(
        ssd_back_kernel,
        out_shape=(struct((ROWS, XBC), bf16), struct((ROWS, QKV), bf16)),
        compiler_params=params(),
        name="ssd_back",
    )(grad_ssd, activated, conv_out, cum_t, gate_t, starts, ends, grad_query, got, cos, sin)


def conv_back_kernel(grad_ref, ahead_ref, conv_in_ref, taps_ref, out_ref, grad_taps_ref, ext_ref, in_ref):
    for at in range(0, XBC, 256):
        cols = slice(at, at + 256)
        grads = grad_ref[:, cols].astype(f32)
        ext_ref[:ROWS] = grads
        ext_ref[ROWS:] = ahead_ref[:, cols].astype(f32)
        in_ref[...] = conv_in_ref[:, cols].astype(f32)
        total = jnp.zeros((ROWS, 256), f32)
        for tap in range(CONV):
            lead = CONV - 1 - tap
            total = total + ext_ref[lead : lead + ROWS, :] * taps_ref[tap : tap + 1, cols]
            start = HALO - lead
            grad_taps_ref[tap : tap + 1, cols] = jnp.sum(
                grads * in_ref[start : start + ROWS, :], axis=0, keepdims=True
            )
        out_ref[:, cols] = total.astype(bf16)


def conv_back(grad_conv_out, ahead, conv_in, taps):
    return pl.pallas_call(
        conv_back_kernel,
        out_shape=(struct((ROWS, XBC), bf16), struct((CONV, XBC), f32)),
        scratch_shapes=[pltpu.VMEM((ROWS + HALO, 256), f32), pltpu.VMEM((ROWS + HALO, 256), f32)],
        compiler_params=params(),
        name="conv_back",
    )(grad_conv_out, ahead, conv_in, taps)


def late_grads_kernel(shared_ref, grad_ref, out_ref):
    for block in range(4):
        part = dot_first(shared_ref[...], grad_ref[:, D * block : D * (block + 1)]).astype(bf16)
        for owner in range(2):
            out_ref[owner, 128 * block : 128 * (block + 1)] = part[128 * owner : 128 * (owner + 1)]


def late_grads(shared, grad_proj):
    return pl.pallas_call(
        late_grads_kernel,
        grid=(OWNERS // 2,),
        in_specs=[pl.BlockSpec((ROWS, 256), lambda f: (0, f)), whole((ROWS, 4 * D))],
        out_specs=pl.BlockSpec((2, 512, D), lambda f: (f, 0, 0)),
        out_shape=struct((OWNERS, 512, D), bf16),
        compiler_params=params(),
        name="late_grads",
    )(shared, grad_proj)


def summed(parts_ref):
    total = parts_ref[0].astype(f32)
    for part in range(1, CTX):
        total = total + parts_ref[part].astype(f32)
    return total.astype(bf16)


def early_fold_kernel(parts_ref, small_ref, out_ref):
    out_ref[:64] = summed(parts_ref)
    out_ref[64:] = small_ref[...]


def early_fold(parts, small):
    return pl.pallas_call(
        early_fold_kernel,
        out_shape=struct((80, D), bf16),
        compiler_params=params(),
        name="early_fold",
    )(parts, small)


def fold_kernel(parts_ref, out_ref):
    low = summed(parts_ref)
    for to in range(CTX):
        out_ref[to] = low


def fold(parts):
    return pl.pallas_call(
        fold_kernel,
        out_shape=struct(parts.shape, bf16),
        compiler_params=params(),
        name="fold",
    )(parts)


def early_spread_kernel(parts_ref, mout_ref, aout_ref, down_ref, gu_ref, small_ref):
    for part in range(CTX):
        values = parts_ref[part, :64].astype(f32)
        if part < 3:
            mout_ref[64 * part : 64 * (part + 1)] = values
        elif part < 4:
            aout_ref[...] = values
        elif part < 8:
            down_ref[64 * (part - 4) : 64 * (part - 3)] = values
        else:
            at = D * ((part - 8) // 2)
            row = 64 * (part % 2)
            gu_ref[row : row + 64, at : at + D] = values
    total = parts_ref[0, 64:].astype(f32)
    for part in range(1, CTX):
        total = total + parts_ref[part, 64:].astype(f32)
    small_ref[...] = total


def early_spread(parts):
    return pl.pallas_call(
        early_spread_kernel,
        out_shape=(
            struct((192, D), f32),
            struct((64, D), f32),
            struct((256, D), f32),
            struct((ROWS, 2 * FF), f32),
            struct((16, D), f32),
        ),
        compiler_params=params(),
        name="early_spread",
    )(parts)


def spread_kernel(parts_ref, mamba_ref, qkv_ref):
    for block in range(4):
        part = parts_ref[4 * block : 4 * (block + 1)].reshape(ROWS, D).astype(f32)
        if block < 3:
            mamba_ref[:, D * block : D * (block + 1)] = part
        else:
            mamba_ref[:, 3 * D :] = part[:, :256]
            qkv_ref[...] = part[:, 256:]


def spread(parts):
    return pl.pallas_call(
        spread_kernel,
        out_shape=(struct((ROWS, MI + XBC), f32), struct((ROWS, QKV), f32)),
        compiler_params=params(),
        name="spread",
    )(parts)


def on_device(
    tokens,
    gain_one,
    w_mamba_in,
    conv_weight,
    w_mamba_out,
    w_qkv,
    w_attn_out,
    gain_two,
    w_gate_up,
    w_down,
    decays,
    input_gates,
    grad_out,
):
    tokens = tokens[0]
    decays = decays[0].T
    input_gates = input_gates[0].T
    grad_out = grad_out[0]
    ctx_index = lax.axis_index("ctx")
    offset = ctx_index * ROWS
    first_row = offset.astype(jnp.int32).reshape(1)

    first_weights = lax.all_gather(
        jnp.concatenate([w_mamba_in, w_qkv], axis=1), "fsdp", axis=0, tiled=True
    )
    rest = pack_rest(w_mamba_out, w_attn_out, w_down, w_gate_up)
    small = jnp.concatenate(
        [gain_one, gain_two, conv_weight.T.reshape(-1), jnp.zeros((16 * 640 - 1152,), bf16)]
    )
    piece = lax.dynamic_slice(w_down, (ctx_index * 16, 0), (16, 640))
    piece = jnp.concatenate([piece, small.reshape(16, 640)], axis=0)
    pieces = swap(jnp.broadcast_to(piece[None], (OWNERS, 32, 640)), "fsdp")
    small_all = pieces[:, 16:18].reshape(OWNERS, 1280)[:, :1152]
    gain_first = small_all[:, :128].reshape(1, D).astype(f32)
    gain_second = small_all[:, 128:256].reshape(1, D).astype(f32)
    conv_taps = small_all[:, 256:].reshape(OWNERS, CONV, XBC // OWNERS).transpose(1, 0, 2)
    conv_taps = conv_taps.reshape(CONV, XBC).astype(f32)

    cumulative = jnp.cumsum(jnp.log(decays), axis=1)
    whole_decay = jnp.exp(cumulative[:, -1])[None]
    decay_parts = []
    for _ in range(3):
        decay_parts.append(whole_decay.astype(bf16))
        whole_decay = whole_decay - decay_parts[-1].astype(f32)
    decay_parts = jnp.pad(jnp.concatenate(decay_parts, axis=1), ((0, 15), (0, 384 - 72)))
    sent_down = jnp.concatenate([pieces[:, :16, :384].reshape(ROWS, 384), decay_parts], axis=0)
    down_weights = swap(jnp.broadcast_to(sent_down[None], (CTX, ROWS + 16, 384)), "ctx")
    decay_parts = down_weights[:, ROWS, :72].astype(f32)
    decays_all = decay_parts[:, :24] + decay_parts[:, 24:48] + decay_parts[:, 48:]
    decay_rows = lax.dynamic_slice_in_dim(
        jnp.repeat(decays_all, MP, axis=1), ctx_index * STATE_ROWS, STATE_ROWS, 1
    )[:, :, None]

    halo = passed_along(tokens[ROWS - HALO :], "ctx", 1)
    hidden_ext = jnp.concatenate([halo, tokens], axis=0).astype(f32)
    inverse_ext = lax.rsqrt(jnp.mean(hidden_ext * hidden_ext, axis=-1, keepdims=True) + epsilon)
    normed_ext = hidden_ext * inverse_ext
    shared_ext = (normed_ext * gain_first).astype(bf16)
    inverse_one = inverse_ext[HALO:]
    normed, shared = normed_ext[HALO:], shared_ext[HALO:]

    pair_index = jnp.remainder(jnp.arange(128), HD // 2).astype(f32)
    frequency = jnp.exp(-jnp.log(rope_base) * (2.0 * pair_index / HD))
    positions = (offset + jnp.arange(ROWS)).astype(f32)
    angles = positions[:, None] * frequency[None, :]
    cosine, sine = jnp.cos(angles), jnp.sin(angles)

    (
        first_weights,
        decay_rows,
        shared_ext,
        cosine,
        sine,
        conv_taps,
        cumulative,
        rest,
        down_weights,
        pieces,
    ) = lax.optimization_barrier(
        (
            first_weights,
            decay_rows,
            shared_ext,
            cosine,
            sine,
            conv_taps,
            cumulative,
            rest,
            down_weights,
            pieces,
        )
    )
    sent_middle = jnp.broadcast_to(pieces[None, :, :16, 384:], (CTX, OWNERS, 16, 256))
    middle_weights = swap(sent_middle.reshape(CTX, ROWS, 256), "ctx")
    rest_weights = lax.all_gather(rest, "fsdp", axis=0, tiled=False)
    projected = dot(shared_ext, first_weights)
    conv_in, conv_out, activated, local_out, queries, sent = enter(
        projected, conv_taps, cumulative, input_gates, cosine, sine
    )
    got = swap(sent, "ctx")
    starts = swap(prefix(got, decay_rows, False), "ctx")
    attended, total = attend(first_row, queries, got)
    ssd_out, mamba_in = leave(local_out, starts, activated, cumulative, projected)
    residual, hidden_act, grad_residual, branch_grad, grad_g_two, early = middle(
        mamba_in,
        attended,
        tokens,
        grad_out,
        gain_second,
        rest_weights,
        down_weights,
        middle_weights,
    )
    early_share = lax.psum_scatter(
        early, "fsdp", scatter_dimension=0, tiled=True
    )[0]
    grad_attended, grad_ssd, grad_gating = branch_back(
        branch_grad, ssd_out, projected, rest_weights
    )
    grad_query, sent_back = attend_back(
        first_row, queries, got, total, grad_attended, grad_ssd, activated, cumulative
    )
    got_back = swap(sent_back, "ctx")
    ends = swap(prefix(got_back, decay_rows, True), "ctx")
    grad_conv_out, grad_proj_a = ssd_back(
        grad_ssd,
        activated,
        conv_out,
        cumulative,
        input_gates,
        starts,
        ends,
        grad_query,
        got_back,
        cosine,
        sine,
    )
    ahead = passed_along(grad_conv_out[:HALO], "ctx", -1)
    grad_conv_in, grad_conv = conv_back(grad_conv_out, ahead, conv_in, conv_taps)
    grad_proj = jnp.concatenate([grad_gating, grad_conv_in, grad_proj_a], axis=1)
    grad_shared = dot_last(grad_proj, first_weights)
    grad_g_one = jnp.sum(grad_shared * normed, axis=0)
    grad_tokens = grad_residual + rms_back(grad_shared, normed, inverse_one, gain_first)

    conv_owned = grad_conv.reshape(CONV, OWNERS, XBC // OWNERS).transpose(1, 0, 2)
    small_grads = jnp.concatenate(
        [
            grad_g_one.reshape(OWNERS, 128),
            conv_owned.reshape(OWNERS, 896),
            grad_g_two[0].reshape(OWNERS, 128),
            jnp.zeros((OWNERS, 896), f32),
        ],
        axis=1,
    ).astype(bf16).reshape(OWNERS, 2, D)
    small_got = jnp.sum(swap(small_grads, "fsdp").astype(f32), axis=0).astype(bf16)
    late_share = lax.psum_scatter(
        late_grads(shared, grad_proj), "fsdp", scatter_dimension=0, tiled=True
    )[0]
    early_share, small_got, hidden_act = lax.optimization_barrier(
        (early_share, small_got, hidden_act)
    )
    output = finish(hidden_act, residual, rest_weights, down_weights, middle_weights)
    early_got = swap(early_share.reshape(CTX, 64, D), "ctx")
    small_rows = jnp.concatenate([small_got, jnp.zeros((14, D), bf16)], axis=0)
    early_mine = early_fold(early_got, small_rows)
    late_share, early_mine = lax.optimization_barrier((late_share, early_mine))
    early_sum = lax.all_gather(early_mine, "ctx", axis=0, tiled=False)
    late_sum = swap(fold(swap(late_share.reshape(CTX, 32, D), "ctx")), "ctx")
    grad_mout, grad_aout, grad_down, grad_gate_up, small_sum = early_spread(early_sum)
    grad_in, grad_qkv = spread(late_sum)
    return (
        output[None],
        grad_tokens[None],
        small_sum[0, :128],
        grad_in,
        small_sum[0, 128:].reshape(CONV, XBC // OWNERS).T,
        grad_mout,
        grad_qkv,
        grad_aout,
        small_sum[1, :128],
        grad_gate_up,
        grad_down,
    )


def solution(mesh):
    in_specs = (
        P("fsdp", "ctx", None),
        P("fsdp"),
        P("fsdp", None),
        P("fsdp", None),
        P("fsdp", None),
        P("fsdp", None),
        P("fsdp", None),
        P("fsdp"),
        P("fsdp", None),
        P("fsdp", None),
        P("fsdp", "ctx", None),
        P("fsdp", "ctx", None),
        P("fsdp", "ctx", None),
    )
    out_specs = (
        P("fsdp", "ctx", None),
        P("fsdp", "ctx", None),
        P("fsdp"),
        P("fsdp", None),
        P("fsdp", None),
        P("fsdp", None),
        P("fsdp", None),
        P("fsdp", None),
        P("fsdp"),
        P("fsdp", None),
        P("fsdp", None),
    )
    return jax.shard_map(
        on_device, mesh=mesh, in_specs=in_specs, out_specs=out_specs, check_vma=False
    )
```

```python
import functools

import jax
import jax.numpy as jnp
from jax import lax
from jax.experimental import pallas as pl
from jax.experimental.pallas import tpu as pltpu
from jax.sharding import PartitionSpec as P

D = 1024
QH = 8
KH = 2
HD = 64
MIXER_HEADS = 24
MP = 64
NS = 128
CONV = 4
FF = 2048
MI = MIXER_HEADS * MP
XBC = MI + 2 * NS
Q_WIDTH = QH * HD
KV_WIDTH = KH * HD
QKV = Q_WIDTH + 2 * KV_WIDTH
CTX = 16
OWNERS = 8
ROWS = 128
KEYS = CTX * ROWS
HALO = 16
PAIRS = MIXER_HEADS // 2
STATE_ROWS = MI // CTX
SENT_ROWS = STATE_ROWS + 2 * ROWS

epsilon = 1e-05
rope_base = 10000.0
masked_value = -1e30
score_scale = HD ** (-0.5)
bf16 = jnp.bfloat16
f32 = jnp.float32


def passed_along(value, axis, steps):
    count = lax.axis_size(axis)
    leading, last = (max(0, -steps), min(count, count - steps))
    return lax.ppermute(value, axis, [(source, source + steps) for source in range(leading, last)])


def swap(value, axis):
    return lax.all_to_all(value, axis, 0, 0, tiled=True)


def rms_back(grad_normed, normed, inverse, gain):
    scaled = grad_normed * gain
    return inverse * (scaled - normed * jnp.mean(scaled * normed, axis=-1, keepdims=True))


def params():
    return pltpu.CompilerParams(vmem_limit_bytes=60 * 1024 * 1024)


def whole(shape):
    return pl.BlockSpec(shape, lambda *_: (0,) * len(shape))


def struct(shape, dtype):
    return jax.ShapeDtypeStruct(shape, dtype)


def dot(left, right):
    return jnp.dot(left, right, preferred_element_type=f32)


def dot_last(left, right):
    return lax.dot_general(left, right, (((1,), (1,)), ((), ())), preferred_element_type=f32)


def dot_first(left, right):
    return lax.dot_general(left, right, (((0,), (0,)), ((), ())), preferred_element_type=f32)


def lanes(rows=ROWS):
    return lax.broadcasted_iota(jnp.int32, (rows, 128), 1)


def by_head(first, second):
    return jnp.where(lanes() < MP, first, second)


def turned(values):
    ahead = pltpu.roll(values, 96, 1)
    behind = pltpu.roll(values, 32, 1)
    return jnp.where(lax.rem(lanes(), HD) < HD // 2, -ahead, behind)


def half_filled(pair, head):
    group = head // (QH // KH)
    placed = pair if head % 2 == group else pltpu.roll(pair, 64, 1)
    return jnp.where(lanes() // HD == group, placed, 0.0).astype(bf16)


def state_pieces(block, store):
    for piece in range(4):
        row = ROWS * block[0] + 32 * piece
        store(row // STATE_ROWS, row % STATE_ROWS, block[1][32 * piece : 32 * (piece + 1)])


def pack_rest_kernel(mout_ref, aout_ref, down_ref, gu_ref, out_ref):
    out_ref[:192] = mout_ref[...]
    out_ref[192:256] = aout_ref[...]
    for block in range(3):
        for part in range(8):
            rows = slice(256 + 32 * block, 288 + 32 * block)
            out_ref[rows, 128 * part : 128 * (part + 1)] = down_ref[
                32 * part : 32 * (part + 1), 640 + 128 * block : 768 + 128 * block
            ]
    for block in range(4):
        rows = slice(352 + 128 * block, 480 + 128 * block)
        out_ref[rows] = gu_ref[:, D * block : D * (block + 1)]


def pack_rest(w_mamba_out, w_attn_out, w_down, w_gate_up):
    return pl.pallas_call(
        pack_rest_kernel,
        out_shape=struct((864, D), bf16),
        compiler_params=params(),
        name="pack_rest",
    )(w_mamba_out, w_attn_out, w_down, w_gate_up)


def enter_kernel(
    proj_ref,
    taps_ref,
    cum_t_ref,
    gate_t_ref,
    cos_ref,
    sin_ref,
    conv_in_ref,
    conv_out_ref,
    act_ref,
    local_ref,
    query_ref,
    sent_ref,
    ext_ref,
):
    for at in range(0, XBC, 256):
        cols = slice(at, at + 256)
        low = proj_ref[:, MI + at : MI + at + 256].astype(bf16)
        conv_in_ref[:, cols] = low
        ext_ref[...] = low.astype(f32)
        conv = jnp.zeros((ROWS, 256), f32)
        for tap in range(CONV):
            start = HALO - (CONV - 1) + tap
            conv = conv + ext_ref[start : start + ROWS, :] * taps_ref[tap : tap + 1, cols]
        conv_out_ref[:, cols] = conv
        act_ref[:, cols] = (conv * jax.nn.sigmoid(conv)).astype(bf16)

    cos, sin = cos_ref[...], sin_ref[...]
    for part in range(QKV // 128):
        at = MI + XBC + 128 * part
        values = proj_ref[HALO:, at : at + 128]
        if part < 5:
            values = values * cos + turned(values) * sin
        if part < 4:
            for head in (2 * part, 2 * part + 1):
                query_ref[head * ROWS : (head + 1) * ROWS] = half_filled(values, head)
        else:
            begin = STATE_ROWS + ROWS * (part - 4)
            low = values.astype(bf16)
            for to in range(CTX):
                sent_ref[to, begin : begin + ROWS] = low

    inputs_b = act_ref[:, MI : MI + NS]
    inputs_c = act_ref[:, MI + NS :]
    products = dot_last(inputs_c, inputs_b)
    row_ids = lax.broadcasted_iota(jnp.int32, (ROWS, ROWS), 0)
    causal = lanes() <= row_ids
    cum = cum_t_ref[...].T
    remain_all = jnp.exp(cum[ROWS - 1 : ROWS] - cum) * gate_t_ref[...].T

    def store(to, row, value):
        sent_ref[to, row : row + 32] = value

    for pair in range(PAIRS):
        cols = slice(128 * pair, 128 * (pair + 1))
        inputs_x = act_ref[:, cols]
        outs = []
        for head in (2 * pair, 2 * pair + 1):
            spread = cum[:, head : head + 1] - cum_t_ref[head : head + 1, :]
            weights = jnp.exp(jnp.where(causal, spread, masked_value))
            mixing = weights * products * gate_t_ref[head : head + 1, :]
            outs.append(dot(mixing.astype(bf16), inputs_x))
        local_ref[:, cols] = by_head(*outs)
        remain = by_head(*(remain_all[:, head : head + 1] for head in (2 * pair, 2 * pair + 1)))
        state = dot_first((inputs_x.astype(f32) * remain).astype(bf16), inputs_b).astype(bf16)
        state_pieces((pair, state), store)


def enter(projected, taps, cum_t, gate_t, cos, sin):
    return pl.pallas_call(
        enter_kernel,
        out_shape=(
            struct((ROWS + HALO, XBC), bf16),
            struct((ROWS, XBC), f32),
            struct((ROWS, XBC), bf16),
            struct((ROWS, MI), f32),
            struct((QH * ROWS, 128), bf16),
            struct((CTX, SENT_ROWS, NS), bf16),
        ),
        scratch_shapes=[pltpu.VMEM((ROWS + HALO, 256), f32)],
        compiler_params=params(),
        name="enter",
    )(projected, taps, cum_t, gate_t, cos, sin)


def prefix_kernel(reverse, parts_ref, decay_ref, out_ref):
    running = jnp.zeros(out_ref.shape[1:], f32)
    for at in range(CTX - 1, -1, -1) if reverse else range(CTX):
        out_ref[at] = running.astype(bf16)
        running = decay_ref[at] * running + parts_ref[at].astype(f32)


def prefix(got, decay_rows, reverse):
    return pl.pallas_call(
        functools.partial(prefix_kernel, reverse),
        grid=(1,),
        in_specs=[whole((CTX, STATE_ROWS, NS)), whole((CTX, STATE_ROWS, 1))],
        out_specs=whole((CTX, STATE_ROWS, NS)),
        out_shape=struct((CTX, STATE_ROWS, NS), bf16),
        compiler_params=params(),
        name="state_prefix",
    )(got, decay_rows)


def key_mask(first_row):
    keys = lax.broadcasted_iota(jnp.int32, (KEYS, 4 * ROWS), 0)
    queries = lax.rem(lax.broadcasted_iota(jnp.int32, (KEYS, 4 * ROWS), 1), ROWS)
    return keys <= queries + first_row


def attend_kernel(first_row_ref, query_ref, got_ref, attended_ref, total_ref):
    keys = got_ref[:, STATE_ROWS : STATE_ROWS + ROWS].reshape(KEYS, 128)
    values = got_ref[:, STATE_ROWS + ROWS :].reshape(KEYS, 128)
    allowed = key_mask(first_row_ref[0])
    for group in range(KH):
        queries = query_ref[512 * group : 512 * (group + 1)]
        scores = dot_last(keys, queries) * score_scale
        scores = jnp.where(allowed, scores, masked_value)
        top = jnp.max(scores, axis=0, keepdims=True)
        exponent = jnp.exp(scores - top)
        total = jnp.sum(exponent, axis=0, keepdims=True)
        probs = (exponent * (1.0 / total)).astype(bf16)
        total_ref[group] = jnp.broadcast_to(top + jnp.log(total), (8, 512))
        mixed = dot_first(values, probs)[64 * group : 64 * (group + 1)]
        for part in range(2):
            both = [mixed[:, 128 * (2 * part + k) : 128 * (2 * part + k + 1)] for k in range(2)]
            at = 256 * group + 128 * part
            attended_ref[:, at : at + 128] = jnp.concatenate(both, axis=0).T.astype(bf16)


def attend(first_row, queries, got):
    return pl.pallas_call(
        attend_kernel,
        in_specs=[
            pl.BlockSpec(memory_space=pltpu.SMEM),
            pl.BlockSpec(memory_space=pltpu.VMEM),
            pl.BlockSpec(memory_space=pltpu.VMEM),
        ],
        out_shape=(struct((ROWS, Q_WIDTH), bf16), struct((KH, 8, 512), f32)),
        compiler_params=params(),
        name="attend",
    )(first_row, queries, got)


def leave_kernel(local_ref, starts_ref, act_ref, cum_t_ref, gating_ref, ssd_ref, mamba_ref):
    inputs_c = act_ref[...]
    reach = jnp.exp(cum_t_ref[...]).T
    starts = starts_ref[...].reshape(MI, NS)
    for pair in range(PAIRS):
        cols = slice(128 * pair, 128 * (pair + 1))
        scale = by_head(*(reach[:, head : head + 1] for head in (2 * pair, 2 * pair + 1)))
        out = local_ref[:, cols] + scale * dot_last(inputs_c, starts[cols])
        ssd_ref[:, cols] = out
        gating = gating_ref[HALO:, cols]
        mamba_ref[:, cols] = (out * (gating * jax.nn.sigmoid(gating))).astype(bf16)


def leave(local_out, starts, activated, cum, projected):
    return pl.pallas_call(
        leave_kernel,
        grid=(1,),
        in_specs=[
            whole((ROWS, MI)),
            whole((CTX, STATE_ROWS, NS)),
            pl.BlockSpec((ROWS, NS), lambda i: (0, (MI + NS) // NS)),
            whole((MIXER_HEADS, ROWS)),
            whole((ROWS + HALO, MI)),
        ],
        out_specs=(whole((ROWS, MI)), whole((ROWS, MI))),
        out_shape=(struct((ROWS, MI), f32), struct((ROWS, MI), bf16)),
        compiler_params=params(),
        name="leave",
    )(local_out, starts, activated, cum, projected)


def middle_kernel(
    mamba_ref,
    attended_ref,
    tokens_ref,
    grad_out_ref,
    gain_ref,
    rest_ref,
    down_hbm_ref,
    middle_hbm_ref,
    residual_ref,
    hidden_ref,
    grad_residual_ref,
    branch_ref,
    grad_gain_ref,
    early_ref,
    mout_ref,
    aout_ref,
    left_ref,
    mid_ref,
    right_ref,
    gu_ref,
    own_gu_ref,
    own_down_ref,
    own_mout_ref,
    own_aout_ref,
    sems,
    own_sems,
):
    def fetch(begin, rows, target, sem):
        copy = pltpu.make_async_copy(rest_ref.at[:, pl.ds(begin, rows)], target, sems.at[sem])
        copy.start()
        return copy

    get_mout = fetch(0, 192, mout_ref, 0)
    get_aout = fetch(192, 64, aout_ref, 1)
    get_gu = {}
    for order, block in enumerate((0, 2)):
        get_gu[block] = fetch(352 + 128 * block, 128, gu_ref.at[block], 2 + order)
    get_down = []
    for owner in range(OWNERS):
        source = down_hbm_ref.at[:, pl.ds(16 * owner, 16)]
        get_down.append(pltpu.make_async_copy(source, left_ref.at[owner], sems.at[6 + owner]))
        source = middle_hbm_ref.at[:, pl.ds(16 * owner, 16)]
        get_down.append(pltpu.make_async_copy(source, mid_ref.at[owner], sems.at[14 + owner]))
    for block in range(3):
        for part in range(8):
            source = rest_ref.at[:, pl.ds(256 + 32 * block, 32), pl.ds(128 * part, 128)]
            target = right_ref.at[:, pl.ds(32 * part, 32), pl.ds(128 * block, 128)]
            sem = sems.at[22 + 8 * block + part]
            get_down.append(pltpu.make_async_copy(source, target, sem))
    for copy in get_down:
        copy.start()
    for order, block in enumerate((1, 3)):
        get_gu[block] = fetch(352 + 128 * block, 128, gu_ref.at[block], 4 + order)

    get_mout.wait()
    mamba_out = dot(mamba_ref[...], mout_ref[...].reshape(MI, D))
    get_aout.wait()
    attn_out = dot(attended_ref[...], aout_ref[...].reshape(Q_WIDTH, D))
    residual = tokens_ref[...].astype(f32) + attn_out + mamba_out
    inverse = lax.rsqrt(jnp.mean(residual * residual, axis=-1, keepdims=True) + epsilon)
    normed = residual * inverse
    gain = gain_ref[...]
    second = (normed * gain).astype(bf16)
    second_turned = second.T
    sending = []

    def send(source, target, sem):
        copy = pltpu.make_async_copy(source, target, own_sems.at[sem])
        copy.start()
        sending.append(copy)

    grad_out = grad_out_ref[...]
    residual_ref[...] = residual
    grad_second = jnp.zeros((ROWS, D), f32)
    for half in range(2):
        get_gu[half].wait()
        get_gu[2 + half].wait()
        w_gate = gu_ref[half].reshape(D, D)
        w_up = gu_ref[2 + half].reshape(D, D)
        gate = dot(second, w_gate)
        up = dot(second, w_up)
        logistic = jax.nn.sigmoid(gate)
        active = gate * logistic
        hidden = (active * up).astype(bf16)
        if half == 0:
            for copy in get_down:
                copy.wait()
        w_left = left_ref[4 * half : 4 * (half + 1)].reshape(D, 384)
        w_right = right_ref[4 * half : 4 * (half + 1)].reshape(D, 384)
        w_mid = mid_ref[4 * half : 4 * (half + 1)].reshape(D, 256)
        hidden_ref[:, D * half : D * (half + 1)] = hidden
        grad_hidden = (
            dot_last(grad_out[:, :384], w_left)
            + dot_last(grad_out[:, 384:640], w_mid)
            + dot_last(grad_out[:, 640:], w_right)
        )
        slope = logistic * (1.0 + gate * (1.0 - logistic))
        grad_gate = (grad_hidden * up * slope).astype(bf16)
        grad_up = (grad_hidden * active).astype(bf16)
        grad_second = grad_second + dot_last(grad_gate, w_gate) + dot_last(grad_up, w_up)
        while sending:
            sending.pop().wait()
        for side, grads in enumerate((grad_gate, grad_up)):
            own_gu_ref[side] = dot(second_turned, grads).astype(bf16).reshape(OWNERS, 128, D)
            begin = 512 + 128 * (half + 2 * side)
            send(own_gu_ref.at[side], early_ref.at[:, pl.ds(begin, 128)], side)
        own_down_ref[...] = dot_first(hidden, grad_out).astype(bf16).reshape(4, 256, D)
        send(own_down_ref, early_ref.at[pl.ds(4 * half, 4), pl.ds(256, 256)], 2)
    grad_gain_ref[...] = jnp.broadcast_to(
        jnp.sum(grad_second * normed, axis=0, keepdims=True), (8, D)
    )
    grad_residual = grad_out.astype(f32) + rms_back(grad_second, normed, inverse, gain)
    grad_residual_ref[...] = grad_residual
    branch = grad_residual.astype(bf16)
    branch_ref[...] = branch
    own_mout_ref[...] = dot_first(mamba_ref[...], branch).astype(bf16).reshape(OWNERS, 192, D)
    send(own_mout_ref, early_ref.at[:, pl.ds(0, 192)], 3)
    own_aout_ref[...] = dot_first(attended_ref[...], branch).astype(bf16).reshape(OWNERS, 64, D)
    send(own_aout_ref, early_ref.at[:, pl.ds(192, 64)], 4)
    while sending:
        sending.pop().wait()


def middle(
    mamba_in,
    attended,
    tokens,
    grad_out,
    gain,
    rest_weights,
    down_weights,
    middle_weights,
):
    return pl.pallas_call(
        middle_kernel,
        grid=(1,),
        in_specs=[
            whole((ROWS, MI)),
            whole((ROWS, Q_WIDTH)),
            whole((ROWS, D)),
            whole((ROWS, D)),
            whole((1, D)),
            pl.BlockSpec(memory_space=pl.ANY),
            pl.BlockSpec(memory_space=pl.ANY),
            pl.BlockSpec(memory_space=pl.ANY),
        ],
        out_specs=(
            whole((ROWS, D)),
            whole((ROWS, FF)),
            whole((ROWS, D)),
            whole((ROWS, D)),
            whole((8, D)),
            pl.BlockSpec(memory_space=pl.ANY),
        ),
        out_shape=(
            struct((ROWS, D), f32),
            struct((ROWS, FF), bf16),
            struct((ROWS, D), f32),
            struct((ROWS, D), bf16),
            struct((8, D), f32),
            struct((OWNERS, D, D), bf16),
        ),
        scratch_shapes=[
            pltpu.VMEM((OWNERS, 192, D), bf16),
            pltpu.VMEM((OWNERS, 64, D), bf16),
            pltpu.VMEM((OWNERS, CTX, 16, 384), bf16),
            pltpu.VMEM((OWNERS, CTX, 16, 256), bf16),
            pltpu.VMEM((OWNERS, 256, 384), bf16),
            pltpu.VMEM((4, OWNERS, 128, D), bf16),
            pltpu.VMEM((2, OWNERS, 128, D), bf16),
            pltpu.VMEM((4, 256, D), bf16),
            pltpu.VMEM((OWNERS, 192, D), bf16),
            pltpu.VMEM((OWNERS, 64, D), bf16),
            pltpu.SemaphoreType.DMA((46,)),
            pltpu.SemaphoreType.DMA((5,)),
        ],
        compiler_params=params(),
        name="middle",
    )(
        mamba_in,
        attended,
        tokens,
        grad_out,
        gain,
        rest_weights,
        down_weights,
        middle_weights,
    )


def branch_back_kernel(
    branch_ref,
    ssd_ref,
    gating_ref,
    rest_ref,
    grad_attended_ref,
    grad_ssd_ref,
    grad_gating_ref,
    mout_ref,
    aout_ref,
    sems,
):
    get_mout = pltpu.make_async_copy(rest_ref.at[:, pl.ds(0, 192)], mout_ref, sems.at[0])
    get_aout = pltpu.make_async_copy(rest_ref.at[:, pl.ds(192, 64)], aout_ref, sems.at[1])
    get_mout.start()
    get_aout.start()
    branch = branch_ref[...]
    get_mout.wait()
    get_aout.wait()
    grad_attended_ref[...] = dot_last(branch, aout_ref[...].reshape(Q_WIDTH, D)).astype(bf16)
    for at in range(0, MI, 384):
        cols = slice(at, at + 384)
        w_part = mout_ref[at // 192 : at // 192 + 2].reshape(384, D)
        grad_mamba = dot_last(branch, w_part)
        gating = gating_ref[HALO:, cols]
        logistic = jax.nn.sigmoid(gating)
        grad_ssd_ref[:, cols] = (grad_mamba * (gating * logistic)).astype(bf16)
        slope = logistic * (1.0 + gating * (1.0 - logistic))
        grad_gating_ref[:, cols] = (grad_mamba * ssd_ref[:, cols] * slope).astype(bf16)


def branch_back(branch_grad, ssd_out, projected, rest_weights):
    return pl.pallas_call(
        branch_back_kernel,
        grid=(1,),
        in_specs=[
            whole((ROWS, D)),
            whole((ROWS, MI)),
            whole((ROWS + HALO, MI)),
            pl.BlockSpec(memory_space=pl.ANY),
        ],
        out_specs=(whole((ROWS, Q_WIDTH)), whole((ROWS, MI)), whole((ROWS, MI))),
        out_shape=(
            struct((ROWS, Q_WIDTH), bf16),
            struct((ROWS, MI), bf16),
            struct((ROWS, MI), bf16),
        ),
        scratch_shapes=[
            pltpu.VMEM((OWNERS, 192, D), bf16),
            pltpu.VMEM((OWNERS, 64, D), bf16),
            pltpu.SemaphoreType.DMA((2,)),
        ],
        compiler_params=params(),
        name="branch_back",
    )(branch_grad, ssd_out, projected, rest_weights)


def finish_kernel(
    hidden_ref,
    residual_ref,
    rest_ref,
    left_hbm_ref,
    mid_hbm_ref,
    output_ref,
    left_ref,
    mid_ref,
    right_ref,
    sems,
):
    copies = []
    for owner in range(OWNERS):
        rows = pl.ds(16 * owner, 16)
        sem = sems.at[owner]
        copies.append(pltpu.make_async_copy(left_hbm_ref.at[:, rows], left_ref.at[owner], sem))
        sem = sems.at[OWNERS + owner]
        copies.append(pltpu.make_async_copy(mid_hbm_ref.at[:, rows], mid_ref.at[owner], sem))
    for block in range(3):
        for part in range(8):
            source = rest_ref.at[:, pl.ds(256 + 32 * block, 32), pl.ds(128 * part, 128)]
            target = right_ref.at[:, pl.ds(32 * part, 32), pl.ds(128 * block, 128)]
            sem = sems.at[2 * OWNERS + 8 * block + part]
            copies.append(pltpu.make_async_copy(source, target, sem))
    for copy in copies:
        copy.start()
    hidden = hidden_ref[...]
    residual = residual_ref[...]
    for copy in copies:
        copy.wait()
    left = dot(hidden, left_ref[...].reshape(FF, 384))
    mid = dot(hidden, mid_ref[...].reshape(FF, 256))
    right = dot(hidden, right_ref[...].reshape(FF, 384))
    output_ref[...] = (residual + jnp.concatenate([left, mid, right], axis=1)).astype(bf16)


def finish(hidden_act, residual, rest_weights, down_weights, middle_weights):
    return pl.pallas_call(
        finish_kernel,
        grid=(1,),
        in_specs=[
            whole((ROWS, FF)),
            whole((ROWS, D)),
            pl.BlockSpec(memory_space=pl.ANY),
            pl.BlockSpec(memory_space=pl.ANY),
            pl.BlockSpec(memory_space=pl.ANY),
        ],
        out_specs=whole((ROWS, D)),
        out_shape=struct((ROWS, D), bf16),
        scratch_shapes=[
            pltpu.VMEM((OWNERS, CTX, 16, 384), bf16),
            pltpu.VMEM((OWNERS, CTX, 16, 256), bf16),
            pltpu.VMEM((OWNERS, 256, 384), bf16),
            pltpu.SemaphoreType.DMA((40,)),
        ],
        compiler_params=params(),
        name="finish",
    )(hidden_act, residual, rest_weights, down_weights, middle_weights)


def attend_back_kernel(
    first_row_ref,
    query_ref,
    got_ref,
    total_ref,
    grad_attended_ref,
    grad_ssd_ref,
    inputs_c_ref,
    cum_t_ref,
    grad_query_ref,
    sent_ref,
):
    keys = got_ref[:, STATE_ROWS : STATE_ROWS + ROWS].reshape(KEYS, 128)
    values = got_ref[:, STATE_ROWS + ROWS :].reshape(KEYS, 128)
    allowed = key_mask(first_row_ref[0])
    grad_keys = jnp.zeros((KEYS, 128), f32)
    grad_values = jnp.zeros((KEYS, 128), f32)
    for group in range(KH):
        queries = query_ref[512 * group : 512 * (group + 1)]
        grads = []
        for head in range(4 * group, 4 * group + 4):
            pair = grad_attended_ref[:, 128 * (head // 2) : 128 * (head // 2 + 1)].astype(f32)
            grads.append(half_filled(pair, head))
        grads = jnp.concatenate(grads, axis=0)
        scores = dot_last(keys, queries) * score_scale
        scores = jnp.where(allowed, scores, masked_value)
        probs = jnp.exp(scores - total_ref[group, 0:1, :])
        grad_probs = dot_last(values, grads)
        delta = jnp.sum(probs * grad_probs, axis=0, keepdims=True)
        grad_scores = (probs * (grad_probs - delta)).astype(bf16)
        grad_values = grad_values + dot(probs.astype(bf16), grads)
        grad_keys = grad_keys + dot(grad_scores, queries)
        turned_query = dot_first(keys, grad_scores)[64 * group : 64 * (group + 1)]
        for part in range(2):
            both = [
                turned_query[:, 128 * (2 * part + k) : 128 * (2 * part + k + 1)] for k in range(2)
            ]
            at = 256 * group + 128 * part
            grad_query_ref[:, at : at + 128] = jnp.concatenate(both, axis=0).T
    sent_ref[:, STATE_ROWS : STATE_ROWS + ROWS] = grad_keys.astype(bf16).reshape(CTX, ROWS, 128)
    sent_ref[:, STATE_ROWS + ROWS :] = grad_values.astype(bf16).reshape(CTX, ROWS, 128)

    def store(to, row, value):
        sent_ref[to, row : row + 32] = value

    inputs_c = inputs_c_ref[...]
    reach = jnp.exp(cum_t_ref[...]).T
    for pair in range(PAIRS):
        cols = slice(128 * pair, 128 * (pair + 1))
        scale = by_head(*(reach[:, head : head + 1] for head in (2 * pair, 2 * pair + 1)))
        scaled = (grad_ssd_ref[:, cols].astype(f32) * scale).astype(bf16)
        state_pieces((pair, dot_first(scaled, inputs_c).astype(bf16)), store)


def attend_back(first_row, queries, got, total, grad_attended, grad_ssd, activated, cum):
    return pl.pallas_call(
        attend_back_kernel,
        grid=(1,),
        in_specs=[
            pl.BlockSpec(memory_space=pltpu.SMEM),
            whole((QH * ROWS, 128)),
            whole((CTX, SENT_ROWS, 128)),
            whole((KH, 8, 512)),
            whole((ROWS, Q_WIDTH)),
            whole((ROWS, MI)),
            pl.BlockSpec((ROWS, NS), lambda i: (0, (MI + NS) // NS)),
            whole((MIXER_HEADS, ROWS)),
        ],
        out_specs=(whole((ROWS, Q_WIDTH)), whole((CTX, SENT_ROWS, NS))),
        out_shape=(struct((ROWS, Q_WIDTH), f32), struct((CTX, SENT_ROWS, NS), bf16)),
        compiler_params=params(),
        name="attend_back",
    )(first_row, queries, got, total, grad_attended, grad_ssd, activated, cum)


def ssd_back_kernel(
    grad_ssd_ref,
    act_ref,
    conv_out_ref,
    cum_t_ref,
    gate_t_ref,
    starts_ref,
    ends_ref,
    grad_query_ref,
    got_ref,
    cos_ref,
    sin_ref,
    grad_conv_ref,
    grad_a_ref,
):
    inputs_b = act_ref[:, MI : MI + NS]
    inputs_c = act_ref[:, MI + NS :]
    products = dot_last(inputs_b, inputs_c)
    row_ids = lax.broadcasted_iota(jnp.int32, (ROWS, ROWS), 0)
    causal = row_ids <= lanes()
    cum = cum_t_ref[...].T
    reach = jnp.exp(cum)
    gates = gate_t_ref[...].T
    remain_all = jnp.exp(cum[ROWS - 1 : ROWS] - cum) * gates
    starts = starts_ref[...].reshape(MI, NS)
    ends = ends_ref[...].reshape(MI, NS)
    grad_products = jnp.zeros((ROWS, ROWS), f32)
    grad_b = jnp.zeros((ROWS, NS), f32)
    grad_c = jnp.zeros((ROWS, NS), f32)

    def through(conv, grad):
        logistic = jax.nn.sigmoid(conv)
        return (grad * (logistic * (1.0 + conv * (1.0 - logistic)))).astype(bf16)

    for pair in range(PAIRS):
        cols = slice(128 * pair, 128 * (pair + 1))
        heads = (2 * pair, 2 * pair + 1)
        inputs_x = act_ref[:, cols]
        grads = grad_ssd_ref[:, cols]
        wide_x = inputs_x.astype(f32)
        back = []
        for side, head in enumerate(heads):
            spread = cum_t_ref[head : head + 1, :] - cum[:, head : head + 1]
            weights = jnp.exp(jnp.where(causal, spread, masked_value)) * gates[:, head : head + 1]
            back.append(dot((weights * products).astype(bf16), grads))
            own = jnp.where(lanes() // MP == side, wide_x, 0.0).astype(bf16)
            grad_products = grad_products + weights * dot_last(own, grads)
        remain = by_head(*(remain_all[:, head : head + 1] for head in heads))
        scale = by_head(*(reach[:, head : head + 1] for head in heads))
        grad_x = by_head(*back) + remain * dot_last(inputs_b, ends[cols])
        grad_conv_ref[:, cols] = through(conv_out_ref[:, cols], grad_x)
        grad_b = grad_b + dot((wide_x * remain).astype(bf16), ends[cols])
        grad_c = grad_c + dot((grads.astype(f32) * scale).astype(bf16), starts[cols])
    low = grad_products.astype(bf16)
    grad_b = grad_b + dot(low, inputs_c)
    grad_c = grad_c + dot_first(low, inputs_b)
    grad_conv_ref[:, MI : MI + NS] = through(conv_out_ref[:, MI : MI + NS], grad_b)
    grad_conv_ref[:, MI + NS :] = through(conv_out_ref[:, MI + NS :], grad_c)

    cos, sin = cos_ref[...], sin_ref[...]
    for part in range(QKV // 128):
        if part < 4:
            values = grad_query_ref[:, 128 * part : 128 * (part + 1)]
        else:
            begin = STATE_ROWS + ROWS * (part - 4)
            values = jnp.sum(got_ref[:, begin : begin + ROWS].astype(f32), axis=0)
        if part < 5:
            values = (values * cos - turned(values) * sin) * score_scale
        grad_a_ref[:, 128 * part : 128 * (part + 1)] = values.astype(bf16)


def ssd_back(
    grad_ssd, activated, conv_out, cum_t, gate_t, starts, ends, grad_query, got, cos, sin
):
    return pl.pallas_call(
        ssd_back_kernel,
        out_shape=(struct((ROWS, XBC), bf16), struct((ROWS, QKV), bf16)),
        compiler_params=params(),
        name="ssd_back",
    )(grad_ssd, activated, conv_out, cum_t, gate_t, starts, ends, grad_query, got, cos, sin)


def conv_back_kernel(grad_ref, ahead_ref, conv_in_ref, taps_ref, out_ref, grad_taps_ref, ext_ref, in_ref):
    for at in range(0, XBC, 256):
        cols = slice(at, at + 256)
        grads = grad_ref[:, cols].astype(f32)
        ext_ref[:ROWS] = grads
        ext_ref[ROWS:] = ahead_ref[:, cols].astype(f32)
        in_ref[...] = conv_in_ref[:, cols].astype(f32)
        total = jnp.zeros((ROWS, 256), f32)
        for tap in range(CONV):
            lead = CONV - 1 - tap
            total = total + ext_ref[lead : lead + ROWS, :] * taps_ref[tap : tap + 1, cols]
            start = HALO - lead
            grad_taps_ref[tap : tap + 1, cols] = jnp.sum(
                grads * in_ref[start : start + ROWS, :], axis=0, keepdims=True
            )
        out_ref[:, cols] = total.astype(bf16)


def conv_back(grad_conv_out, ahead, conv_in, taps):
    return pl.pallas_call(
        conv_back_kernel,
        out_shape=(struct((ROWS, XBC), bf16), struct((CONV, XBC), f32)),
        scratch_shapes=[pltpu.VMEM((ROWS + HALO, 256), f32), pltpu.VMEM((ROWS + HALO, 256), f32)],
        compiler_params=params(),
        name="conv_back",
    )(grad_conv_out, ahead, conv_in, taps)


def late_grads_kernel(shared_ref, grad_ref, out_ref):
    for block in range(4):
        part = dot_first(shared_ref[...], grad_ref[:, D * block : D * (block + 1)]).astype(bf16)
        for owner in range(2):
            out_ref[owner, 128 * block : 128 * (block + 1)] = part[128 * owner : 128 * (owner + 1)]


def late_grads(shared, grad_proj):
    return pl.pallas_call(
        late_grads_kernel,
        grid=(OWNERS // 2,),
        in_specs=[pl.BlockSpec((ROWS, 256), lambda f: (0, f)), whole((ROWS, 4 * D))],
        out_specs=pl.BlockSpec((2, 512, D), lambda f: (f, 0, 0)),
        out_shape=struct((OWNERS, 512, D), bf16),
        compiler_params=params(),
        name="late_grads",
    )(shared, grad_proj)


def summed(parts_ref):
    total = parts_ref[0].astype(f32)
    for part in range(1, CTX):
        total = total + parts_ref[part].astype(f32)
    return total.astype(bf16)


def early_fold_kernel(parts_ref, small_ref, out_ref):
    out_ref[:64] = summed(parts_ref)
    out_ref[64:] = small_ref[...]


def early_fold(parts, small):
    return pl.pallas_call(
        early_fold_kernel,
        out_shape=struct((80, D), bf16),
        compiler_params=params(),
        name="early_fold",
    )(parts, small)


def fold_kernel(parts_ref, out_ref):
    low = summed(parts_ref)
    for to in range(CTX):
        out_ref[to] = low


def fold(parts):
    return pl.pallas_call(
        fold_kernel,
        out_shape=struct(parts.shape, bf16),
        compiler_params=params(),
        name="fold",
    )(parts)


def early_spread_kernel(parts_ref, mout_ref, aout_ref, down_ref, gu_ref, conv_ref, one_ref, two_ref):
    for part in range(CTX):
        values = parts_ref[part, :64].astype(f32)
        if part < 3:
            mout_ref[64 * part : 64 * (part + 1)] = values
        elif part < 4:
            aout_ref[...] = values
        elif part < 8:
            down_ref[64 * (part - 4) : 64 * (part - 3)] = values
        else:
            at = D * ((part - 8) // 2)
            row = 64 * (part % 2)
            gu_ref[row : row + 64, at : at + D] = values
    total = parts_ref[0, 64:].astype(f32)
    for part in range(1, CTX):
        total = total + parts_ref[part, 64:].astype(f32)
    conv_ref[...] = total[:CONV, : XBC // OWNERS]
    one_ref[...] = total[4:5, :128]
    two_ref[...] = total[4:5, 128:256]


def early_spread(parts):
    return pl.pallas_call(
        early_spread_kernel,
        out_shape=(
            struct((192, D), f32),
            struct((64, D), f32),
            struct((256, D), f32),
            struct((ROWS, 2 * FF), f32),
            struct((CONV, XBC // OWNERS), f32),
            struct((1, 128), f32),
            struct((1, 128), f32),
        ),
        compiler_params=params(),
        name="early_spread",
    )(parts)


def spread_kernel(parts_ref, mamba_ref, qkv_ref):
    for block in range(4):
        part = parts_ref[4 * block : 4 * (block + 1)].reshape(ROWS, D).astype(f32)
        if block < 3:
            mamba_ref[:, D * block : D * (block + 1)] = part
        else:
            mamba_ref[:, 3 * D :] = part[:, :256]
            qkv_ref[...] = part[:, 256:]


def spread(parts):
    return pl.pallas_call(
        spread_kernel,
        out_shape=(struct((ROWS, MI + XBC), f32), struct((ROWS, QKV), f32)),
        compiler_params=params(),
        name="spread",
    )(parts)


def on_device(
    tokens,
    gain_one,
    w_mamba_in,
    conv_weight,
    w_mamba_out,
    w_qkv,
    w_attn_out,
    gain_two,
    w_gate_up,
    w_down,
    decays,
    input_gates,
    grad_out,
):
    tokens = tokens[0]
    decays = decays[0].T
    input_gates = input_gates[0].T
    grad_out = grad_out[0]
    ctx_index = lax.axis_index("ctx")
    offset = ctx_index * ROWS
    first_row = offset.astype(jnp.int32).reshape(1)

    first_weights = lax.all_gather(
        jnp.concatenate([w_mamba_in, w_qkv], axis=1), "fsdp", axis=0, tiled=True
    )
    rest = pack_rest(w_mamba_out, w_attn_out, w_down, w_gate_up)
    small = jnp.concatenate(
        [gain_one, gain_two, conv_weight.T.reshape(-1), jnp.zeros((16 * 640 - 1152,), bf16)]
    )
    piece = lax.dynamic_slice(w_down, (ctx_index * 16, 0), (16, 640))
    piece = jnp.concatenate([piece, small.reshape(16, 640)], axis=0)
    pieces = swap(jnp.broadcast_to(piece[None], (OWNERS, 32, 640)), "fsdp")
    small_all = pieces[:, 16:18].reshape(OWNERS, 1280)[:, :1152]
    gain_first = small_all[:, :128].reshape(1, D).astype(f32)
    gain_second = small_all[:, 128:256].reshape(1, D).astype(f32)
    conv_taps = small_all[:, 256:].reshape(OWNERS, CONV, XBC // OWNERS).transpose(1, 0, 2)
    conv_taps = conv_taps.reshape(CONV, XBC).astype(f32)

    cumulative = jnp.cumsum(jnp.log(decays), axis=1)
    whole_decay = jnp.exp(cumulative[:, -1])[None]
    decay_parts = []
    for _ in range(3):
        decay_parts.append(whole_decay.astype(bf16))
        whole_decay = whole_decay - decay_parts[-1].astype(f32)
    decay_parts = jnp.pad(jnp.concatenate(decay_parts, axis=1), ((0, 15), (0, 384 - 72)))
    sent_down = jnp.concatenate([pieces[:, :16, :384].reshape(ROWS, 384), decay_parts], axis=0)
    down_weights = swap(jnp.broadcast_to(sent_down[None], (CTX, ROWS + 16, 384)), "ctx")
    decay_parts = down_weights[:, ROWS, :72].astype(f32)
    decays_all = decay_parts[:, :24] + decay_parts[:, 24:48] + decay_parts[:, 48:]
    decay_rows = lax.dynamic_slice_in_dim(
        jnp.repeat(decays_all, MP, axis=1), ctx_index * STATE_ROWS, STATE_ROWS, 1
    )[:, :, None]

    halo = passed_along(tokens[ROWS - HALO :], "ctx", 1)
    hidden_ext = jnp.concatenate([halo, tokens], axis=0).astype(f32)
    inverse_ext = lax.rsqrt(jnp.mean(hidden_ext * hidden_ext, axis=-1, keepdims=True) + epsilon)
    normed_ext = hidden_ext * inverse_ext
    shared_ext = (normed_ext * gain_first).astype(bf16)
    inverse_one = inverse_ext[HALO:]
    normed, shared = normed_ext[HALO:], shared_ext[HALO:]

    pair_index = jnp.remainder(jnp.arange(128), HD // 2).astype(f32)
    frequency = jnp.exp(-jnp.log(rope_base) * (2.0 * pair_index / HD))
    positions = (offset + jnp.arange(ROWS)).astype(f32)
    angles = positions[:, None] * frequency[None, :]
    cosine, sine = jnp.cos(angles), jnp.sin(angles)

    (
        first_weights,
        decay_rows,
        shared_ext,
        cosine,
        sine,
        conv_taps,
        cumulative,
        rest,
        down_weights,
        pieces,
    ) = lax.optimization_barrier(
        (
            first_weights,
            decay_rows,
            shared_ext,
            cosine,
            sine,
            conv_taps,
            cumulative,
            rest,
            down_weights,
            pieces,
        )
    )
    sent_middle = jnp.broadcast_to(pieces[None, :, :16, 384:], (CTX, OWNERS, 16, 256))
    middle_weights = swap(sent_middle.reshape(CTX, ROWS, 256), "ctx")
    rest_weights = lax.all_gather(rest, "fsdp", axis=0, tiled=False)
    projected = dot(shared_ext, first_weights)
    conv_in, conv_out, activated, local_out, queries, sent = enter(
        projected, conv_taps, cumulative, input_gates, cosine, sine
    )
    got = swap(sent, "ctx")
    starts = swap(prefix(got, decay_rows, False), "ctx")
    attended, total = attend(first_row, queries, got)
    ssd_out, mamba_in = leave(local_out, starts, activated, cumulative, projected)
    residual, hidden_act, grad_residual, branch_grad, grad_g_two, early = middle(
        mamba_in,
        attended,
        tokens,
        grad_out,
        gain_second,
        rest_weights,
        down_weights,
        middle_weights,
    )
    early_share = lax.psum_scatter(
        early, "fsdp", scatter_dimension=0, tiled=True
    )[0]
    grad_attended, grad_ssd, grad_gating = branch_back(
        branch_grad, ssd_out, projected, rest_weights
    )
    grad_query, sent_back = attend_back(
        first_row, queries, got, total, grad_attended, grad_ssd, activated, cumulative
    )
    got_back = swap(sent_back, "ctx")
    ends = swap(prefix(got_back, decay_rows, True), "ctx")
    grad_conv_out, grad_proj_a = ssd_back(
        grad_ssd,
        activated,
        conv_out,
        cumulative,
        input_gates,
        starts,
        ends,
        grad_query,
        got_back,
        cosine,
        sine,
    )
    ahead = passed_along(grad_conv_out[:HALO], "ctx", -1)
    grad_conv_in, grad_conv = conv_back(grad_conv_out, ahead, conv_in, conv_taps)
    grad_proj = jnp.concatenate([grad_gating, grad_conv_in, grad_proj_a], axis=1)
    grad_shared = dot_last(grad_proj, first_weights)
    grad_g_one = jnp.sum(grad_shared * normed, axis=0)
    grad_tokens = grad_residual + rms_back(grad_shared, normed, inverse_one, gain_first)

    conv_owned = grad_conv.reshape(CONV, OWNERS, XBC // OWNERS).transpose(1, 0, 2)
    gain_grads = jnp.concatenate(
        [grad_g_one.reshape(OWNERS, 1, 128), grad_g_two[0].reshape(OWNERS, 1, 128)], axis=2
    )
    small_grads = jnp.concatenate(
        [
            jnp.pad(conv_owned, ((0, 0), (0, 0), (0, 32))),
            gain_grads,
            jnp.zeros((OWNERS, 3, 256), f32),
        ],
        axis=1,
    ).astype(bf16)
    small_got = jnp.sum(swap(small_grads, "fsdp").astype(f32), axis=0).astype(bf16)
    late_share = lax.psum_scatter(
        late_grads(shared, grad_proj), "fsdp", scatter_dimension=0, tiled=True
    )[0]
    early_share, small_got, hidden_act = lax.optimization_barrier(
        (early_share, small_got, hidden_act)
    )
    output = finish(hidden_act, residual, rest_weights, down_weights, middle_weights)
    early_got = swap(early_share.reshape(CTX, 64, D), "ctx")
    small_rows = jnp.pad(small_got, ((0, 8), (0, D - 256)))
    early_mine = early_fold(early_got, small_rows)
    late_share, early_mine = lax.optimization_barrier((late_share, early_mine))
    early_sum = lax.all_gather(early_mine, "ctx", axis=0, tiled=False)
    late_sum = swap(fold(swap(late_share.reshape(CTX, 32, D), "ctx")), "ctx")
    grad_mout, grad_aout, grad_down, grad_gate_up, conv_sum, one_sum, two_sum = early_spread(early_sum)
    grad_in, grad_qkv = spread(late_sum)
    return (
        output[None],
        grad_tokens[None],
        one_sum.reshape(128),
        grad_in,
        conv_sum.T,
        grad_mout,
        grad_qkv,
        grad_aout,
        two_sum.reshape(128),
        grad_gate_up,
        grad_down,
    )


def solution(mesh):
    in_specs = (
        P("fsdp", "ctx", None),
        P("fsdp"),
        P("fsdp", None),
        P("fsdp", None),
        P("fsdp", None),
        P("fsdp", None),
        P("fsdp", None),
        P("fsdp"),
        P("fsdp", None),
        P("fsdp", None),
        P("fsdp", "ctx", None),
        P("fsdp", "ctx", None),
        P("fsdp", "ctx", None),
    )
    out_specs = (
        P("fsdp", "ctx", None),
        P("fsdp", "ctx", None),
        P("fsdp"),
        P("fsdp", None),
        P("fsdp", None),
        P("fsdp", None),
        P("fsdp", None),
        P("fsdp", None),
        P("fsdp"),
        P("fsdp", None),
        P("fsdp", None),
    )
    return jax.shard_map(
        on_device, mesh=mesh, in_specs=in_specs, out_specs=out_specs, check_vma=False
    )
```
